128 devices in a mesh: dp: 16 (over x, y_hi, core), tensor: 8 (over z, y_lo).
Axes of the slice: x: 4, y: 4 (y_hi: 2, y_lo: 2; y = y_hi * 2 + y_lo), z: 4, core: 2. Of those that a mesh axis runs over, the one named last changes fastest.
Arguments:
- hidden_in: bfloat16 [4096, 2048], P('dp'), may hold values from -6 to 6
- norm_attn: float32 [2048], replicated, may hold values from 0.1 to 1.9
- q_weight: bfloat16 [2048, 3072], P(None, 'tensor'), may hold values from -0.125 to 0.125
- kv_down: bfloat16 [2048, 576], replicated, may hold values from -0.125 to 0.125
- kv_norm: float32 [512], replicated, may hold values from 0.1 to 1.9
- kv_up: bfloat16 [512, 4096], P(None, 'tensor'), may hold values from -0.25 to 0.25
- out_weight: bfloat16 [2048, 2048], P('tensor'), may hold values from -2 to 2
- norm_ffn: float32 [2048], replicated, may hold values from 0.1 to 1.9
- router: bfloat16 [2048, 64], replicated, may hold values from -0.0625 to 0.0625
- expert_gate: bfloat16 [64, 2048, 1408], P('dp', None, 'tensor'), may hold values from -0.125 to 0.125
- expert_up: bfloat16 [64, 2048, 1408], P('dp', None, 'tensor'), may hold values from -0.125 to 0.125
- expert_down: bfloat16 [64, 1408, 2048], P('dp', 'tensor'), may hold values from -4 to 4
- shared_gate: bfloat16 [2048, 2816], P(None, 'tensor'), may hold values from -0.125 to 0.125
- shared_up: bfloat16 [2048, 2816], P(None, 'tensor'), may hold values from -0.125 to 0.125
- shared_down: bfloat16 [2816, 2048], P('tensor'), may hold values from -0.109375 to 0.109375
- routes: int32 [4096, 6], P('dp'), may hold values from 0 to 63, all different within a row; in each aligned block of 256 rows (0 to 255, 256 to 511, ...) at most 32 rows name the same one
- cotangent: bfloat16 [4096, 2048], P('dp'), may hold values from -6 to 6
Outputs:
- output: bfloat16 [4096, 2048], P('dp')
- input_grad: bfloat16 [4096, 2048], P('dp')
- norm_attn_grad: float32 [2048], P('dp')
- q_weight_grad: float32 [2048, 3072], P('dp', 'tensor')
- kv_down_grad: float32 [2048, 576], P('dp')
- kv_norm_grad: float32 [512], P('dp')
- kv_up_grad: float32 [512, 4096], P('dp', 'tensor')
- out_weight_grad: float32 [2048, 2048], P('tensor', 'dp')
- norm_ffn_grad: float32 [2048], P('dp')
- router_grad: float32 [2048, 64], P('dp')
- expert_gate_grad: float32 [64, 2048, 1408], P('dp', None, 'tensor')
- expert_up_grad: float32 [64, 2048, 1408], P('dp', None, 'tensor')
- expert_down_grad: float32 [64, 1408, 2048], P('dp', 'tensor')
- shared_gate_grad: float32 [2048, 2816], P('dp', 'tensor')
- shared_up_grad: float32 [2048, 2816], P('dp', 'tensor')
- shared_down_grad: float32 [2816, 2048], P('tensor', 'dp')
- rms_values: float32 [5], replicated
The draws below stay inside these ranges and needn't reach their ends.
Inputs may be any that keep to these rules, and one draw needn't show every extreme that they name: `routes`: each row names 6 different experts. In the rows of one index of dp no expert is named by more than 32 rows, and in every draw some expert is named by exactly 32 rows of some index.
All inputs are finite; a program needn't handle non-finite values.
Results may differ from the reference program's by a relative error of at most 0.019.
Values may be sent and summed in bfloat16 or wider, within the bound.
No kernel may reach another device: no remote copies, remote signals or barrier semaphores. Data moves between devices by JAX's collectives and lax.ppermute only.
A program may use at most 320 MiB of HBM per device.

```python
import math
import jax
import jax.numpy as jnp
import numpy as np
from jax import lax

D = 2048
H = 16
NOPE = 128
ROPE = 64
RANK = 512
VDIM = 128
FFE = 1408
TOP = 6
PROMPT = 1024
CONT = 128
TOK_DEV = 256
SHARED = 2816
EXPERTS = 64
GROUP = 2048
TOKENS = 4096
CAP = 32
N_DP = 16


def draw_hidden_in(key, part):
    key = jax.random.fold_in(key, 11)
    row_place = jnp.arange(TOKENS, dtype=jnp.float32)[:, None] / TOKENS
    values = jnp.clip(jax.random.normal(key, (TOKENS, D), jnp.float32), -4.0, 4.0) * (0.5 + row_place)
    return values.astype(jnp.bfloat16)


def draw_cotangent(key, part):
    key = jax.random.fold_in(key, 23)
    row_place = jnp.arange(TOKENS, dtype=jnp.float32)[:, None] / TOKENS
    values = jnp.clip(jax.random.normal(key, (TOKENS, D), jnp.float32), -4.0, 4.0) * (0.5 + row_place)
    return values.astype(jnp.bfloat16)


def block_levels(key, shape, cuts, least, largest):
    factor_of, own = 1.0, jax.random.fold_in(key, 6)
    for dim, parts in cuts:
        draws = jnp.exp(jax.random.uniform(jax.random.fold_in(own, dim), (parts,), jnp.float32, least / len(cuts), largest / len(cuts)))
        factor_of = factor_of * jnp.repeat(draws, shape[dim] // parts).reshape([-1 if axis == dim else 1 for axis in range(len(shape))])
    return factor_of


def assign_block(rng, own, number, rows, amount, top, bound, skew):
    order = jax.random.permutation(rng, amount)
    packed, ordinary = shares(amount, rows * top, bound, skew, True), shares(amount, rows * top, bound, skew, False)
    places = jnp.arange(amount)

    def named(sizes, turn):
        used = int((sizes > 0).sum())
        fixed = max(1, used // 4)
        shifted = fixed + (places - fixed + turn * (used - fixed)) % max(1, amount - fixed)
        return jnp.zeros((amount,), jnp.int32).at[order[jnp.where(places < fixed, places, shifted)]].set(jnp.asarray(sizes, jnp.int32))

    sizes = jnp.where(number % 4 == 0, named(packed, number // 4), named(ordinary, number - number // 4 - 1))
    mixed = jax.random.permutation(jax.random.fold_in(own, 3), amount)
    donor, sink = mixed[0:amount // 2 * 2:2], mixed[1:amount // 2 * 2:2]
    slack = jnp.minimum(sizes[donor] - 1, bound - sizes[sink]) // 2
    slack = jnp.where((donor == order[0]) | (sink == order[0]) | (sizes[sink] == 0), 0, jnp.maximum(slack, 0))
    shifted = jax.random.randint(jax.random.fold_in(own, 4), (amount // 2,), 0, 1 << 20) % (slack + 1)
    sizes = sizes.at[donor].add(-shifted).at[sink].add(shifted)
    members = jnp.searchsorted(jnp.cumsum(sizes), jnp.arange(rows * top), side="right").astype(jnp.int32)
    listing = members.reshape(top, rows).T
    listing = listing[jax.random.permutation(jax.random.fold_in(own, 1), rows)]
    turn = jax.random.randint(jax.random.fold_in(own, 2), (rows, 1), 0, top)
    return jnp.take_along_axis(listing, (jnp.arange(top)[None, :] + turn) % top, axis=1)


def shares(number_of, total, limit, lean, full):
    loads = [(1 << 20) // math.isqrt(standing ** lean) + 1 for standing in range(1, number_of + 1)]
    largest = limit if full else min(limit, max(-(-total // number_of), total * loads[0] // sum(loads)))
    least = 1 if total - largest >= number_of - 1 else 0
    counts, rest = [largest] + [least] * (number_of - 1), total - largest - least * (number_of - 1)
    while rest > 0:
        free = [i for i in range(1, number_of) if counts[i] < largest] or [i for i in range(1, number_of) if counts[i] < limit]
        pool, budget = sum([loads[i] for i in free]), rest
        for i in free:
            more = min(limit - counts[i], max(1, budget * loads[i] // pool), rest)
            counts[i] = counts[i] + more
            rest = rest - more
    return np.array(counts)


def scatter_about(stream_key, dims, scale, limit, cuts=(), kind=jnp.bfloat16):
    array = scale * jax.random.normal(stream_key, dims, jnp.float32)
    if cuts:
        array = array * block_levels(stream_key, dims, cuts, -0.22, 0.18)
    return jnp.clip(array, -limit, limit).astype(kind)


def setup_inputs(seed: int = 0) -> dict:
    arg_keys = jax.random.split(jax.random.key(seed), 18)
    hidden_in = draw_hidden_in(jax.random.fold_in(arg_keys[17], 71), 0)
    norm_attn = jnp.clip(1.0 + 0.18 * jax.random.normal(arg_keys[1], (D,), jnp.float32), 0.1, 1.9)
    q_weight = scatter_about(arg_keys[2], (D, H * (NOPE + ROPE)), D ** -0.5, 0.125, ((1, 8),))
    kv_down = scatter_about(arg_keys[3], (D, RANK + ROPE), D ** -0.5, 0.125)
    kv_norm = jnp.clip(1.0 + 0.18 * jax.random.normal(arg_keys[4], (RANK,), jnp.float32), 0.1, 1.9)
    kv_up = scatter_about(arg_keys[5], (RANK, H * (NOPE + VDIM)), RANK ** -0.5, 0.25, ((1, 8),))
    out_weight = scatter_about(arg_keys[6], (H * VDIM, D), (max(D // 256, 1)) ** -0.5, 2.0, ((0, 8),))
    norm_ffn = jnp.clip(1.0 + 0.18 * jax.random.normal(arg_keys[7], (D,), jnp.float32), 0.1, 1.9)
    router = scatter_about(arg_keys[8], (D, EXPERTS), (4 * D) ** -0.5, 0.0625)
    expert_gate = scatter_about(arg_keys[9], (EXPERTS, D, FFE), D ** -0.5, 0.125, ((0, 16), (2, 8)))
    expert_up = scatter_about(arg_keys[10], (EXPERTS, D, FFE), D ** -0.5, 0.125, ((0, 16), (2, 8)))
    expert_down = scatter_about(arg_keys[11], (EXPERTS, FFE, D), (max(FFE // 512, 1)) ** -0.5, 4.0, ((0, 16), (1, 8)))
    shared_gate = scatter_about(arg_keys[12], (D, SHARED), D ** -0.5, 0.125, ((1, 8),))
    shared_up = scatter_about(arg_keys[13], (D, SHARED), D ** -0.5, 0.125, ((1, 8),))
    shared_down = scatter_about(arg_keys[14], (SHARED, D), SHARED ** -0.5, 0.109375, ((0, 8),))
    routes_keys = jax.random.split(jax.random.fold_in(arg_keys[15], 1), TOKENS // TOK_DEV)
    routes_turns = jax.random.permutation(jax.random.fold_in(arg_keys[15], 3), TOKENS // TOK_DEV)
    routes = jax.vmap(lambda own, number: assign_block(jax.random.fold_in(arg_keys[15], 2), own, number, TOK_DEV, EXPERTS, TOP, CAP, 1))(routes_keys, routes_turns).reshape((TOKENS, TOP))
    cotangent = draw_cotangent(jax.random.fold_in(arg_keys[17], 71), 0)
    return dict(hidden_in=hidden_in, norm_attn=norm_attn, q_weight=q_weight, kv_down=kv_down, kv_norm=kv_norm, kv_up=kv_up, out_weight=out_weight, norm_ffn=norm_ffn, router=router, expert_gate=expert_gate, expert_up=expert_up, expert_down=expert_down, shared_gate=shared_gate, shared_up=shared_up, shared_down=shared_down, routes=routes, cotangent=cotangent)


EPSILON = 1e-06
THETA = 10000.0
HIGHEST = lax.Precision.HIGHEST

@jax.custom_vjp
def low(v):
    return lax.optimization_barrier(v.astype(jnp.bfloat16)).astype(jnp.float32)

@jax.custom_vjp
def low_back(v):
    return v

def low_keep(v):
    return (low(v), None)

def low_pass(kept, grad):
    return (grad,)

def back_keep(v):
    return (v, None)

def back_low(kept, grad):
    return (low(grad),)
low.defvjp(low_keep, low_pass)
low_back.defvjp(back_keep, back_low)

def matmul(first_arr, second_arr):
    return jnp.dot(first_arr, second_arr, precision=HIGHEST, preferred_element_type=jnp.float32)

def rms_scale(values, gain):
    return values * lax.rsqrt(lax.optimization_barrier(jnp.mean(values * values, -1, keepdims=True)) + EPSILON) * gain

def rotate(values, cos_table, sin_table):
    half_width = values.shape[-1] // 2
    front = values[..., :half_width]
    behind = values[..., half_width:]
    return jnp.concatenate([front * cos_table - behind * sin_table, behind * cos_table + front * sin_table], -1)

def token_layout(row_index):
    offset = row_index % GROUP
    in_prompt = offset < PROMPT
    position = jnp.where(in_prompt, offset, PROMPT + (offset - PROMPT) % CONT)
    segment = jnp.where(in_prompt, 0, 1 + (offset - PROMPT) // CONT)
    return (position, segment, row_index // GROUP)

def angle_tables(position):
    half_width = ROPE // 2
    frequency = THETA ** (-2.0 * jnp.arange(half_width, dtype=jnp.float32) / ROPE)
    angles = position.astype(jnp.float32)[:, None] * frequency[None]
    return (jnp.cos(angles), jnp.sin(angles))

def reference(hidden_in, norm_attn, q_weight, kv_down, kv_norm, kv_up, out_weight, norm_ffn, router, expert_gate, expert_up, expert_down, shared_gate, shared_up, shared_down, routes, cotangent):
    row_index = jnp.arange(TOKENS, dtype=jnp.int32)
    position, segment, group_id = token_layout(row_index)
    cos_table, sin_table = angle_tables(position)
    scaling = (NOPE + ROPE) ** (-0.5)
    block_rows = min(512, TOKENS)
    slot_rows = N_DP * CAP
    flat_expert = routes.reshape(-1).astype(jnp.int32)
    flat_index = jnp.arange(TOKENS * TOP, dtype=jnp.int32)
    chosen = (flat_expert[:, None] == jnp.arange(EXPERTS, dtype=jnp.int32)[None]).astype(jnp.int32)
    chosen = chosen.reshape(N_DP, TOK_DEV * TOP, EXPERTS)
    ranking = lax.optimization_barrier(jnp.sum(chosen * (jnp.cumsum(chosen, 1) - 1), -1)).reshape(-1).astype(jnp.int32)
    slot_target = (flat_expert * slot_rows + flat_index // TOP // TOK_DEV * CAP + ranking).astype(jnp.int32)
    token_of_slot = jnp.full((EXPERTS * slot_rows,), TOKENS, jnp.int32).at[slot_target].set(flat_index // TOP)

    def attend_block(block_start, query_all, key_all, value_all):
        query_block = lax.dynamic_slice_in_dim(query_all, block_start, block_rows, 0)
        query_index = block_start + jnp.arange(block_rows, dtype=jnp.int32)
        unused_pos, query_seg, query_group = token_layout(query_index)
        allowed = (query_group[:, None] == group_id[None]) & (row_index[None] <= query_index[:, None]) & ((segment[None] == 0) | (segment[None] == query_seg[:, None]))
        raw_dot = jnp.einsum('qhd,khd->hqk', query_block, key_all, precision=HIGHEST)
        scores = jnp.where(allowed[None], low_back(raw_dot) * scaling, -1e+30)
        attn_prob = jax.nn.softmax(scores, -1)
        return jnp.einsum('hqk,khd->qhd', low(attn_prob), value_all, precision=HIGHEST)

    def expert_row_block(pieces):
        rows_in, gate_w, up_w, down_w = pieces
        gate_pre = low_back(matmul(rows_in, gate_w))
        up_pre = low_back(matmul(rows_in, up_w))
        hidden_act = low(jax.nn.silu(gate_pre) * up_pre)
        return low_back(matmul(hidden_act, down_w))

    def forward(layer_parameters):
        hidden_state, attention_gain, query_weight, latent_down_weight, latent_norm_gain, latent_up_weight, output_weight, feedforward_gain, router_weight, routed_gate_weight, routed_up_weight, routed_down_weight, common_gate_weight, common_up_weight, common_down_weight = layer_parameters
        attn_in = low(rms_scale(hidden_state, attention_gain))
        query_raw = low_back(matmul(attn_in, query_weight)).reshape(TOKENS, H, NOPE + ROPE)
        kv_raw = low_back(matmul(attn_in, latent_down_weight))
        latent = kv_raw[:, :RANK]
        latent_n = low(rms_scale(latent, latent_norm_gain))
        key_rope = low(rotate(kv_raw[:, RANK:], cos_table, sin_table))
        query_all = low(jnp.concatenate([query_raw[..., :NOPE], rotate(query_raw[..., NOPE:], cos_table[:, None], sin_table[:, None])], -1))
        kv_heads = low(low_back(matmul(latent_n, latent_up_weight))).reshape(TOKENS, H, NOPE + VDIM)
        key_all = jnp.concatenate([kv_heads[..., :NOPE], jnp.broadcast_to(key_rope[:, None, :], (TOKENS, H, ROPE))], -1)
        value_all = kv_heads[..., NOPE:]
        checked = jax.checkpoint(attend_block)
        starts = jnp.arange(TOKENS // block_rows, dtype=jnp.int32) * block_rows
        blocks = lax.map(lambda block_start: checked(block_start, query_all, key_all, value_all), starts)
        attn_o = low(low_back(blocks.reshape(TOKENS, H * VDIM)))
        middle = hidden_state + low_back(matmul(attn_o, output_weight))
        ffn_in = low(rms_scale(middle, feedforward_gain))
        router_prob = jax.nn.softmax(low_back(matmul(ffn_in, router_weight)), -1)
        gate_vals = jnp.take_along_axis(router_prob, routes.astype(jnp.int32), 1)
        padded = jnp.concatenate([ffn_in, jnp.zeros((1, D), jnp.float32)], 0)
        expert_token_rows = jnp.take(padded, token_of_slot, axis=0).reshape(EXPERTS, slot_rows, D)
        expert_output = lax.map(jax.checkpoint(expert_row_block), (expert_token_rows, routed_gate_weight, routed_up_weight, routed_down_weight))
        picked = jnp.take(expert_output.reshape(-1, D), slot_target, axis=0).reshape(TOKENS, TOP, D)
        routed = lax.optimization_barrier(jnp.sum(gate_vals[:, :, None] * picked, 1))
        shared_gpre = low_back(matmul(ffn_in, common_gate_weight))
        shared_upre = low_back(matmul(ffn_in, common_up_weight))
        shared_act = low(jax.nn.silu(shared_gpre) * shared_upre)
        shared_out = low_back(matmul(shared_act, common_down_weight))
        result = middle + routed + shared_out
        return (result, (latent, middle))
    layer_parameters = tuple((weight_arr.astype(jnp.float32) for weight_arr in (hidden_in, norm_attn, q_weight, kv_down, kv_norm, kv_up, out_weight, norm_ffn, router, expert_gate, expert_up, expert_down, shared_gate, shared_up, shared_down)))
    result, backward, kept = jax.vjp(forward, layer_parameters, has_aux=True)
    grads = backward(cotangent.astype(jnp.float32))[0]
    latent, middle = kept
    input_float = grads[0]
    hidden_float = layer_parameters[0]
    rms_values = jnp.stack([jnp.sqrt(jnp.mean(hidden_float * hidden_float)), jnp.sqrt(jnp.mean(latent * latent)), jnp.sqrt(jnp.mean(middle * middle)), jnp.sqrt(jnp.mean(result * result)), jnp.sqrt(jnp.mean(input_float * input_float))])
    return (result.astype(jnp.bfloat16), input_float.astype(jnp.bfloat16), grads[1], grads[2], grads[3], grads[4], grads[5], grads[6], grads[7], grads[8], grads[9], grads[10], grads[11], grads[12], grads[13], grads[14], rms_values)
```

```python
import functools

import jax
import jax.numpy as jnp
from jax import lax
from jax.experimental import pallas as pl
from jax.experimental.pallas import tpu as pltpu
from jax.sharding import PartitionSpec as P

NOPE = 128
ROPE = 64
RANK = 512
VDIM = 128
TOP = 6
CAP = 32
PROMPT = 1024
CONT = 128
GROUP = 2048
EXPERTS = 64
LANES = 128
EPSILON = 1e-06
THETA = 10000.0
LOW = jnp.bfloat16
FULL = jnp.float32


def contract(first_arr, second_arr, first_axis, second_axis):
    return lax.dot_general(
        first_arr,
        second_arr,
        (((first_axis,), (second_axis,)), ((), ())),
        preferred_element_type=FULL,
    )


def rotate(values, cos_table, sin_table):
    half_width = values.shape[-1] // 2
    front = values[..., :half_width]
    behind = values[..., half_width:]
    return jnp.concatenate(
        [front * cos_table - behind * sin_table, behind * cos_table + front * sin_table], -1
    )


def token_layout(row_index):
    offset = row_index % GROUP
    in_prompt = offset < PROMPT
    position = jnp.where(in_prompt, offset, PROMPT + (offset - PROMPT) % CONT)
    segment = jnp.where(in_prompt, 0, 1 + (offset - PROMPT) // CONT)
    return (position, segment, row_index // GROUP)


def angle_tables(position):
    half_width = ROPE // 2
    frequency = THETA ** (-2.0 * jnp.arange(half_width, dtype=FULL) / ROPE)
    angles = position.astype(FULL)[:, None] * frequency[None]
    return (jnp.cos(angles), jnp.sin(angles))


def inverse_rms(values):
    return lax.rsqrt(jnp.mean(values * values, -1, keepdims=True) + EPSILON)


def norm_backward(grad_normed, normed, inverse, gain):
    scaled = grad_normed * gain
    return (
        inverse * (scaled - normed * jnp.mean(scaled * normed, -1, keepdims=True)),
        jnp.sum(grad_normed * normed, 0, keepdims=True),
    )


VMEM = pl.BlockSpec(memory_space=pltpu.VMEM)
SMEM = pl.BlockSpec(memory_space=pltpu.SMEM)
HBM = pl.BlockSpec(memory_space=pl.ANY)
VMEM_BYTES = 56 * 1024 * 1024


def run_kernel(kernel, operands, specs, outs, scratch=(), out_specs=None):
    shapes = [jax.ShapeDtypeStruct(shape, dtype) for shape, dtype in outs]
    return pl.pallas_call(
        kernel,
        out_shape=shapes,
        in_specs=list(specs),
        out_specs=list(out_specs or [VMEM] * len(shapes)),
        scratch_shapes=list(scratch),
        compiler_params=pltpu.CompilerParams(vmem_limit_bytes=VMEM_BYTES),
        cost_estimate=pl.CostEstimate(flops=1000, bytes_accessed=1000, transcendentals=0),
    )(*operands)


def latent_kernel(hidden, gain, down_rows, kv_gain, cos, sin, attn_in, packed, kv_raw):
    values = hidden[...].astype(FULL)
    normed = (values * inverse_rms(values) * gain[...]).astype(LOW)
    attn_in[...] = normed
    raw = contract(normed, down_rows[...], 1, 1)
    kv_raw[...] = raw
    latent = raw[:, :RANK]
    packed[:, :RANK] = (latent * inverse_rms(latent) * kv_gain[...]).astype(LOW)
    rope = rotate(raw[:, RANK:], cos[...], sin[...]).astype(LOW)
    packed[:, RANK:] = jnp.concatenate([rope, jnp.zeros_like(rope)], -1)


def query_kernel(attn_in, q_weight, cos, sin, query):
    turned = jnp.dot(attn_in[...], q_weight[...], preferred_element_type=FULL)
    step = NOPE + ROPE
    for head in range(turned.shape[1] // step):
        place = head * 2 * LANES
        start = head * step
        query[:, place : place + NOPE] = turned[:, start : start + NOPE].astype(LOW)
        rope = rotate(turned[:, start + NOPE : start + step], cos[...], sin[...]).astype(LOW)
        query[:, place + NOPE : place + 2 * LANES] = jnp.concatenate(
            [rope, jnp.zeros_like(rope)], -1
        )


def visible_keys(meta, block, shape):
    rows = lax.broadcasted_iota(jnp.int32, shape, 0)
    cols = lax.broadcasted_iota(jnp.int32, shape, 1)
    place, prompt_devs = meta[0], PROMPT // shape[1]
    if block < prompt_devs:
        return cols - rows <= (place - meta[1 + block]) * shape[1]
    own = (cols <= rows) & (rows // CONT == cols // CONT)
    return own & (place >= prompt_devs)


def head_key(heads, rope, head):
    start = head * (NOPE + VDIM)
    return jnp.concatenate([heads[:, start : start + NOPE], rope], -1)


def attend_kernel(
    meta, first, second, third, fourth, own, query, kv_up, out_weight, part, attn, heads, log_sum
):
    blocks = (first, second, third, fourth, own)
    rows = own.shape[0]
    scaling = (NOPE + ROPE) ** (-0.5)
    for block, ref in enumerate(blocks):
        heads[block * rows : (block + 1) * rows] = jnp.dot(
            ref[:, :RANK], kv_up[...], preferred_element_type=FULL
        ).astype(LOW)
    masks = [visible_keys(meta, block, (rows, rows)) for block in range(len(blocks))]
    for head in range(query.shape[1] // (2 * LANES)):
        asked = query[:, head * 2 * LANES : (head + 1) * 2 * LANES]
        scores = []
        for block, ref in enumerate(blocks):
            key = head_key(heads[block * rows : (block + 1) * rows], ref[:, RANK:], head)
            raw = contract(asked, key, 1, 1) * scaling
            scores.append(jnp.where(masks[block], raw, -1e30))
        peak = scores[0]
        for score in scores[1:]:
            peak = jnp.maximum(peak, score)
        peak = jnp.max(peak, -1, keepdims=True)
        weights = [jnp.exp(score - peak) for score in scores]
        total = jnp.sum(functools.reduce(jnp.add, weights), -1, keepdims=True)
        scale = 1.0 / total
        summed = 0.0
        start = head * (NOPE + VDIM) + NOPE
        for block, weight in enumerate(weights):
            value = heads[block * rows : (block + 1) * rows, start : start + VDIM]
            summed = summed + jnp.dot(
                (weight * scale).astype(LOW), value, preferred_element_type=FULL
            )
        attn[:, head * VDIM : (head + 1) * VDIM] = summed.astype(LOW)
        log_sum[:, head * LANES : (head + 1) * LANES] = jnp.broadcast_to(
            peak + jnp.log(total), (rows, LANES)
        )
    part[...] = jnp.dot(attn[...], out_weight[...], preferred_element_type=FULL).astype(LOW)


def middle_kernel(meta, got, hidden, gain, middle, copies):
    part_rows = middle.shape[0]
    start = pl.multiple_of(meta[0] * part_rows, part_rows)
    values = hidden[pl.ds(start, part_rows), :].astype(FULL)
    for index in range(got.shape[0]):
        values = values + got[index].astype(FULL)
    middle[...] = values
    normed = (values * inverse_rms(values) * gain[...]).astype(LOW)
    for index in range(copies.shape[0]):
        copies[index] = normed


def shared_kernel(ffn, cot, gate, up, down, back, out, grads):
    rows = gate.shape[0]
    gate_pre = contract(ffn[...], gate[...], 1, 1)
    up_pre = contract(ffn[...], up[...], 1, 1)
    hidden_back = contract(cot[...], down[...], 1, 1)
    sig = jax.nn.sigmoid(gate_pre)
    low = (gate_pre * sig * up_pre).astype(LOW)
    gate_low = (hidden_back * up_pre * sig * (1.0 + gate_pre * (1.0 - sig))).astype(LOW)
    up_low = (hidden_back * gate_pre * sig).astype(LOW)
    out[...] = jnp.dot(low, down[...], preferred_element_type=FULL)
    back[...] = jnp.dot(gate_low, gate[...], preferred_element_type=FULL) + jnp.dot(
        up_low, up[...], preferred_element_type=FULL
    )
    grads[:rows] = contract(gate_low, ffn[...], 0, 0)
    grads[rows : 2 * rows] = contract(up_low, ffn[...], 0, 0)
    grads[2 * rows :] = contract(low, cot[...], 0, 0)


def prepare_kernel(
    grad_in, first, second, third, fourth, gate_w, up_w, down_w, back, held, in_sems, out_sems
):
    part = first.shape[0] // 3
    copies = [
        [
            pltpu.make_async_copy(
                chunk.at[pl.ds(kind * part, part)],
                held.at[kind, pl.ds(index * part, part)],
                in_sems.at[kind, index],
            )
            for index, chunk in enumerate((first, second, third, fourth))
        ]
        for kind in range(3)
    ]
    finals = [
        pltpu.make_async_copy(held.at[kind], out, out_sems.at[kind])
        for kind, out in enumerate((gate_w, up_w, down_w))
    ]
    for kind in (2, 0, 1):
        for copy in copies[kind]:
            copy.start()
    for kind in (2, 0, 1):
        for copy in copies[kind]:
            copy.wait()
        finals[kind].start()
    step = grad_in.shape[0] // 2

    @pl.loop(0, 2)
    def _(turn):
        here = pl.ds(pl.multiple_of(turn * step, step), step)
        back[here, :] = contract(grad_in[here, :], held[2], 1, 1)

    for copy in finals:
        copy.wait()


def expert_kernel(
    meta,
    rows_in,
    gate_in,
    up_in,
    back_in,
    router,
    back,
    hidden_out,
    gate_out,
    up_out,
    slot_gate,
    rows_held,
    gate_w,
    up_w,
    back_held,
    out_held,
    in_sems,
    out_sems,
):
    count, width = rows_in.shape
    step = count // 2
    halves = [pl.ds(turn * step, step) for turn in range(2)]
    get_rows = [
        pltpu.make_async_copy(rows_in.at[here], rows_held.at[here], in_sems.at[turn])
        for turn, here in enumerate(halves)
    ]
    get_gate = pltpu.make_async_copy(gate_in, gate_w, in_sems.at[2])
    get_up = pltpu.make_async_copy(up_in, up_w, in_sems.at[3])
    get_back = pltpu.make_async_copy(back_in, back_held, in_sems.at[4])
    put_back = [
        pltpu.make_async_copy(out_held.at[here], back.at[here], out_sems.at[turn])
        for turn, here in enumerate(halves)
    ]
    for copy in (get_rows[0], get_gate, get_up, get_back, get_rows[1]):
        copy.start()
    for turn, here in enumerate(halves):
        get_rows[turn].wait()
        rows = rows_held[here, :]
        logits = contract(rows, router[...], 1, 1)
        logits = jnp.exp(logits - jnp.max(logits, -1, keepdims=True))
        mine = lax.broadcasted_iota(jnp.int32, logits.shape, 1) == meta[0]
        gate = jnp.sum(jnp.where(mine, logits, 0.0), -1, keepdims=True) / jnp.sum(
            logits, -1, keepdims=True
        )
        slot_gate[here, :] = jnp.broadcast_to(gate, (step, LANES))
        if turn == 0:
            get_gate.wait()
        gate_pre = contract(rows, gate_w[...], 1, 1)
        sig = jax.nn.sigmoid(gate_pre)
        if turn == 0:
            get_up.wait()
        up_pre = contract(rows, up_w[...], 1, 1)
        low = (gate_pre * sig * up_pre).astype(LOW)
        hidden_out[here, :] = low
        if turn == 0:
            get_back.wait()
        hidden_back = back_held[here, :]
        dots = jnp.sum(low.astype(FULL) * hidden_back, -1, keepdims=True)
        hidden_back = hidden_back * gate
        gate_low = (hidden_back * up_pre * sig * (1.0 + gate_pre * (1.0 - sig))).astype(LOW)
        up_low = (hidden_back * gate_pre * sig).astype(LOW)
        gate_out[here, :] = gate_low
        up_out[here, :] = up_low
        out_held[here, :width] = (
            jnp.dot(gate_low, gate_w[...], preferred_element_type=FULL)
            + jnp.dot(up_low, up_w[...], preferred_element_type=FULL)
        ).astype(LOW)
        high = dots.astype(LOW).astype(FULL)
        lane = lax.broadcasted_iota(jnp.int32, (step, LANES), 1)
        out_held[here, width:] = jnp.where(
            lane == 0, high, jnp.where(lane == 1, dots - high, 0.0)
        ).astype(LOW)
        put_back[turn].start()
    for copy in put_back:
        copy.wait()


def expert_in_grad_kernel(rows_in, gate_low, up_low, *grads):
    width = rows_in.shape[1]
    step = width // 4
    part = grads[0].shape[0]

    @pl.loop(0, 4)
    def _(turn):
        here = pl.ds(pl.multiple_of(turn * step, step), step)
        rows = rows_in[:, here]
        for kind, low in enumerate((gate_low, up_low)):
            grad = contract(low[...], rows, 0, 0).astype(LOW)
            for index in range(4):
                grads[kind * 4 + index][:, here] = grad[index * part : (index + 1) * part]


def expert_out_kernel(grad_in, hidden, slot_gate, down_w, out, *grads):
    part, width = grads[0].shape
    step = width // 4
    gate = slot_gate[:, :1]

    @pl.loop(0, 4)
    def _(turn):
        here = pl.ds(pl.multiple_of(turn * step, step), step)
        summed = jnp.dot(hidden[...], down_w[:, here], preferred_element_type=FULL)
        out[:, here] = (summed * gate).astype(LOW)
        scaled = (grad_in[:, here].astype(FULL) * gate).astype(LOW)
        grad = contract(hidden[...], scaled, 0, 0).astype(LOW)
        for index in range(4):
            grads[index][:, here] = grad[index * part : (index + 1) * part]


def combine_kernel(meta, combine, returned, shared_back, *outs):
    payload = outs[-1]
    width = shared_back.shape[1]
    payload[:, :width] = (
        jnp.dot(combine[...], returned[:, :width], preferred_element_type=FULL) + shared_back[...]
    ).astype(LOW)
    slot_rows = returned.shape[0]
    slot = lax.broadcasted_iota(jnp.int32, (slot_rows, EXPERTS), 0) // CAP
    at_expert = slot * meta[2] + meta[1] == lax.broadcasted_iota(
        jnp.int32, (slot_rows, EXPERTS), 1
    )
    dots = returned[:, width:].astype(FULL)
    summed = 0.0
    for index in range(2):
        columns = jnp.where(at_expert, dots[:, index : index + 1], 0.0).astype(LOW)
        summed = summed + jnp.dot(combine[...], columns, preferred_element_type=FULL)
    high = summed.astype(LOW)
    rest = (summed - high.astype(FULL)).astype(LOW)
    payload[:, width:] = jnp.concatenate([high, rest], -1)
    take_parts(meta[0], payload, outs[:-1])


def take_parts(place, values, outs):
    for shift, out in enumerate(outs):
        rows = out.shape[0]
        owner = lax.rem(place + shift, len(outs))
        out[...] = values[pl.ds(pl.multiple_of(owner * rows, rows), rows), :]


def moe_kernel(combine, returned, shared_part, out):
    out[...] = (
        jnp.dot(combine[...], returned[...], preferred_element_type=FULL) + shared_part[...]
    ).astype(LOW)


def token_grad_kernel(attn_in, query_low, attn_low, spread, ffn, heads_low, *refs):
    blocks, grads = refs[:-1], refs[-1]
    width = attn_in.shape[1]
    rows = attn_in.shape[0]
    start = query_low.shape[1]
    grads[:start] = contract(query_low[...], attn_in[...], 0, 0)
    end = start + attn_low.shape[1]
    grads[start:end] = contract(attn_low[...], spread[:, :width], 0, 0)
    start, end = end, end + EXPERTS
    grads[start:end] = contract(spread[:, width:], ffn[...], 0, 0)[:EXPERTS]
    total = 0.0
    for index, ref in enumerate(blocks):
        total = total + contract(ref[:, :RANK], heads_low[index * rows : (index + 1) * rows], 0, 0)
    owners = width // LANES
    lines = total.shape[0] // owners
    for column in range(total.shape[1] // LANES):
        for owner in range(owners):
            grads[
                end + column * lines : end + (column + 1) * lines,
                owner * LANES : (owner + 1) * LANES,
            ] = total[owner * lines : (owner + 1) * lines, column * LANES : (column + 1) * LANES]


def place_kernel(meta, first, second, third, fourth, out):
    for shift, chunk in enumerate((first, second, third, fourth)):
        out[lax.rem(meta[0] + shift, out.shape[0])] = chunk[...].astype(FULL)


def ffn_back_kernel(meta, middle, ffn, router, gain, cot, *refs):
    got, (middle_grad, copies, gain_grad) = refs[:-3], refs[-3:]
    part_rows, width = middle.shape
    start = pl.multiple_of(meta[0] * part_rows, part_rows)
    here = pl.ds(start, part_rows)
    total = got[0][...].astype(FULL)
    for ref in got[1:]:
        total = total + ref[...].astype(FULL)
    extra = total[:, width:]
    prob_grad = extra[:, :EXPERTS] + extra[:, EXPERTS:]
    logits = contract(ffn[here, :], router[...], 1, 1)
    logits = jnp.exp(logits - jnp.max(logits, -1, keepdims=True))
    prob = logits / jnp.sum(logits, -1, keepdims=True)
    logit_low = (
        prob * (prob_grad - jnp.sum(prob * prob_grad, -1, keepdims=True))
    ).astype(LOW)
    ffn_grad = total[:, :width] + jnp.dot(logit_low, router[...], preferred_element_type=FULL)
    values = middle[...]
    inverse = inverse_rms(values)
    back, gains = norm_backward(ffn_grad, values * inverse, inverse, gain[...])
    gain_grad[...] = gains
    grad = cot[here, :].astype(FULL) + back
    middle_grad[...] = grad
    low = grad.astype(LOW)
    tail = jnp.concatenate([logit_low, jnp.zeros_like(logit_low)], -1)
    for index in range(copies.shape[0]):
        copies[index, :, :width] = low
        copies[index, :, width:] = tail


def attend_back_kernel(
    meta,
    out_weight,
    first,
    second,
    third,
    fourth,
    own,
    query,
    heads,
    log_sum,
    kv_up,
    cos,
    sin,
    spread,
    q_weight,
    payload,
    heads_low,
    query_low,
):
    blocks = (first, second, third, fourth, own)
    rows = own.shape[0]
    parts, part_rows, _ = payload.shape
    kv_width = RANK + 2 * ROPE
    scaling = (NOPE + ROPE) ** (-0.5)
    attn_grad = contract(spread[:, : out_weight.shape[1]], out_weight[...], 1, 1).astype(LOW)
    masks = [visible_keys(meta, block, (rows, rows)) for block in range(len(blocks))]
    ropes = [0.0] * len(blocks)
    step = NOPE + ROPE
    for head in range(query.shape[1] // (2 * LANES)):
        asked = query[:, head * 2 * LANES : (head + 1) * 2 * LANES]
        out_grad = attn_grad[:, head * VDIM : (head + 1) * VDIM]
        logs = log_sum[:, head * LANES : head * LANES + 1]
        start = head * (NOPE + VDIM)
        probs, backs = [], []
        summed = 0.0
        for block, ref in enumerate(blocks):
            here = slice(block * rows, (block + 1) * rows)
            key = head_key(heads[here], ref[:, RANK:], head)
            raw = contract(asked, key, 1, 1) * scaling
            prob = jnp.exp(jnp.where(masks[block], raw, -1e30) - logs)
            back = contract(out_grad, heads[here, start + NOPE : start + NOPE + VDIM], 1, 1)
            summed = summed + prob * back
            probs.append(prob)
            backs.append(back)
        total = jnp.sum(summed, -1, keepdims=True)
        asked_grad = 0.0
        for block, ref in enumerate(blocks):
            here = slice(block * rows, (block + 1) * rows)
            score_low = (scaling * probs[block] * (backs[block] - total)).astype(LOW)
            key = head_key(heads[here], ref[:, RANK:], head)
            asked_grad = asked_grad + jnp.dot(score_low, key, preferred_element_type=FULL)
            key_grad = contract(score_low, asked, 0, 0)
            heads_low[here, start : start + NOPE] = key_grad[:, :NOPE].astype(LOW)
            heads_low[here, start + NOPE : start + NOPE + VDIM] = contract(
                probs[block].astype(LOW), out_grad, 0, 0
            ).astype(LOW)
            ropes[block] = ropes[block] + key_grad[:, NOPE:]
        query_low[:, head * step : head * step + NOPE] = asked_grad[:, :NOPE].astype(LOW)
        query_low[:, head * step + NOPE : (head + 1) * step] = rotate(
            asked_grad[:, NOPE:step], cos[...], -sin[...]
        ).astype(LOW)
    for block in range(len(blocks)):
        here = slice(block * rows, (block + 1) * rows)
        latent = contract(heads_low[here], kv_up[...], 1, 1).astype(LOW)
        rope = ropes[block].astype(LOW)
        start = block * kv_width
        for index in range(parts):
            mine = slice(index * part_rows, (index + 1) * part_rows)
            payload[index, :, start : start + RANK] = latent[mine]
            payload[index, :, start + RANK : start + kv_width] = rope[mine]
    attn_in_grad = contract(query_low[...], q_weight[...], 1, 1).astype(LOW)
    for index in range(parts):
        payload[index, :, len(blocks) * kv_width :] = attn_in_grad[
            index * part_rows : (index + 1) * part_rows
        ]


def kv_sum_kernel(meta, got, to_owner, own, query_sum, kept):
    kv_width = own.shape[1]
    blocks = kept.shape[0]
    total = got[0].astype(FULL)
    for index in range(1, got.shape[0]):
        total = total + got[index].astype(FULL)
    for block in range(blocks):
        kept[block] = total[:, block * kv_width : (block + 1) * kv_width].astype(LOW)
    own[...] = total[:, blocks * kv_width : (blocks + 1) * kv_width]
    query_sum[...] = total[:, (blocks + 1) * kv_width :]
    for owner in range(to_owner.shape[0]):
        if owner < blocks:
            to_owner[owner] = kept[lax.rem(meta[0] - owner + blocks, blocks)]
        else:
            to_owner[owner] = jnp.zeros_like(to_owner[owner])


def last_kernel(
    meta,
    got_kv,
    own,
    kv_raw,
    kv_gain,
    cos,
    sin,
    down_rows,
    hidden,
    gain,
    middle_grad,
    got_moe,
    middle,
    query_sum,
    copies,
    gain_grad,
    kv_gain_grad,
    sums,
):
    result = middle[...]
    for index in range(got_moe.shape[0]):
        result = result + got_moe[index].astype(FULL)
    result_low = result.astype(LOW)
    part_rows, width = middle_grad.shape
    here = pl.ds(pl.multiple_of(meta[0] * part_rows, part_rows), part_rows)
    total = own[...]
    for index in range(got_kv.shape[0]):
        total = total + got_kv[index].astype(FULL)
    latent = kv_raw[here, :RANK]
    inverse = inverse_rms(latent)
    latent_grad, kv_gains = norm_backward(
        total[:, :RANK], latent * inverse, inverse, kv_gain[...]
    )
    kv_gain_grad[...] = kv_gains
    rope = rotate(total[:, RANK : RANK + ROPE], cos[here, :], -sin[here, :]).astype(LOW)
    latent_low = latent_grad.astype(LOW)
    kv_low = jnp.concatenate([latent_low, rope], -1)
    attn_in_grad = query_sum[...] + jnp.dot(kv_low, down_rows[...], preferred_element_type=FULL)
    values = hidden[here, :].astype(FULL)
    inverse = inverse_rms(values)
    back, gains = norm_backward(attn_in_grad, values * inverse, inverse, gain[...])
    gain_grad[...] = gains
    grad = middle_grad[...] + back
    low = grad.astype(LOW)
    tail = jnp.concatenate([rope, jnp.zeros_like(rope)], -1)
    for index in range(copies.shape[0]):
        copies[index, :, :width] = low
        copies[index, :, width : width + RANK] = latent_low
        copies[index, :, width + RANK : width + RANK + 2 * ROPE] = tail
        copies[index, :, width + RANK + 2 * ROPE :] = result_low
    lane = lax.broadcasted_iota(jnp.int32, sums.shape, 1)
    found = jnp.zeros(sums.shape, FULL)
    for index, part in enumerate((values, latent, middle[...], result, grad)):
        found = found + jnp.where(lane == index, jnp.sum(part * part), 0.0)
    sums[...] = found


def after(value, *others):
    return lax.optimization_barrier((value, *others))[0]


def swap_blocks(blocks, axis, groups=None):
    return lax.all_to_all(blocks, axis, 0, 0, tiled=True, axis_index_groups=groups)


def shift_z(block, shift):
    if shift == 0:
        return block
    count = lax.axis_size("tensor")
    return lax.ppermute(block, "tensor", [(i, (i + 2 * shift) % count) for i in range(count)])


def shift_tensor(block, shift):
    if shift == 0:
        return block
    count = lax.axis_size("tensor")
    return lax.ppermute(block, "tensor", [(i, (i + shift) % count) for i in range(count)])


def spread_tensor(block):
    count = lax.axis_size("tensor")
    copies = jnp.broadcast_to(block[None], (count,) + block.shape)
    return swap_blocks(copies, "tensor").reshape((count * block.shape[0],) + block.shape[1:])


def column_blocks(values):
    count = lax.axis_size("dp")
    rows, width = values.shape
    return values.reshape(rows, count, width // count).transpose(1, 0, 2)


def per_device(
    hidden_in,
    norm_attn,
    q_weight,
    kv_down,
    kv_norm,
    kv_up,
    out_weight,
    norm_ffn,
    router,
    expert_gate,
    expert_up,
    expert_down,
    shared_gate,
    shared_up,
    shared_down,
    routes,
    cotangent,
):
    tok_rows, width = hidden_in.shape
    dp_count = lax.axis_size("dp")
    tensor_count = lax.axis_size("tensor")
    local_experts = expert_gate.shape[0]
    part_rows = tok_rows // tensor_count
    hidden_part = expert_gate.shape[2]
    heads_local = q_weight.shape[1] // (NOPE + ROPE)
    heads_width = heads_local * (NOPE + VDIM)
    scaling = (NOPE + ROPE) ** (-0.5)
    group_devs = GROUP // tok_rows
    prompt_devs = PROMPT // tok_rows
    dp_place = lax.axis_index("dp")
    tensor_place = lax.axis_index("tensor")
    place = dp_place % group_devs
    quarter = place % prompt_devs
    z_place = tensor_place // 2
    group_base = (dp_place - place) * tok_rows

    def own_part(values):
        return lax.dynamic_slice_in_dim(values, tensor_place * part_rows, part_rows, 0)

    def meta(*entries):
        return jnp.stack([jnp.asarray(entry, jnp.int32) for entry in entries])

    ramp = jnp.arange(tok_rows, dtype=jnp.int32)
    position, unused_seg, unused_group = token_layout(dp_place * tok_rows + ramp)
    cos_table, sin_table = angle_tables(position)
    gain_first, gain_second, gain_kv = norm_attn[None], norm_ffn[None], kv_norm[None]
    down_rows_kv = kv_down.T
    router_rows = router.T
    kv_width = RANK + 2 * ROPE
    own_experts = jnp.arange(dp_count, dtype=jnp.int32) * local_experts + z_place
    chosen = jnp.any(routes.T[None] == own_experts[:, None, None], 1)
    earlier = (ramp[:, None] < ramp[None]).astype(LOW)
    ranking = jnp.dot(chosen.astype(LOW), earlier, preferred_element_type=FULL).astype(jnp.int32)
    slots = jnp.arange(CAP, dtype=jnp.int32)
    dispatch = (
        (chosen[:, None] & (ranking[:, None] == slots[None, :, None]))
        .astype(LOW)
        .reshape(dp_count * CAP, tok_rows)
    )
    combine = dispatch.T

    def take_rows(rows):
        return jnp.dot(dispatch, rows, preferred_element_type=FULL).astype(LOW)

    def to_experts(taken):
        return swap_blocks(taken.reshape(dp_count, CAP, width), "dp").reshape(-1, width)

    taken_grads = take_rows(cotangent)
    grad_rows = to_experts(taken_grads)
    attn_in, packed_own, kv_raw = run_kernel(
        latent_kernel,
        (
            after(hidden_in, taken_grads),
            gain_first,
            down_rows_kv,
            gain_kv,
            cos_table,
            sin_table,
        ),
        [VMEM] * 6,
        [
            ((tok_rows, width), LOW),
            ((tok_rows, kv_width), LOW),
            ((tok_rows, RANK + ROPE), FULL),
        ],
    )
    stacks = lax.optimization_barrier(
        (expert_gate.transpose(0, 2, 1), expert_up.transpose(0, 2, 1), expert_down, packed_own)
    )[:3]
    packed_chunks = []
    for shift in range(local_experts):
        expert = (z_place + shift) % local_experts
        packed = jnp.concatenate(
            [
                lax.dynamic_index_in_dim(stack, expert, 0, keepdims=False)
                for stack in stacks
            ],
            0,
        )
        packed_chunks.append(packed)
    copied = lax.ppermute(
        packed_own,
        "dp",
        [
            (base + i, base + prompt_devs + i)
            for base in range(0, dp_count, group_devs)
            for i in range(prompt_devs)
        ],
    )
    (query,) = run_kernel(
        query_kernel,
        (attn_in, q_weight, cos_table, sin_table),
        [VMEM] * 4,
        [((tok_rows, heads_local * 2 * LANES), LOW)],
    )

    copied = after(copied, query)
    first_block = jnp.where(place < prompt_devs, packed_own, copied)
    chunks = [packed_chunks[0], shift_z(packed_chunks[1], 1), None, shift_z(packed_chunks[3], 3)]
    blocks = [first_block]
    for shift in range(1, prompt_devs):
        blocks.append(
            lax.ppermute(
                first_block,
                "dp",
                [
                    (base + i, base + (i + shift) % prompt_devs)
                    for base in range(0, dp_count, prompt_devs)
                    for i in range(prompt_devs)
                ],
            )
        )
    blocks.append(packed_own)
    attend_meta = meta(
        place, *[(quarter - shift) % prompt_devs for shift in range(prompt_devs)]
    )
    key_rows = len(blocks) * tok_rows
    attn_part, attn_low, kv_heads, log_sum = run_kernel(
        attend_kernel,
        (attend_meta, *blocks, query, kv_up, out_weight),
        [SMEM] + [VMEM] * 8,
        [
            ((tok_rows, width), LOW),
            ((tok_rows, heads_local * VDIM), LOW),
            ((key_rows, heads_width), LOW),
            ((tok_rows, heads_local * LANES), FULL),
        ],
    )
    part_meta = meta(tensor_place)

    def by_part(values):
        return values.reshape(tensor_count, part_rows, values.shape[-1])

    middle, copies = run_kernel(
        middle_kernel,
        (part_meta, swap_blocks(after(by_part(attn_part), grad_rows, packed_chunks[2]), "tensor"), hidden_in, gain_second),
        [SMEM] + [VMEM] * 3,
        [((part_rows, width), FULL), ((tensor_count, part_rows, width), LOW)],
    )
    ffn_in = swap_blocks(after(copies, chunks[1], chunks[3]), "tensor").reshape(tok_rows, width)
    chunks[2] = shift_z(after(packed_chunks[2], chunks[1], chunks[3]), 2)

    taken_rows = take_rows(ffn_in)
    expert_rows = to_experts(taken_rows)

    shared_width = shared_gate.shape[1]
    shared_back, shared_part, shared_grads = run_kernel(
        shared_kernel,
        (after(ffn_in, taken_rows), cotangent, shared_gate.T, shared_up.T, shared_down),
        [VMEM] * 5,
        [
            ((tok_rows, width), FULL),
            ((tok_rows, width), FULL),
            ((3 * shared_width, width), FULL),
        ],
    )
    shared_grads = lax.psum_scatter(shared_grads, "dp", scatter_dimension=1, tiled=True)

    slot_count = dp_count * CAP
    own_hidden = local_experts * hidden_part
    gate_w, up_w, down_w, hidden_back = run_kernel(
        prepare_kernel,
        (after(grad_rows, shared_back), *chunks),
        [VMEM] + [HBM] * 4,
        [((own_hidden, width), LOW)] * 3 + [((slot_count, own_hidden), FULL)],
        [
            pltpu.VMEM((3, own_hidden, width), LOW),
            pltpu.SemaphoreType.DMA((3, 4)),
            pltpu.SemaphoreType.DMA((3,)),
        ],
        [HBM] * 3 + [VMEM],
    )
    back_rows, hidden_low, gate_low, up_low, slot_gate = run_kernel(
        expert_kernel,
        (
            meta(dp_place * local_experts + z_place),
            expert_rows,
            gate_w,
            up_w,
            hidden_back,
            router_rows,
        ),
        [SMEM] + [HBM] * 4 + [VMEM],
        [
            ((slot_count, width + LANES), LOW),
            ((slot_count, own_hidden), LOW),
            ((slot_count, own_hidden), LOW),
            ((slot_count, own_hidden), LOW),
            ((slot_count, LANES), FULL),
        ],
        [
            pltpu.VMEM((slot_count, width), LOW),
            pltpu.VMEM((own_hidden, width), LOW),
            pltpu.VMEM((own_hidden, width), LOW),
            pltpu.VMEM((slot_count, own_hidden), FULL),
            pltpu.VMEM((slot_count, width + LANES), LOW),
            pltpu.SemaphoreType.DMA((5,)),
            pltpu.SemaphoreType.DMA((2,)),
        ],
        [HBM] + [VMEM] * 4,
    )
    back_rows = swap_blocks(back_rows.reshape(dp_count, CAP, width + LANES), "dp").reshape(
        slot_count, width + LANES
    )
    in_grads = run_kernel(
        expert_in_grad_kernel,
        (expert_rows, gate_low, up_low),
        [VMEM] * 3,
        [((hidden_part, width), LOW)] * 8,
    )
    near_homes = [
        [shift_z(in_grads[kind * 4 + shift], local_experts - shift) for shift in (1, 3)]
        for kind in range(2)
    ]
    result_rows, *down_grads = run_kernel(
        expert_out_kernel,
        (grad_rows, hidden_low, slot_gate, down_w),
        [VMEM] * 4,
        [((slot_count, width), LOW)] + [((hidden_part, width), LOW)] * 4,
    )

    payload = run_kernel(
        combine_kernel,
        (
            meta(tensor_place, z_place, local_experts),
            combine,
            after(back_rows, result_rows, *near_homes[0]),
            shared_back,
        ),
        [SMEM] + [VMEM] * 3,
        [((part_rows, width + LANES), LOW)] * tensor_count,
        [pltpu.VMEM((tok_rows, width + LANES), LOW)],
    )
    middle_grad, copies, norm_ffn_grad = run_kernel(
        ffn_back_kernel,
        (
            part_meta,
            after(middle, *near_homes[1]),
            ffn_in,
            router_rows,
            gain_second,
            cotangent,
            *[shift_tensor(block, shift) for shift, block in enumerate(payload)],
        ),
        [SMEM] + [VMEM] * (5 + tensor_count),
        [
            ((part_rows, width), FULL),
            ((tensor_count, part_rows, width + LANES), LOW),
            ((1, width), FULL),
        ],
    )
    result_back = swap_blocks(
        after(result_rows, payload[0]).reshape(dp_count, CAP, width), "dp"
    ).reshape(-1, width)
    (moe_part,) = run_kernel(
        moe_kernel,
        (combine, result_back, shared_part),
        [VMEM] * 3,
        [((tok_rows, width), LOW)],
    )
    spread = swap_blocks(after(copies, result_back), "tensor")
    spread = after(spread, moe_part).reshape(tok_rows, width + LANES)

    got_moe = swap_blocks(after(by_part(moe_part), spread), "tensor")
    far_homes = [shift_z(after(grad, spread), local_experts - 2) for grad in in_grads[2::4]]

    kv_part, heads_low, query_low = run_kernel(
        attend_back_kernel,
        (
            attend_meta,
            out_weight,
            *blocks,
            query,
            kv_heads,
            log_sum,
            kv_up,
            cos_table,
            sin_table,
            spread,
            q_weight,
        ),
        [SMEM] + [VMEM] * 14,
        [
            ((tensor_count, part_rows, len(blocks) * kv_width + width), LOW),
            ((key_rows, heads_width), LOW),
            ((tok_rows, heads_local * (NOPE + ROPE)), LOW),
        ],
    )
    to_owner, kv_own, query_sum = run_kernel(
        kv_sum_kernel,
        (meta(quarter), swap_blocks(after(kv_part, got_moe), "tensor")),
        [SMEM, VMEM],
        [
            ((group_devs, part_rows, kv_width), LOW),
            ((part_rows, kv_width), FULL),
            ((part_rows, width), FULL),
        ],
        [pltpu.VMEM((prompt_devs, part_rows, kv_width), LOW)],
    )
    groups = [
        list(range(base, base + group_devs)) for base in range(0, dp_count, group_devs)
    ]
    got_kv = swap_blocks(after(to_owner, far_homes[0]), "dp", groups)
    down_homes = [
        shift_z(after(down_grads[shift], to_owner), local_experts - shift)
        for shift in range(1, local_experts)
    ]
    copies, norm_attn_grad, kv_norm_grad, square_sums = run_kernel(
        last_kernel,
        (
            part_meta,
            got_kv,
            kv_own,
            kv_raw,
            gain_kv,
            cos_table,
            sin_table,
            down_rows_kv,
            hidden_in,
            gain_first,
            middle_grad,
            got_moe,
            middle,
            query_sum,
        ),
        [SMEM] + [VMEM] * 13,
        [
            ((tensor_count, part_rows, 2 * width + kv_width), LOW),
            ((1, width), FULL),
            ((1, RANK), FULL),
            ((1, LANES), FULL),
        ],
    )
    last = swap_blocks(after(copies, far_homes[1], shared_grads), "tensor").reshape(tok_rows, 2 * width + kv_width)
    output = last[:, width + kv_width :]

    query_width = q_weight.shape[1]
    own_width, own_rank = width // dp_count, RANK // dp_count
    up_lines = own_rank * heads_width // LANES
    attn_width = heads_local * VDIM
    (token_grads,) = run_kernel(
        token_grad_kernel,
        (attn_in, after(query_low, got_moe), attn_low, spread, ffn_in, heads_low, *blocks),
        [VMEM] * (6 + len(blocks)),
        [((query_width + attn_width + EXPERTS + up_lines, width), FULL)],
    )
    token_grads = lax.psum_scatter(token_grads, "dp", scatter_dimension=1, tiled=True)
    ends = [query_width, query_width + attn_width, query_width + attn_width + EXPERTS]
    up_grad = (
        token_grads[ends[2] :]
        .reshape(heads_width // LANES, own_rank, LANES)
        .transpose(1, 0, 2)
        .reshape(own_rank, heads_width)
    )

    homes = [
        [in_grads[kind * 4], near_homes[kind][0], far_homes[kind], near_homes[kind][1]]
        for kind in range(2)
    ] + [[down_grads[0], *down_homes]]
    wgrads = [
        run_kernel(
            place_kernel,
            (meta(z_place), *home),
            [SMEM] + [VMEM] * 4,
            [((local_experts, hidden_part, width), FULL)],
        )[0]
        for home in homes
    ]

    squares = square_sums[0, :5]
    gain_rows = jnp.concatenate(
        [
            norm_attn_grad.reshape(dp_count, -1),
            norm_ffn_grad.reshape(dp_count, -1),
            kv_norm_grad.reshape(dp_count, -1),
            jnp.broadcast_to(squares[None], (dp_count, 5)),
        ],
        -1,
    )
    gain_width = gain_rows.shape[-1]
    gain_rows = jnp.pad(gain_rows, ((0, 0), (0, -gain_width % (8 * LANES))))
    gain_lines = gain_rows.shape[-1] // LANES
    padded = kv_width
    share = padded // tensor_count
    select = (
        jnp.arange(padded, dtype=jnp.int32)[:, None]
        == tensor_place * share + jnp.arange(share, dtype=jnp.int32)[None]
    ).astype(LOW)
    kv_low_share = jnp.dot(last[:, width : width + kv_width], select, preferred_element_type=FULL).astype(LOW)
    down_blocks = column_blocks(contract(kv_low_share, attn_in, 0, 0).astype(LOW))

    def split_low(values):
        high = values.astype(LOW)
        return jnp.concatenate([high, (values - high.astype(FULL)).astype(LOW)], -2)

    def join_low(rows):
        return rows[:, :gain_lines].astype(FULL) + rows[:, gain_lines:].astype(FULL)

    mixed = swap_blocks(
        jnp.concatenate(
            [down_blocks, split_low(gain_rows.reshape(dp_count, gain_lines, LANES))], 1
        ),
        "dp",
    )
    down_share = jnp.sum(mixed[:, :share].astype(FULL), 0)
    gain_share = jnp.sum(join_low(mixed[:, share:]), 0)
    mixed = spread_tensor(
        jnp.concatenate([down_share.astype(LOW), split_low(gain_share)], 0)[None]
    )
    down_grad = mixed[:, :share].reshape(padded, LANES)[: RANK + ROPE].astype(FULL)
    totals = jnp.sum(join_low(mixed[:, share:]), 0).reshape(-1)
    sums = totals[2 * own_width + own_rank : gain_width]
    all_rows = tok_rows * dp_count
    counts = jnp.array([width, RANK, width, width, width], FULL) * all_rows
    return (
        output,
        last[:, :width],
        totals[:own_width],
        token_grads[: ends[0]].T,
        down_grad.T,
        totals[2 * own_width : 2 * own_width + own_rank],
        up_grad,
        token_grads[ends[0] : ends[1]],
        totals[own_width : 2 * own_width],
        token_grads[ends[1] : ends[2]].T,
        wgrads[0].transpose(0, 2, 1),
        wgrads[1].transpose(0, 2, 1),
        wgrads[2],
        shared_grads[:shared_width].T,
        shared_grads[shared_width : 2 * shared_width].T,
        shared_grads[2 * shared_width :],
        jnp.sqrt(sums / counts),
    )


def solution(mesh):
    return jax.shard_map(
        per_device,
        mesh=mesh,
        in_specs=(
            P("dp", None),
            P(),
            P(None, "tensor"),
            P(),
            P(),
            P(None, "tensor"),
            P("tensor", None),
            P(),
            P(),
            P("dp", None, "tensor"),
            P("dp", None, "tensor"),
            P("dp", "tensor", None),
            P(None, "tensor"),
            P(None, "tensor"),
            P("tensor", None),
            P("dp", None),
            P("dp", None),
        ),
        out_specs=(
            P("dp", None),
            P("dp", None),
            P("dp"),
            P("dp", "tensor"),
            P("dp", None),
            P("dp"),
            P("dp", "tensor"),
            P("tensor", "dp"),
            P("dp"),
            P("dp", None),
            P("dp", None, "tensor"),
            P("dp", None, "tensor"),
            P("dp", "tensor", None),
            P("dp", "tensor"),
            P("dp", "tensor"),
            P("tensor", "dp"),
            P(),
        ),
        check_vma=False,
    )
```

```python
import functools

import jax
import jax.numpy as jnp
from jax import lax
from jax.experimental import pallas as pl
from jax.experimental.pallas import tpu as pltpu
from jax.sharding import PartitionSpec as P

NOPE = 128
ROPE = 64
RANK = 512
VDIM = 128
TOP = 6
CAP = 32
PROMPT = 1024
CONT = 128
GROUP = 2048
EXPERTS = 64
LANES = 128
EPSILON = 1e-06
THETA = 10000.0
LOW = jnp.bfloat16
FULL = jnp.float32


def contract(first_arr, second_arr, first_axis, second_axis):
    return lax.dot_general(
        first_arr,
        second_arr,
        (((first_axis,), (second_axis,)), ((), ())),
        preferred_element_type=FULL,
    )


def rotate(values, cos_table, sin_table):
    half_width = values.shape[-1] // 2
    front = values[..., :half_width]
    behind = values[..., half_width:]
    return jnp.concatenate(
        [front * cos_table - behind * sin_table, behind * cos_table + front * sin_table], -1
    )


def token_layout(row_index):
    offset = row_index % GROUP
    in_prompt = offset < PROMPT
    position = jnp.where(in_prompt, offset, PROMPT + (offset - PROMPT) % CONT)
    segment = jnp.where(in_prompt, 0, 1 + (offset - PROMPT) // CONT)
    return (position, segment, row_index // GROUP)


def angle_tables(position):
    half_width = ROPE // 2
    frequency = THETA ** (-2.0 * jnp.arange(half_width, dtype=FULL) / ROPE)
    angles = position.astype(FULL)[:, None] * frequency[None]
    return (jnp.cos(angles), jnp.sin(angles))


def inverse_rms(values):
    return lax.rsqrt(jnp.mean(values * values, -1, keepdims=True) + EPSILON)


def norm_backward(grad_normed, normed, inverse, gain):
    scaled = grad_normed * gain
    return (
        inverse * (scaled - normed * jnp.mean(scaled * normed, -1, keepdims=True)),
        jnp.sum(grad_normed * normed, 0, keepdims=True),
    )


VMEM = pl.BlockSpec(memory_space=pltpu.VMEM)
SMEM = pl.BlockSpec(memory_space=pltpu.SMEM)
HBM = pl.BlockSpec(memory_space=pl.ANY)


def run_kernel(
    kernel, operands, specs, outs, scratch=(), out_specs=None, grid=(), aliases=None, mib=56
):
    shapes = [jax.ShapeDtypeStruct(shape, dtype) for shape, dtype in outs]
    return pl.pallas_call(
        kernel,
        out_shape=shapes,
        grid=grid,
        input_output_aliases=aliases or {},
        in_specs=list(specs),
        out_specs=list(out_specs or [VMEM] * len(shapes)),
        scratch_shapes=list(scratch),
        compiler_params=pltpu.CompilerParams(vmem_limit_bytes=mib * 1024 * 1024),
        cost_estimate=pl.CostEstimate(flops=1000, bytes_accessed=1000, transcendentals=0),
    )(*operands)


def latent_kernel(
    hidden,
    gain,
    down_rows,
    kv_gain,
    cos,
    sin,
    gate,
    up,
    down,
    attn_in,
    packed,
    kv_raw,
    ahead,
    behind,
    held,
    sems,
):
    parts = [[(kind, shift) for kind in range(3)] for shift in (1, 3)]
    picks = RowPicks((gate, up, down), (ahead, behind), parts, held, sems)
    picks.get()
    values = hidden[...].astype(FULL)
    normed = (values * inverse_rms(values) * gain[...]).astype(LOW)
    attn_in[...] = normed
    picks.put()
    raw = contract(normed, down_rows[...], 1, 1)
    kv_raw[...] = raw
    latent = raw[:, :RANK]
    packed[:, :RANK] = (latent * inverse_rms(latent) * kv_gain[...]).astype(LOW)
    rope = rotate(raw[:, RANK:], cos[...], sin[...]).astype(LOW)
    packed[:, RANK:] = jnp.concatenate([rope, jnp.zeros_like(rope)], -1)
    picks.wait()


def turn_queries(attn_in, q_weight, cos, sin, query):
    turned = jnp.dot(attn_in[...], q_weight[...], preferred_element_type=FULL)
    step = NOPE + ROPE
    for head in range(turned.shape[1] // step):
        place = head * 2 * LANES
        start = head * step
        query[:, place : place + NOPE] = turned[:, start : start + NOPE].astype(LOW)
        rope = rotate(turned[:, start + NOPE : start + step], cos[...], sin[...]).astype(LOW)
        query[:, place + NOPE : place + 2 * LANES] = jnp.concatenate(
            [rope, jnp.zeros_like(rope)], -1
        )


def visible_keys(meta, block, shape):
    rows = lax.broadcasted_iota(jnp.int32, shape, 0)
    cols = lax.broadcasted_iota(jnp.int32, shape, 1)
    place, prompt_devs = meta[0], PROMPT // shape[1]
    if block < prompt_devs:
        return cols - rows <= (place - meta[1 + block]) * shape[1]
    own = (cols <= rows) & (rows // CONT == cols // CONT)
    return own & (place >= prompt_devs)


def head_key(heads, rope, head):
    start = head * (NOPE + VDIM)
    return jnp.concatenate([heads[:, start : start + NOPE], rope], -1)


def attend_kernel(
    meta, first, second, third, fourth, own, query, kv_up, out_weight, part, attn, heads, log_sum
):
    blocks = (first, second, third, fourth, own)
    rows = own.shape[0]
    scaling = (NOPE + ROPE) ** (-0.5)
    for block, ref in enumerate(blocks):
        heads[block * rows : (block + 1) * rows] = jnp.dot(
            ref[:, :RANK], kv_up[...], preferred_element_type=FULL
        ).astype(LOW)
    masks = [visible_keys(meta, block, (rows, rows)) for block in range(len(blocks))]
    for head in range(query.shape[1] // (2 * LANES)):
        asked = query[:, head * 2 * LANES : (head + 1) * 2 * LANES]
        scores = []
        for block, ref in enumerate(blocks):
            key = head_key(heads[block * rows : (block + 1) * rows], ref[:, RANK:], head)
            raw = contract(asked, key, 1, 1) * scaling
            scores.append(jnp.where(masks[block], raw, -1e30))
        peak = scores[0]
        for score in scores[1:]:
            peak = jnp.maximum(peak, score)
        peak = jnp.max(peak, -1, keepdims=True)
        weights = [jnp.exp(score - peak) for score in scores]
        total = jnp.sum(functools.reduce(jnp.add, weights), -1, keepdims=True)
        scale = 1.0 / total
        summed = 0.0
        start = head * (NOPE + VDIM) + NOPE
        for block, weight in enumerate(weights):
            value = heads[block * rows : (block + 1) * rows, start : start + VDIM]
            summed = summed + jnp.dot(
                (weight * scale).astype(LOW), value, preferred_element_type=FULL
            )
        attn[:, head * VDIM : (head + 1) * VDIM] = summed.astype(LOW)
        log_sum[:, head * LANES : (head + 1) * LANES] = jnp.broadcast_to(
            peak + jnp.log(total), (rows, LANES)
        )
    part[...] = jnp.dot(attn[...], out_weight[...], preferred_element_type=FULL).astype(LOW)


def middle_kernel(meta, got, hidden, gain, middle, copies):
    part_rows = middle.shape[0]
    start = pl.multiple_of(meta[0] * part_rows, part_rows)
    values = hidden[pl.ds(start, part_rows), :].astype(FULL)
    for index in range(got.shape[0]):
        values = values + got[index].astype(FULL)
    middle[...] = values
    normed = (values * inverse_rms(values) * gain[...]).astype(LOW)
    for index in range(copies.shape[0]):
        copies[index] = normed


def split_cores(grads, keep, send):
    core = lax.axis_index("dp") % 2
    for chip in range(keep.shape[1] // LANES):
        here = slice(chip * LANES, (chip + 1) * LANES)
        first = pl.multiple_of((2 * chip + core) * LANES, LANES)
        other = pl.multiple_of((2 * chip + 1 - core) * LANES, LANES)
        keep[:, here] = grads[:, pl.ds(first, LANES)].astype(LOW)
        send[:, here] = grads[:, pl.ds(other, LANES)].astype(LOW)


def join_cores_kernel(kept, arrived, keep, send):
    side = lax.axis_index("dp") // 2 % 2
    for row in range(keep.shape[1] // LANES):
        here = slice(row * LANES, (row + 1) * LANES)
        for out, which in ((keep, 2 * row + side), (send, 2 * row + 1 - side)):
            there = pl.ds(pl.multiple_of(which * LANES, LANES), LANES)
            total = kept[:, there].astype(FULL) + arrived[:, there].astype(FULL)
            out[:, here] = total.astype(out.dtype)


def join_sides_kernel(kept, arrived, own, *outs):
    place, count = lax.axis_index("dp") // 4, len(outs) + 1
    for shift, out in enumerate((own, *outs)):
        owner = lax.rem(place + shift, count)
        there = pl.ds(pl.multiple_of(owner * LANES, LANES), LANES)
        total = kept[:, there] + arrived[:, there].astype(FULL)
        out[...] = total.astype(out.dtype)


def shared_kernel(ffn, cot, gate, up, down, back, out, keep, send, grads):
    rows = gate.shape[0]
    gate_pre = contract(ffn[...], gate[...], 1, 1)
    up_pre = contract(ffn[...], up[...], 1, 1)
    hidden_back = contract(cot[...], down[...], 1, 1)
    sig = jax.nn.sigmoid(gate_pre)
    low = (gate_pre * sig * up_pre).astype(LOW)
    gate_low = (hidden_back * up_pre * sig * (1.0 + gate_pre * (1.0 - sig))).astype(LOW)
    up_low = (hidden_back * gate_pre * sig).astype(LOW)
    out[...] = jnp.dot(low, down[...], preferred_element_type=FULL).astype(LOW)
    back[...] = (
        jnp.dot(gate_low, gate[...], preferred_element_type=FULL)
        + jnp.dot(up_low, up[...], preferred_element_type=FULL)
    ).astype(LOW)
    grads[:rows] = contract(gate_low, ffn[...], 0, 0)
    grads[rows : 2 * rows] = contract(up_low, ffn[...], 0, 0)
    grads[2 * rows :] = contract(low, cot[...], 0, 0)
    split_cores(grads, keep, send)


class RowPicks:
    def __init__(self, stacks, outs, parts, held, sems):
        count, rows = stacks[0].shape[:2]
        z_place = lax.axis_index("tensor") // 2
        self.gets, self.puts, start = [], [], 0
        for out, wanted in zip(outs, parts):
            first = start
            for kind, shift in wanted:
                source = stacks[kind].at[lax.rem(z_place + shift, count)]
                target = held.at[pl.ds(start, rows)]
                self.gets.append(pltpu.make_async_copy(source, target, sems.at[len(self.gets)]))
                start += rows
            self.puts.append((first, start, out, len(self.gets)))
        self.puts = [
            (
                needed,
                pltpu.make_async_copy(
                    held.at[pl.ds(first, end - first)], out, sems.at[len(self.gets) + index]
                ),
            )
            for index, (first, end, out, needed) in enumerate(self.puts)
        ]

    def get(self):
        for copy in self.gets:
            copy.start()

    def put(self):
        done = 0
        for needed, copy in self.puts:
            for earlier in self.gets[done:needed]:
                earlier.wait()
            done = needed
            copy.start()

    def wait(self):
        for needed, copy in self.puts:
            copy.wait()


def far_pack_kernel(gate, up, down, far, held, sems):
    picks = RowPicks((gate, up, down), (far,), [[(kind, 2) for kind in range(3)]], held, sems)
    picks.get()
    picks.put()
    picks.wait()


def early_kernel(
    attn_in, q_weight, cos, sin, routes, cot, query, dispatch, taken, held, sem
):
    copy = dispatch_rows(routes, cot, dispatch, held, taken, sem)
    turn_queries(attn_in, q_weight, cos, sin, query)
    copy.wait()


def dispatch_rows(routes, cot, dispatch, held, taken, sem):
    owners, tokens = dispatch.shape[0] // CAP, routes.shape[1]
    local_experts = EXPERTS // owners
    owner = lax.broadcasted_iota(jnp.int32, (owners, tokens), 0)
    expert = owner * local_experts + lax.axis_index("tensor") // 2
    chosen = jnp.zeros((owners, tokens), FULL)
    for turn in range(routes.shape[0]):
        chosen = jnp.where(routes[turn : turn + 1, :] == expert, 1.0, chosen)
    square = (tokens, tokens)
    earlier = lax.broadcasted_iota(jnp.int32, square, 0) < lax.broadcasted_iota(
        jnp.int32, square, 1
    )
    ranking = jnp.dot(
        chosen.astype(LOW), earlier.astype(FULL).astype(LOW), preferred_element_type=FULL
    )
    ranking = jnp.where(chosen > 0.0, ranking, -1.0)
    slot = lax.broadcasted_iota(jnp.int32, (CAP, tokens), 0).astype(FULL)
    for index in range(owners):
        dispatch[index * CAP : (index + 1) * CAP] = jnp.where(
            ranking[index : index + 1, :] == slot, 1.0, 0.0
        ).astype(LOW)
    held[...] = jnp.dot(dispatch[...], cot[...], preferred_element_type=FULL).astype(LOW)
    width = cot.shape[1]
    copy = pltpu.make_async_copy(held, taken.at[:, pl.ds(width, width)], sem)
    copy.start()
    return copy


def take_kernel(dispatch, rows, grads, taken, held, sem):
    held[...] = jnp.dot(dispatch[...], rows[...], preferred_element_type=FULL).astype(LOW)
    copy = pltpu.make_async_copy(held, taken.at[:, pl.ds(0, rows.shape[1])], sem)
    copy.start()
    copy.wait()


def chunk_copies(own, pieces, held, sems):
    part = own.shape[1]
    sources = [own.at[lax.axis_index("tensor") // 2]]
    sources += [ref.at[pl.ds(first, part)] for ref, first in pieces]
    return [
        pltpu.make_async_copy(source, held.at[pl.ds(index * part, part)], sems.at[index])
        for index, source in enumerate(sources)
    ]


def expert_kernel(
    meta,
    rows_in,
    gate_in,
    up_in,
    down_in,
    ahead,
    far,
    behind,
    router,
    back,
    hidden_out,
    gate_out,
    up_out,
    slot_gate,
    rows_held,
    grad_held,
    weights,
    out_held,
    row_sems,
    weight_sems,
    out_sems,
):
    count, width = rows_held.shape
    part = gate_in.shape[1]
    get_rows, get_grads = [
        pltpu.make_async_copy(rows_in.at[:, pl.ds(first, width)], held, row_sems.at[index])
        for index, (first, held) in enumerate(((0, rows_held), (width, grad_held)))
    ]
    get_gate, get_up, get_down = [
        chunk_copies(
            own,
            [(ref, kind * part) for ref in (ahead, far, behind)],
            weights.at[kind],
            weight_sems.at[kind],
        )
        for kind, own in enumerate((gate_in, up_in, down_in))
    ]
    gate_w, up_w, down_w = [weights.at[kind] for kind in range(3)]
    split = width + LANES
    puts = [
        pltpu.make_async_copy(
            out_held.at[:, pl.ds(first, size)],
            back.at[:, pl.ds(first, size)],
            out_sems.at[index],
        )
        for index, (first, size) in enumerate(((0, split), (split, width)))
    ]
    for copy in (get_rows, *get_gate, *get_up, get_grads, *get_down):
        copy.start()

    def wait_all(copies):
        for copy in copies:
            copy.wait()

    get_rows.wait()
    rows = rows_held[...]
    logits = contract(rows, router[...], 1, 1)
    logits = jnp.exp(logits - jnp.max(logits, -1, keepdims=True))
    mine = lax.broadcasted_iota(jnp.int32, logits.shape, 1) == meta[0]
    gate = jnp.sum(jnp.where(mine, logits, 0.0), -1, keepdims=True) / jnp.sum(
        logits, -1, keepdims=True
    )
    slot_gate[...] = jnp.broadcast_to(gate, (count, LANES))
    wait_all(get_gate)
    gate_pre = contract(rows, gate_w[...], 1, 1)
    sig = jax.nn.sigmoid(gate_pre)
    wait_all(get_up)
    up_pre = contract(rows, up_w[...], 1, 1)
    low = (gate_pre * sig * up_pre).astype(LOW)
    hidden_out[...] = low
    get_grads.wait()
    wait_all(get_down)
    hidden_back = contract(grad_held[...], down_w[...], 1, 1)
    dots = jnp.sum(low.astype(FULL) * hidden_back, -1, keepdims=True)
    hidden_back = hidden_back * gate
    gate_low = (hidden_back * up_pre * sig * (1.0 + gate_pre * (1.0 - sig))).astype(LOW)
    up_low = (hidden_back * gate_pre * sig).astype(LOW)
    gate_out[...] = gate_low
    up_out[...] = up_low
    out_held[:, :width] = (
        jnp.dot(gate_low, gate_w[...], preferred_element_type=FULL)
        + jnp.dot(up_low, up_w[...], preferred_element_type=FULL)
    ).astype(LOW)
    high = dots.astype(LOW).astype(FULL)
    lane = lax.broadcasted_iota(jnp.int32, (count, LANES), 1)
    out_held[:, width:split] = jnp.where(
        lane == 0, high, jnp.where(lane == 1, dots - high, 0.0)
    ).astype(LOW)
    puts[0].start()
    out_held[:, split:] = (jnp.dot(low, down_w[...], preferred_element_type=FULL) * gate).astype(
        LOW
    )
    puts[1].start()
    wait_all(puts)


def expert_in_grad_kernel(rows, low, *grads):
    part = grads[0].shape[0]
    grad = contract(low[...], rows[...], 0, 0).astype(LOW)
    for index, ref in enumerate(grads):
        ref[...] = grad[index * part : (index + 1) * part]


def expert_out_grad_kernel(grad_in, hidden, slot_gate, *grads):
    part = grads[0].shape[0]
    scaled = (grad_in[...].astype(FULL) * slot_gate[:, :1]).astype(LOW)
    grad = contract(hidden[...], scaled, 0, 0).astype(LOW)
    for index, ref in enumerate(grads):
        ref[...] = grad[index * part : (index + 1) * part]


def combine_kernel(meta, combine, returned, shared_back, shared_part, payload):
    width = shared_back.shape[1]
    payload[:, :width] = (
        jnp.dot(combine[...], returned[:, :width], preferred_element_type=FULL)
        + shared_back[...].astype(FULL)
    ).astype(LOW)
    slot_rows = returned.shape[0]
    slot = lax.broadcasted_iota(jnp.int32, (slot_rows, EXPERTS), 0) // CAP
    at_expert = slot * meta[1] + meta[0] == lax.broadcasted_iota(
        jnp.int32, (slot_rows, EXPERTS), 1
    )
    dots = returned[:, width : width + LANES].astype(FULL)
    summed = 0.0
    for index in range(2):
        columns = jnp.where(at_expert, dots[:, index : index + 1], 0.0).astype(LOW)
        summed = summed + jnp.dot(combine[...], columns, preferred_element_type=FULL)
    high = summed.astype(LOW)
    rest = (summed - high.astype(FULL)).astype(LOW)
    payload[:, width : width + LANES] = jnp.concatenate([high, rest], -1)
    payload[:, width + LANES :] = (
        jnp.dot(combine[...], returned[:, width + LANES :], preferred_element_type=FULL)
        + shared_part[...].astype(FULL)
    ).astype(LOW)


def token_grad_kernel(attn_in, query_low, attn_low, spread, ffn, heads_low, *refs):
    blocks, (grads, output) = refs[:-2], refs[-2:]
    width = attn_in.shape[1]
    output[...] = spread[:, width + LANES :]
    rows = attn_in.shape[0]
    start = query_low.shape[1]
    grads[:start] = contract(query_low[...], attn_in[...], 0, 0)
    end = start + attn_low.shape[1]
    grads[start:end] = contract(attn_low[...], spread[:, :width], 0, 0)
    start, end = end, end + EXPERTS
    grads[start:end] = contract(spread[:, width : width + LANES], ffn[...], 0, 0)[:EXPERTS]
    total = 0.0
    for index, ref in enumerate(blocks):
        total = total + contract(ref[:, :RANK], heads_low[index * rows : (index + 1) * rows], 0, 0)
    owners = width // LANES
    lines = total.shape[0] // owners
    for column in range(total.shape[1] // LANES):
        for owner in range(owners):
            grads[
                end + column * lines : end + (column + 1) * lines,
                owner * LANES : (owner + 1) * LANES,
            ] = total[owner * lines : (owner + 1) * lines, column * LANES : (column + 1) * LANES]


def place_kernel(meta, first, second, third, fourth, out):
    for shift, chunk in enumerate((first, second, third, fourth)):
        out[lax.rem(meta[0] + shift, out.shape[0])] = chunk[...].astype(FULL)


def ffn_back_kernel(
    meta, middle, ffn, router, gain, cot, got, middle_grad, copies, gain_grad, sums
):
    part_rows, width = middle.shape
    start = pl.multiple_of(meta[0] * part_rows, part_rows)
    here = pl.ds(start, part_rows)
    total = got[0].astype(FULL)
    for index in range(1, got.shape[0]):
        total = total + got[index].astype(FULL)
    extra = total[:, width : width + LANES]
    prob_grad = extra[:, :EXPERTS] + extra[:, EXPERTS:]
    logits = contract(ffn[here, :], router[...], 1, 1)
    logits = jnp.exp(logits - jnp.max(logits, -1, keepdims=True))
    prob = logits / jnp.sum(logits, -1, keepdims=True)
    logit_low = (
        prob * (prob_grad - jnp.sum(prob * prob_grad, -1, keepdims=True))
    ).astype(LOW)
    ffn_grad = total[:, :width] + jnp.dot(logit_low, router[...], preferred_element_type=FULL)
    values = middle[...]
    inverse = inverse_rms(values)
    back, gains = norm_backward(ffn_grad, values * inverse, inverse, gain[...])
    gain_grad[...] = gains
    grad = cot[here, :].astype(FULL) + back
    middle_grad[...] = grad
    low = grad.astype(LOW)
    tail = jnp.concatenate([logit_low, jnp.zeros_like(logit_low)], -1)
    result = values + total[:, width + LANES :]
    result_low = result.astype(LOW)
    for index in range(copies.shape[0]):
        copies[index, :, :width] = low
        copies[index, :, width : width + LANES] = tail
        copies[index, :, width + LANES :] = result_low
    lane = lax.broadcasted_iota(jnp.int32, sums.shape, 1)
    sums[...] = jnp.where(lane == 2, jnp.sum(values * values), 0.0) + jnp.where(
        lane == 3, jnp.sum(result * result), 0.0
    )


def attend_back_kernel(
    meta,
    out_weight,
    first,
    second,
    third,
    fourth,
    own,
    query,
    heads,
    log_sum,
    kv_up,
    cos,
    sin,
    spread,
    q_weight,
    kv_part,
    query_part,
    heads_low,
    query_low,
):
    blocks = (first, second, third, fourth, own)
    rows = own.shape[0]
    parts, part_rows, _ = kv_part.shape
    kv_width = RANK + 2 * ROPE
    scaling = (NOPE + ROPE) ** (-0.5)
    attn_grad = contract(spread[:, : out_weight.shape[1]], out_weight[...], 1, 1).astype(LOW)
    masks = [visible_keys(meta, block, (rows, rows)) for block in range(len(blocks))]
    ropes = [0.0] * len(blocks)
    step = NOPE + ROPE
    for head in range(query.shape[1] // (2 * LANES)):
        asked = query[:, head * 2 * LANES : (head + 1) * 2 * LANES]
        out_grad = attn_grad[:, head * VDIM : (head + 1) * VDIM]
        logs = log_sum[:, head * LANES : head * LANES + 1]
        start = head * (NOPE + VDIM)
        probs, backs = [], []
        summed = 0.0
        for block, ref in enumerate(blocks):
            here = slice(block * rows, (block + 1) * rows)
            key = head_key(heads[here], ref[:, RANK:], head)
            raw = contract(asked, key, 1, 1) * scaling
            prob = jnp.exp(jnp.where(masks[block], raw, -1e30) - logs)
            back = contract(out_grad, heads[here, start + NOPE : start + NOPE + VDIM], 1, 1)
            summed = summed + prob * back
            probs.append(prob)
            backs.append(back)
        total = jnp.sum(summed, -1, keepdims=True)
        asked_grad = 0.0
        for block, ref in enumerate(blocks):
            here = slice(block * rows, (block + 1) * rows)
            score_low = (scaling * probs[block] * (backs[block] - total)).astype(LOW)
            key = head_key(heads[here], ref[:, RANK:], head)
            asked_grad = asked_grad + jnp.dot(score_low, key, preferred_element_type=FULL)
            key_grad = contract(score_low, asked, 0, 0)
            heads_low[here, start : start + NOPE] = key_grad[:, :NOPE].astype(LOW)
            heads_low[here, start + NOPE : start + NOPE + VDIM] = contract(
                probs[block].astype(LOW), out_grad, 0, 0
            ).astype(LOW)
            ropes[block] = ropes[block] + key_grad[:, NOPE:]
        query_low[:, head * step : head * step + NOPE] = asked_grad[:, :NOPE].astype(LOW)
        query_low[:, head * step + NOPE : (head + 1) * step] = rotate(
            asked_grad[:, NOPE:step], cos[...], -sin[...]
        ).astype(LOW)
    for block in range(len(blocks)):
        here = slice(block * rows, (block + 1) * rows)
        latent = contract(heads_low[here], kv_up[...], 1, 1).astype(LOW)
        rope = ropes[block].astype(LOW)
        start = block * kv_width
        for index in range(parts):
            mine = slice(index * part_rows, (index + 1) * part_rows)
            kv_part[index, :, start : start + RANK] = latent[mine]
            kv_part[index, :, start + RANK : start + kv_width] = rope[mine]
    query_part[...] = contract(query_low[...], q_weight[...], 1, 1).astype(LOW)


def kv_sum_kernel(got, first, second, third, fourth, own):
    kv_width = own.shape[1]
    total = got[0].astype(FULL)
    for index in range(1, got.shape[0]):
        total = total + got[index].astype(FULL)
    blocks = (first, second, third, fourth)
    for block, out in enumerate(blocks):
        out[...] = total[:, block * kv_width : (block + 1) * kv_width].astype(LOW)
    own[...] = total[:, len(blocks) * kv_width :]


def kv_join_kernel(first, second, third, fourth, out):
    total = first[...].astype(FULL) + second[...].astype(FULL)
    out[...] = (total + third[...].astype(FULL) + fourth[...].astype(FULL)).astype(LOW)


def last_kernel(
    meta,
    joined,
    other,
    own,
    kv_raw,
    kv_gain,
    cos,
    sin,
    down_rows,
    hidden,
    gain,
    middle_grad,
    sums_in,
    got_query,
    copies,
    grad_low,
    gain_grad,
    kv_gain_grad,
    sums,
):
    part_rows, width = middle_grad.shape
    here = pl.ds(pl.multiple_of(meta[0] * part_rows, part_rows), part_rows)
    in_prompt = meta[1] < PROMPT // hidden.shape[0]
    found = joined[...].astype(FULL) + other[...].astype(FULL)
    total = jnp.where(in_prompt, found, own[...])
    latent = kv_raw[here, :RANK]
    inverse = inverse_rms(latent)
    latent_grad, kv_gains = norm_backward(
        total[:, :RANK], latent * inverse, inverse, kv_gain[...]
    )
    kv_gain_grad[...] = kv_gains
    rope = rotate(total[:, RANK : RANK + ROPE], cos[here, :], -sin[here, :]).astype(LOW)
    latent_low = latent_grad.astype(LOW)
    kv_low = jnp.concatenate([latent_low, rope], -1)
    tail = jnp.concatenate([rope, jnp.zeros_like(rope)], -1)
    for index in range(copies.shape[0]):
        copies[index, :, :RANK] = latent_low
        copies[index, :, RANK:] = tail
    attn_in_grad = jnp.dot(kv_low, down_rows[...], preferred_element_type=FULL)
    for index in range(got_query.shape[0]):
        attn_in_grad = attn_in_grad + got_query[index].astype(FULL)
    values = hidden[here, :].astype(FULL)
    inverse = inverse_rms(values)
    back, gains = norm_backward(attn_in_grad, values * inverse, inverse, gain[...])
    gain_grad[...] = gains
    grad = middle_grad[...] + back
    grad_low[...] = grad.astype(LOW)
    lane = lax.broadcasted_iota(jnp.int32, sums.shape, 1)
    found = sums_in[...]
    for index, part in ((0, values), (1, latent), (4, grad)):
        found = found + jnp.where(lane == index, jnp.sum(part * part), 0.0)
    sums[...] = found


def split_rows(rows):
    high = [row.astype(LOW).astype(FULL) for row in rows]
    low = [row - part for row, part in zip(rows, high)]
    blank = jnp.zeros((16 - 2 * len(rows), LANES), FULL)
    return jnp.concatenate(high + low + [blank], 0).astype(LOW)


def mix_kernel(meta, kv_low, attn_in, attn_gain, ffn_gain, kv_gain, sums, payload):
    owners, rows, _ = payload.shape
    share = rows - 16
    shape = (kv_low.shape[1], share)
    pick = lax.broadcasted_iota(jnp.int32, shape, 0) == meta[0] * share + lax.broadcasted_iota(
        jnp.int32, shape, 1
    )
    mine = jnp.dot(
        kv_low[...], pick.astype(FULL).astype(LOW), preferred_element_type=FULL
    ).astype(LOW)
    grad = contract(mine, attn_in[...], 0, 0).astype(LOW)
    own_rank = RANK // owners
    blank = jnp.zeros((1, LANES - own_rank), FULL)
    for owner in range(owners):
        here = slice(owner * LANES, (owner + 1) * LANES)
        payload[owner, :share] = grad[:, here]
        own_kv = jnp.concatenate(
            [kv_gain[:, owner * own_rank : (owner + 1) * own_rank], blank], -1
        )
        payload[owner, share:] = split_rows(
            [attn_gain[:, here], ffn_gain[:, here], own_kv, sums[...]]
        )


def join_rows(rows, count=4):
    values = rows.astype(FULL)
    return [values[i : i + 1] + values[count + i : count + i + 1] for i in range(count)]


def mix_sum_kernel(got, copies):
    share = got.shape[1] - 16
    total = got[0].astype(FULL)
    for index in range(1, got.shape[0]):
        total = total + got[index].astype(FULL)
    mixed = jnp.concatenate(
        [total[:share].astype(LOW), split_rows(join_rows(total[share:]))], 0
    )
    for index in range(copies.shape[0]):
        copies[index] = mixed


def final_kernel(
    got,
    tokens,
    *refs,
):
    grads, refs = refs[: got.shape[0]], refs[got.shape[0] :]
    shared, refs = refs[:4], refs[4:]
    input_grad, down_grad, attn_gain, ffn_gain, kv_gain, rms = refs[:6]
    query_grad, up_grad, out_grad, router_grad = refs[6:10]
    gate_grad, shared_up_grad, shared_down_grad, held = refs[10:]
    count, share, _ = got.shape
    share = share - 16
    rows, width = grads[0].shape
    gains = 0.0
    for index in range(count):
        owner = lax.rem(lax.axis_index("tensor") + count - index, count)
        input_grad[pl.ds(pl.multiple_of(owner * rows, rows), rows), :] = grads[index][...]
        held[index * share : (index + 1) * share] = got[index, :share].astype(FULL)
        gains = gains + jnp.concatenate(join_rows(got[index, share:]), 0)
    down_grad[...] = held[: down_grad.shape[0]]
    attn_gain[...] = gains[0:1]
    ffn_gain[...] = gains[1:2]
    kv_gain[...] = gains[2:3]
    entries = jnp.where(
        lax.broadcasted_iota(jnp.int32, rms.shape, 1) == 1, float(RANK), float(width)
    )
    rms[...] = jnp.sqrt(gains[3:4] / (entries * (rows * count * lax.axis_size("dp"))))
    start = query_grad.shape[1]
    query_grad[...] = tokens[:start].T
    end = start + out_grad.shape[0]
    out_grad[...] = tokens[start:end]
    router_grad[...] = tokens[end : end + EXPERTS]
    lines = up_grad.shape[0]
    for column in range(up_grad.shape[1] // LANES):
        first = end + EXPERTS + column * lines
        up_grad[:, column * LANES : (column + 1) * LANES] = tokens[first : first + lines]
    rows = gate_grad.shape[0]
    for index, out in enumerate((gate_grad, shared_up_grad, shared_down_grad)):
        here = slice(index * rows, (index + 1) * rows)
        total = shared[0][here]
        for ref in shared[1:]:
            total = total + ref[here].astype(FULL)
        out[...] = total


def after(value, *others):
    return lax.optimization_barrier((value, *others))[0]


def swap_blocks(blocks, axis, groups=None):
    return lax.all_to_all(blocks, axis, 0, 0, tiled=True, axis_index_groups=groups)


def shift_z(block, shift):
    if shift == 0:
        return block
    count = lax.axis_size("tensor")
    return lax.ppermute(block, "tensor", [(i, (i + 2 * shift) % count) for i in range(count)])


def shift_tensor(block, shift):
    if shift == 0:
        return block
    count = lax.axis_size("tensor")
    return lax.ppermute(block, "tensor", [(i, (i + shift) % count) for i in range(count)])


def per_device(
    hidden_in,
    norm_attn,
    q_weight,
    kv_down,
    kv_norm,
    kv_up,
    out_weight,
    norm_ffn,
    router,
    expert_gate,
    expert_up,
    expert_down,
    shared_gate,
    shared_up,
    shared_down,
    routes,
    cotangent,
):
    tok_rows, width = hidden_in.shape
    dp_count = lax.axis_size("dp")
    tensor_count = lax.axis_size("tensor")
    local_experts = expert_gate.shape[0]
    part_rows = tok_rows // tensor_count
    hidden_part = expert_gate.shape[2]
    heads_local = q_weight.shape[1] // (NOPE + ROPE)
    heads_width = heads_local * (NOPE + VDIM)
    scaling = (NOPE + ROPE) ** (-0.5)
    group_devs = GROUP // tok_rows
    prompt_devs = PROMPT // tok_rows
    dp_place = lax.axis_index("dp")
    tensor_place = lax.axis_index("tensor")
    place = dp_place % group_devs
    quarter = place % prompt_devs
    z_place = tensor_place // 2
    group_base = (dp_place - place) * tok_rows

    def own_part(values):
        return lax.dynamic_slice_in_dim(values, tensor_place * part_rows, part_rows, 0)

    def meta(*entries):
        return jnp.stack([jnp.asarray(entry, jnp.int32) for entry in entries])

    ramp = jnp.arange(tok_rows, dtype=jnp.int32)
    position, unused_seg, unused_group = token_layout(dp_place * tok_rows + ramp)
    cos_table, sin_table = angle_tables(position)
    gain_first, gain_second, gain_kv = norm_attn[None], norm_ffn[None], kv_norm[None]
    down_rows_kv = kv_down.T
    router_rows = router.T
    kv_width = RANK + 2 * ROPE
    stacks = [expert_gate.transpose(0, 2, 1), expert_up.transpose(0, 2, 1), expert_down]
    near_rows = 3 * hidden_part
    slot_count = dp_count * CAP
    attn_in, packed_own, kv_raw, pack_ahead, pack_behind = run_kernel(
        latent_kernel,
        (hidden_in, gain_first, down_rows_kv, gain_kv, cos_table, sin_table, *stacks),
        [VMEM] * 6 + [HBM] * 3,
        [
            ((tok_rows, width), LOW),
            ((tok_rows, kv_width), LOW),
            ((tok_rows, RANK + ROPE), FULL),
            ((near_rows, width), LOW),
            ((near_rows, width), LOW),
        ],
        [pltpu.VMEM((2 * near_rows, width), LOW), pltpu.SemaphoreType.DMA((8,))],
        [VMEM] * 3 + [HBM] * 2,
    )
    ahead, behind = shift_z(pack_ahead, 1), shift_z(pack_behind, 3)
    copied = lax.ppermute(
        packed_own,
        "dp",
        [
            (base + i, base + prompt_devs + i)
            for base in range(0, dp_count, group_devs)
            for i in range(prompt_devs)
        ],
    )
    query, dispatch, taken_grads = run_kernel(
        early_kernel,
        (after(attn_in, copied), q_weight, cos_table, sin_table, routes.T, cotangent),
        [VMEM] * 6,
        [
            ((tok_rows, heads_local * 2 * LANES), LOW),
            ((slot_count, tok_rows), LOW),
            ((slot_count, 2 * width), LOW),
        ],
        [pltpu.VMEM((slot_count, width), LOW), pltpu.SemaphoreType.DMA],
        [VMEM] * 2 + [HBM],
    )
    combine = dispatch.T
    (pack_far,) = run_kernel(
        far_pack_kernel,
        (*stacks[:2], after(stacks[2], query)),
        [HBM] * 3,
        [((near_rows, width), LOW)],
        [pltpu.VMEM((near_rows, width), LOW), pltpu.SemaphoreType.DMA((4,))],
        [HBM],
    )
    first_block = jnp.where(place < prompt_devs, packed_own, copied)
    blocks = [first_block]
    for shift in range(1, prompt_devs):
        blocks.append(
            lax.ppermute(
                first_block,
                "dp",
                [
                    (base + i, base + (i + shift) % prompt_devs)
                    for base in range(0, dp_count, prompt_devs)
                    for i in range(prompt_devs)
                ],
            )
        )
    blocks.append(packed_own)
    attend_meta = meta(
        place, *[(quarter - shift) % prompt_devs for shift in range(prompt_devs)]
    )
    key_rows = len(blocks) * tok_rows
    attn_part, attn_low, kv_heads, log_sum = run_kernel(
        attend_kernel,
        (attend_meta, *blocks, query, kv_up, out_weight),
        [SMEM] + [VMEM] * 8,
        [
            ((tok_rows, width), LOW),
            ((tok_rows, heads_local * VDIM), LOW),
            ((key_rows, heads_width), LOW),
            ((tok_rows, heads_local * LANES), FULL),
        ],
    )
    part_meta = meta(tensor_place)

    def by_part(values):
        return values.reshape(tensor_count, part_rows, values.shape[-1])

    middle, copies = run_kernel(
        middle_kernel,
        (part_meta, swap_blocks(by_part(attn_part), "tensor"), hidden_in, gain_second),
        [SMEM] + [VMEM] * 3,
        [((part_rows, width), FULL), ((tensor_count, part_rows, width), LOW)],
    )
    ffn_in = swap_blocks(after(copies, ahead, behind, pack_far), "tensor").reshape(tok_rows, width)

    (taken_rows,) = run_kernel(
        take_kernel,
        (dispatch, ffn_in, taken_grads),
        [VMEM] * 2 + [HBM],
        [((slot_count, 2 * width), LOW)],
        [pltpu.VMEM((slot_count, width), LOW), pltpu.SemaphoreType.DMA],
        [HBM],
        aliases={2: 0},
    )
    expert_rows = swap_blocks(taken_rows.reshape(dp_count, CAP, 2 * width), "dp").reshape(
        slot_count, 2 * width
    )
    far = shift_z(after(pack_far, taken_rows), 2)

    shared_width = shared_gate.shape[1]
    shared_back, shared_part, shared_keep, shared_send = run_kernel(
        shared_kernel,
        (after(ffn_in, taken_rows), cotangent, shared_gate.T, shared_up.T, shared_down),
        [VMEM] * 5,
        [
            ((tok_rows, width), LOW),
            ((tok_rows, width), LOW),
            ((3 * shared_width, width // 2), LOW),
            ((3 * shared_width, width // 2), LOW),
        ],
        [pltpu.VMEM((3 * shared_width, width), FULL)],
        mib=32,
    )

    def exchange_dp(block, flip):
        return lax.ppermute(block, "dp", [(i, i ^ flip) for i in range(dp_count)])

    def join_cores(keep, arrived):
        shape = (keep.shape[0], keep.shape[1] // 2)
        return run_kernel(
            join_cores_kernel, (keep, arrived), [VMEM] * 2, [(shape, FULL), (shape, LOW)],
        mib=16,
    )

    def join_sides(keep, arrived):
        shape = (keep.shape[0], LANES)
        return run_kernel(
            join_sides_kernel, (keep, arrived), [VMEM] * 2, [(shape, FULL)] + [(shape, LOW)] * 3
        )

    def along_x(blocks):
        return [
            lax.ppermute(block, "dp", [(i, (i + 4 * shift) % dp_count) for i in range(dp_count)])
            for shift, block in enumerate(blocks, 1)
        ]

    shared_keep, shared_send = join_cores(shared_keep, after(exchange_dp(shared_send, 1), far))
    shared_arrived = exchange_dp(after(shared_send, expert_rows), 2)

    own_hidden = local_experts * hidden_part
    wide = 2 * width + LANES
    back_rows, hidden_low, gate_low, up_low, slot_gate = run_kernel(
        expert_kernel,
        (
            meta(dp_place * local_experts + z_place),
            expert_rows,
            *stacks,
            ahead,
            far,
            behind,
            after(router_rows, shared_keep),
        ),
        [SMEM] + [HBM] * 7 + [VMEM],
        [
            ((slot_count, wide), LOW),
            ((slot_count, own_hidden), LOW),
            ((slot_count, own_hidden), LOW),
            ((slot_count, own_hidden), LOW),
            ((slot_count, LANES), FULL),
        ],
        [
            pltpu.VMEM((slot_count, width), LOW),
            pltpu.VMEM((slot_count, width), LOW),
            pltpu.VMEM((3, own_hidden, width), LOW),
            pltpu.VMEM((slot_count, wide), LOW),
            pltpu.SemaphoreType.DMA((2,)),
            pltpu.SemaphoreType.DMA((3, 4)),
            pltpu.SemaphoreType.DMA((2,)),
        ],
        [HBM] + [VMEM] * 4,
        mib=44,
    )

    back_rows = swap_blocks(
        after(back_rows, shared_arrived).reshape(dp_count, CAP, wide), "dp"
    ).reshape(slot_count, wide)
    shared_own, *shared_blocks = join_sides(shared_keep, shared_arrived)
    turns = 2
    step = width // turns

    def weight_grad(kernel, operands, first):
        whole = [pl.BlockSpec(v.shape, lambda turn: (0, 0)) for v in operands]
        return run_kernel(
            kernel,
            (expert_rows, *operands),
            [pl.BlockSpec((slot_count, step), lambda turn: (0, first * turns + turn))] + whole,
            [((hidden_part, width), LOW)] * local_experts,
            out_specs=[pl.BlockSpec((hidden_part, step), lambda turn: (0, turn))] * local_experts,
            grid=(turns,),
            mib=20,
        )

    in_grads = [weight_grad(expert_in_grad_kernel, (low,), 0) for low in (gate_low, up_low)]
    down_grads = weight_grad(expert_out_grad_kernel, (hidden_low, slot_gate), 1)
    back_rows = after(
        back_rows, in_grads[0][0], in_grads[1][0], down_grads[0], shared_own
    )
    early = [(0, 1), (0, 3), (1, 1), (1, 3), (0, 2)]
    early_homes = {
        (kind, shift): shift_z(in_grads[kind][shift], local_experts - shift)
        for kind, shift in early
    }

    (payload,) = run_kernel(
        combine_kernel,
        (
            meta(z_place, local_experts),
            combine,
            after(back_rows, down_grads[0], *early_homes.values()),
            shared_back,
            shared_part,
        ),
        [SMEM] + [VMEM] * 4,
        [((tok_rows, wide), LOW)],
        mib=24,
    )
    middle_grad, copies, norm_ffn_grad, middle_sums = run_kernel(
        ffn_back_kernel,
        (
            part_meta,
            middle,
            ffn_in,
            router_rows,
            gain_second,
            cotangent,
            swap_blocks(by_part(payload), "tensor"),
        ),
        [SMEM] + [VMEM] * 6,
        [
            ((part_rows, width), FULL),
            ((tensor_count, part_rows, wide), LOW),
            ((1, width), FULL),
            ((1, LANES), FULL),
        ],
        mib=20,
    )
    shared_blocks = along_x(lax.optimization_barrier((*shared_blocks, payload))[:-1])
    shared_blocks = [shared_own, *shared_blocks]
    spread = after(swap_blocks(copies, "tensor"), *shared_blocks).reshape(tok_rows, wide)
    late_homes = {(1, 2): shift_z(after(in_grads[1][2], spread), local_experts - 2)}

    kv_part, query_part, heads_low, query_low = run_kernel(
        attend_back_kernel,
        (
            attend_meta,
            out_weight,
            *blocks,
            query,
            kv_heads,
            log_sum,
            kv_up,
            cos_table,
            sin_table,
            spread,
            q_weight,
        ),
        [SMEM] + [VMEM] * 14,
        [
            ((tensor_count, part_rows, len(blocks) * kv_width), LOW),
            ((tok_rows, width), LOW),
            ((key_rows, heads_width), LOW),
            ((tok_rows, heads_local * (NOPE + ROPE)), LOW),
        ],
    )
    *prompt_parts, kv_own = run_kernel(
        kv_sum_kernel,
        (swap_blocks(after(kv_part, late_homes[1, 2]), "tensor"),),
        [VMEM],
        [((part_rows, kv_width), LOW)] * prompt_devs + [((part_rows, kv_width), FULL)],
    )
    (joined,) = run_kernel(
        kv_join_kernel,
        [prompt_parts[0]]
        + [
            lax.ppermute(
                prompt_parts[shift],
                "dp",
                [
                    (base + i, base + (i - shift) % prompt_devs)
                    for base in range(0, dp_count, prompt_devs)
                    for i in range(prompt_devs)
                ],
            )
            for shift in range(1, prompt_devs)
        ],
        [VMEM] * prompt_devs,
        [((part_rows, kv_width), LOW)],
    )
    other = lax.ppermute(
        joined,
        "dp",
        [
            (base + prompt_devs + i, base + i)
            for base in range(0, dp_count, group_devs)
            for i in range(prompt_devs)
        ],
    )
    got_query = swap_blocks(after(by_part(query_part), kv_own), "tensor")
    for shift in (1, 3, 2):
        late_homes[2, shift] = shift_z(after(down_grads[shift], kv_own), local_experts - shift)

    def place_grads(kind):
        grads = (*in_grads, down_grads)[kind]
        arrived = early_homes | late_homes
        return run_kernel(
            place_kernel,
            (
                meta(z_place),
                grads[0],
                *[arrived[kind, shift] for shift in range(1, local_experts)],
            ),
            [SMEM] + [VMEM] * 4,
            [((local_experts, hidden_part, width), FULL)],
        )[0]

    gate_wgrad = place_grads(0)
    copies, grad_low, norm_attn_grad, kv_norm_grad, square_sums = run_kernel(
        last_kernel,
        (
            meta(tensor_place, place),
            joined,
            other,
            kv_own,
            kv_raw,
            gain_kv,
            cos_table,
            sin_table,
            down_rows_kv,
            hidden_in,
            gain_first,
            after(middle_grad, gate_wgrad),
            middle_sums,
            got_query,
        ),
        [SMEM] + [VMEM] * 13,
        [
            ((tensor_count, part_rows, kv_width), LOW),
            ((part_rows, width), LOW),
            ((1, width), FULL),
            ((1, RANK), FULL),
            ((1, LANES), FULL),
        ],
    )
    up_wgrad = place_grads(1)
    kv_low_all = swap_blocks(copies, "tensor").reshape(tok_rows, kv_width)
    down_wgrad = place_grads(2)

    query_width = q_weight.shape[1]
    own_width, own_rank = width // dp_count, RANK // dp_count
    up_lines = own_rank * heads_width // LANES
    attn_width = heads_local * VDIM
    token_rows = query_width + attn_width + EXPERTS + up_lines
    token_grads, output = run_kernel(
        token_grad_kernel,
        (attn_in, query_low, attn_low, spread, ffn_in, heads_low, *blocks),
        [VMEM] * (6 + len(blocks)),
        [
            ((token_rows, width), FULL),
            ((tok_rows, width), LOW),
        ],
        mib=28,
    )
    token_grads = lax.psum_scatter(
        after(token_grads, kv_own), "dp", scatter_dimension=1, tiled=True
    )
    share = kv_width // tensor_count
    (mixed,) = run_kernel(
        mix_kernel,
        (
            part_meta,
            after(kv_low_all, up_wgrad, late_homes[2, 1], late_homes[2, 3]),
            attn_in,
            norm_attn_grad,
            norm_ffn_grad,
            kv_norm_grad,
            square_sums,
        ),
        [SMEM] + [VMEM] * 6,
        [((dp_count, share + 16, LANES), LOW)],
        mib=16,
    )
    (copies,) = run_kernel(
        mix_sum_kernel,
        (after(swap_blocks(mixed, "dp"), late_homes[2, 2]),),
        [VMEM],
        [((tensor_count, share + 16, LANES), LOW)],
        mib=16,
    )
    grad_low = after(grad_low, kv_low_all)
    grad_parts = [shift_tensor(grad_low, shift) for shift in range(tensor_count)]
    shared_width = shared_gate.shape[1]
    (
        input_grad,
        down_grad,
        attn_gain,
        ffn_gain,
        kv_gain,
        rms,
        query_grad,
        up_grad,
        out_grad,
        router_grad,
        *shared_out,
    ) = run_kernel(
        final_kernel,
        (swap_blocks(copies, "tensor"), token_grads, *grad_parts, *shared_blocks),
        [VMEM] * (2 + tensor_count + len(shared_blocks)),
        [
            ((tok_rows, width), LOW),
            ((RANK + ROPE, own_width), FULL),
            ((1, LANES), FULL),
            ((1, LANES), FULL),
            ((1, LANES), FULL),
            ((1, LANES), FULL),
            ((own_width, query_width), FULL),
            ((own_rank, heads_width), FULL),
            ((attn_width, own_width), FULL),
            ((EXPERTS, own_width), FULL),
        ]
        + [((shared_width, own_width), FULL)] * 3,
        [pltpu.VMEM((kv_width, LANES), FULL)],
        mib=16,
    )
    return (
        output,
        input_grad,
        attn_gain.reshape(own_width),
        query_grad,
        down_grad.T,
        kv_gain[0, :own_rank],
        up_grad,
        out_grad,
        ffn_gain.reshape(own_width),
        router_grad.T,
        gate_wgrad.transpose(0, 2, 1),
        up_wgrad.transpose(0, 2, 1),
        down_wgrad,
        shared_out[0].T,
        shared_out[1].T,
        shared_out[2],
        rms[0, :5],
    )


def solution(mesh):
    return jax.shard_map(
        per_device,
        mesh=mesh,
        in_specs=(
            P("dp", None),
            P(),
            P(None, "tensor"),
            P(),
            P(),
            P(None, "tensor"),
            P("tensor", None),
            P(),
            P(),
            P("dp", None, "tensor"),
            P("dp", None, "tensor"),
            P("dp", "tensor", None),
            P(None, "tensor"),
            P(None, "tensor"),
            P("tensor", None),
            P("dp", None),
            P("dp", None),
        ),
        out_specs=(
            P("dp", None),
            P("dp", None),
            P("dp"),
            P("dp", "tensor"),
            P("dp", None),
            P("dp"),
            P("dp", "tensor"),
            P("tensor", "dp"),
            P("dp"),
            P("dp", None),
            P("dp", None, "tensor"),
            P("dp", None, "tensor"),
            P("dp", "tensor", None),
            P("dp", "tensor"),
            P("dp", "tensor"),
            P("tensor", "dp"),
            P(),
        ),
        check_vma=False,
    )
```

```python
import functools

import jax
import jax.numpy as jnp
from jax import lax
from jax.experimental import pallas as pl
from jax.experimental.pallas import tpu as pltpu
from jax.sharding import PartitionSpec as P

NOPE = 128
ROPE = 64
RANK = 512
VDIM = 128
TOP = 6
CAP = 32
PROMPT = 1024
CONT = 128
GROUP = 2048
EXPERTS = 64
LANES = 128
EPSILON = 1e-06
THETA = 10000.0
LOW = jnp.bfloat16
FULL = jnp.float32


def contract(first_arr, second_arr, first_axis, second_axis):
    return lax.dot_general(
        first_arr,
        second_arr,
        (((first_axis,), (second_axis,)), ((), ())),
        preferred_element_type=FULL,
    )


def rotate(values, cos_table, sin_table):
    half_width = values.shape[-1] // 2
    front = values[..., :half_width]
    behind = values[..., half_width:]
    return jnp.concatenate(
        [front * cos_table - behind * sin_table, behind * cos_table + front * sin_table], -1
    )


def token_layout(row_index):
    offset = row_index % GROUP
    in_prompt = offset < PROMPT
    position = jnp.where(in_prompt, offset, PROMPT + (offset - PROMPT) % CONT)
    segment = jnp.where(in_prompt, 0, 1 + (offset - PROMPT) // CONT)
    return (position, segment, row_index // GROUP)


def angle_tables(position):
    half_width = ROPE // 2
    frequency = THETA ** (-2.0 * jnp.arange(half_width, dtype=FULL) / ROPE)
    angles = position.astype(FULL)[:, None] * frequency[None]
    return (jnp.cos(angles), jnp.sin(angles))


def inverse_rms(values):
    return lax.rsqrt(jnp.mean(values * values, -1, keepdims=True) + EPSILON)


def norm_backward(grad_normed, normed, inverse, gain):
    scaled = grad_normed * gain
    return (
        inverse * (scaled - normed * jnp.mean(scaled * normed, -1, keepdims=True)),
        jnp.sum(grad_normed * normed, 0, keepdims=True),
    )


VMEM = pl.BlockSpec(memory_space=pltpu.VMEM)
SMEM = pl.BlockSpec(memory_space=pltpu.SMEM)
HBM = pl.BlockSpec(memory_space=pl.ANY)


def run_kernel(
    kernel, operands, specs, outs, scratch=(), out_specs=None, grid=(), aliases=None, mib=56
):
    shapes = [jax.ShapeDtypeStruct(shape, dtype) for shape, dtype in outs]
    return pl.pallas_call(
        kernel,
        out_shape=shapes,
        grid=grid,
        input_output_aliases=aliases or {},
        in_specs=list(specs),
        out_specs=list(out_specs or [VMEM] * len(shapes)),
        scratch_shapes=list(scratch),
        compiler_params=pltpu.CompilerParams(vmem_limit_bytes=mib * 1024 * 1024),
        cost_estimate=pl.CostEstimate(flops=1000, bytes_accessed=1000, transcendentals=0),
    )(*operands)


def latent_kernel(
    hidden,
    gain,
    down_rows,
    kv_gain,
    cos,
    sin,
    gate,
    up,
    down,
    attn_in,
    packed,
    kv_raw,
    ahead,
    behind,
    held,
    sems,
):
    parts = [[(kind, shift) for kind in range(3)] for shift in (1, 3)]
    picks = RowPicks((gate, up, down), (ahead, behind), parts, held, sems)
    picks.get()
    values = hidden[...].astype(FULL)
    normed = (values * inverse_rms(values) * gain[...]).astype(LOW)
    attn_in[...] = normed
    picks.put()
    raw = contract(normed, down_rows[...], 1, 1)
    kv_raw[...] = raw
    latent = raw[:, :RANK]
    packed[:, :RANK] = (latent * inverse_rms(latent) * kv_gain[...]).astype(LOW)
    rope = rotate(raw[:, RANK:], cos[...], sin[...]).astype(LOW)
    packed[:, RANK:] = jnp.concatenate([rope, jnp.zeros_like(rope)], -1)
    picks.wait()


def turn_queries(attn_in, q_weight, cos, sin, query):
    turned = jnp.dot(attn_in[...], q_weight[...], preferred_element_type=FULL)
    step = NOPE + ROPE
    for head in range(turned.shape[1] // step):
        place = head * 2 * LANES
        start = head * step
        query[:, place : place + NOPE] = turned[:, start : start + NOPE].astype(LOW)
        rope = rotate(turned[:, start + NOPE : start + step], cos[...], sin[...]).astype(LOW)
        query[:, place + NOPE : place + 2 * LANES] = jnp.concatenate(
            [rope, jnp.zeros_like(rope)], -1
        )


def visible_keys(meta, block, shape):
    rows = lax.broadcasted_iota(jnp.int32, shape, 0)
    cols = lax.broadcasted_iota(jnp.int32, shape, 1)
    place, prompt_devs = meta[0], PROMPT // shape[1]
    if block < prompt_devs:
        return cols - rows <= (place - meta[1 + block]) * shape[1]
    own = (cols <= rows) & (rows // CONT == cols // CONT)
    return own & (place >= prompt_devs)


def head_key(heads, rope, head):
    start = head * (NOPE + VDIM)
    return jnp.concatenate([heads[:, start : start + NOPE], rope], -1)


def attend_kernel(
    meta, first, second, third, fourth, own, query, kv_up, out_weight, part, attn, heads, log_sum
):
    blocks = (first, second, third, fourth, own)
    rows = own.shape[0]
    scaling = (NOPE + ROPE) ** (-0.5)
    for block, ref in enumerate(blocks):
        heads[block * rows : (block + 1) * rows] = jnp.dot(
            ref[:, :RANK], kv_up[...], preferred_element_type=FULL
        ).astype(LOW)
    masks = [visible_keys(meta, block, (rows, rows)) for block in range(len(blocks))]
    for head in range(query.shape[1] // (2 * LANES)):
        asked = query[:, head * 2 * LANES : (head + 1) * 2 * LANES]
        scores = []
        for block, ref in enumerate(blocks):
            key = head_key(heads[block * rows : (block + 1) * rows], ref[:, RANK:], head)
            raw = contract(asked, key, 1, 1) * scaling
            scores.append(jnp.where(masks[block], raw, -1e30))
        peak = scores[0]
        for score in scores[1:]:
            peak = jnp.maximum(peak, score)
        peak = jnp.max(peak, -1, keepdims=True)
        weights = [jnp.exp(score - peak) for score in scores]
        total = jnp.sum(functools.reduce(jnp.add, weights), -1, keepdims=True)
        scale = 1.0 / total
        summed = 0.0
        start = head * (NOPE + VDIM) + NOPE
        for block, weight in enumerate(weights):
            value = heads[block * rows : (block + 1) * rows, start : start + VDIM]
            summed = summed + jnp.dot(
                (weight * scale).astype(LOW), value, preferred_element_type=FULL
            )
        attn[:, head * VDIM : (head + 1) * VDIM] = summed.astype(LOW)
        log_sum[:, head * LANES : (head + 1) * LANES] = jnp.broadcast_to(
            peak + jnp.log(total), (rows, LANES)
        )
    part[...] = jnp.dot(attn[...], out_weight[...], preferred_element_type=FULL).astype(LOW)


def middle_kernel(meta, got, hidden, gain, middle, copies):
    part_rows = middle.shape[0]
    start = pl.multiple_of(meta[0] * part_rows, part_rows)
    values = hidden[pl.ds(start, part_rows), :].astype(FULL)
    for index in range(got.shape[0]):
        values = values + got[index].astype(FULL)
    middle[...] = values
    normed = (values * inverse_rms(values) * gain[...]).astype(LOW)
    for index in range(copies.shape[0]):
        copies[index] = normed


def split_cores(grads, keep, send):
    core = lax.axis_index("dp") % 2
    for chip in range(keep.shape[1] // LANES):
        here = slice(chip * LANES, (chip + 1) * LANES)
        first = pl.multiple_of((2 * chip + core) * LANES, LANES)
        other = pl.multiple_of((2 * chip + 1 - core) * LANES, LANES)
        keep[:, here] = grads[:, pl.ds(first, LANES)].astype(LOW)
        send[:, here] = grads[:, pl.ds(other, LANES)].astype(LOW)


def join_cores_kernel(kept, arrived, keep, send):
    side = lax.axis_index("dp") // 2 % 2
    for row in range(keep.shape[1] // LANES):
        here = slice(row * LANES, (row + 1) * LANES)
        for out, which in ((keep, 2 * row + side), (send, 2 * row + 1 - side)):
            there = pl.ds(pl.multiple_of(which * LANES, LANES), LANES)
            total = kept[:, there].astype(FULL) + arrived[:, there].astype(FULL)
            out[:, here] = total.astype(out.dtype)


def join_sides_kernel(kept, arrived, own, *outs):
    place, count = lax.axis_index("dp") // 4, len(outs) + 1
    for shift, out in enumerate((own, *outs)):
        owner = lax.rem(place + shift, count)
        there = pl.ds(pl.multiple_of(owner * LANES, LANES), LANES)
        total = kept[:, there] + arrived[:, there].astype(FULL)
        out[...] = total.astype(out.dtype)


def shared_kernel(ffn, cot, gate, up, down, back, out, keep, send, grads):
    rows = gate.shape[0]
    gate_pre = contract(ffn[...], gate[...], 1, 1)
    up_pre = contract(ffn[...], up[...], 1, 1)
    hidden_back = contract(cot[...], down[...], 1, 1)
    sig = jax.nn.sigmoid(gate_pre)
    low = (gate_pre * sig * up_pre).astype(LOW)
    gate_low = (hidden_back * up_pre * sig * (1.0 + gate_pre * (1.0 - sig))).astype(LOW)
    up_low = (hidden_back * gate_pre * sig).astype(LOW)
    out[...] = jnp.dot(low, down[...], preferred_element_type=FULL).astype(LOW)
    back[...] = (
        jnp.dot(gate_low, gate[...], preferred_element_type=FULL)
        + jnp.dot(up_low, up[...], preferred_element_type=FULL)
    ).astype(LOW)
    grads[:rows] = contract(gate_low, ffn[...], 0, 0)
    grads[rows : 2 * rows] = contract(up_low, ffn[...], 0, 0)
    grads[2 * rows :] = contract(low, cot[...], 0, 0)
    split_cores(grads, keep, send)


class RowPicks:
    def __init__(self, stacks, outs, parts, held, sems):
        count, rows = stacks[0].shape[:2]
        z_place = lax.axis_index("tensor") // 2
        self.gets, self.puts, start = [], [], 0
        for out, wanted in zip(outs, parts):
            first = start
            for kind, shift in wanted:
                source = stacks[kind].at[lax.rem(z_place + shift, count)]
                target = held.at[pl.ds(start, rows)]
                self.gets.append(pltpu.make_async_copy(source, target, sems.at[len(self.gets)]))
                start += rows
            self.puts.append((first, start, out, len(self.gets)))
        self.puts = [
            (
                needed,
                pltpu.make_async_copy(
                    held.at[pl.ds(first, end - first)], out, sems.at[len(self.gets) + index]
                ),
            )
            for index, (first, end, out, needed) in enumerate(self.puts)
        ]

    def get(self):
        for copy in self.gets:
            copy.start()

    def put(self):
        done = 0
        for needed, copy in self.puts:
            for earlier in self.gets[done:needed]:
                earlier.wait()
            done = needed
            copy.start()

    def wait(self):
        for needed, copy in self.puts:
            copy.wait()


def far_pack_kernel(gate, up, down, far, held, sems):
    picks = RowPicks((gate, up, down), (far,), [[(kind, 2) for kind in range(3)]], held, sems)
    picks.get()
    picks.put()
    picks.wait()


def early_kernel(
    attn_in, q_weight, cos, sin, routes, cot, query, dispatch, taken, held, sem
):
    copy = dispatch_rows(routes, cot, dispatch, held, taken, sem)
    turn_queries(attn_in, q_weight, cos, sin, query)
    copy.wait()


def dispatch_rows(routes, cot, dispatch, held, taken, sem):
    owners, tokens = dispatch.shape[0] // CAP, routes.shape[1]
    local_experts = EXPERTS // owners
    owner = lax.broadcasted_iota(jnp.int32, (owners, tokens), 0)
    expert = owner * local_experts + lax.axis_index("tensor") // 2
    chosen = jnp.zeros((owners, tokens), FULL)
    for turn in range(routes.shape[0]):
        chosen = jnp.where(routes[turn : turn + 1, :] == expert, 1.0, chosen)
    square = (tokens, tokens)
    earlier = lax.broadcasted_iota(jnp.int32, square, 0) < lax.broadcasted_iota(
        jnp.int32, square, 1
    )
    ranking = jnp.dot(
        chosen.astype(LOW), earlier.astype(FULL).astype(LOW), preferred_element_type=FULL
    )
    ranking = jnp.where(chosen > 0.0, ranking, -1.0)
    slot = lax.broadcasted_iota(jnp.int32, (CAP, tokens), 0).astype(FULL)
    for index in range(owners):
        dispatch[index * CAP : (index + 1) * CAP] = jnp.where(
            ranking[index : index + 1, :] == slot, 1.0, 0.0
        ).astype(LOW)
    held[...] = jnp.dot(dispatch[...], cot[...], preferred_element_type=FULL).astype(LOW)
    width = cot.shape[1]
    copy = pltpu.make_async_copy(held, taken.at[:, pl.ds(width, width)], sem)
    copy.start()
    return copy


def take_kernel(dispatch, rows, grads, taken, held, sem):
    held[...] = jnp.dot(dispatch[...], rows[...], preferred_element_type=FULL).astype(LOW)
    copy = pltpu.make_async_copy(held, taken.at[:, pl.ds(0, rows.shape[1])], sem)
    copy.start()
    copy.wait()


def chunk_copies(own, pieces, held, sems):
    part = own.shape[1]
    sources = [own.at[lax.axis_index("tensor") // 2]]
    sources += [ref.at[pl.ds(first, part)] for ref, first in pieces]
    return [
        pltpu.make_async_copy(source, held.at[pl.ds(index * part, part)], sems.at[index])
        for index, source in enumerate(sources)
    ]


def expert_kernel(
    meta,
    rows_in,
    gate_in,
    up_in,
    down_in,
    ahead,
    far,
    behind,
    router,
    back,
    hidden_out,
    gate_out,
    up_out,
    slot_gate,
    rows_held,
    grad_held,
    weights,
    out_held,
    row_sems,
    weight_sems,
    out_sems,
):
    count, width = rows_held.shape
    part = gate_in.shape[1]
    get_rows, get_grads = [
        pltpu.make_async_copy(rows_in.at[:, pl.ds(first, width)], held, row_sems.at[index])
        for index, (first, held) in enumerate(((0, rows_held), (width, grad_held)))
    ]
    get_gate, get_up, get_down = [
        chunk_copies(
            own,
            [(ref, kind * part) for ref in (ahead, far, behind)],
            weights.at[kind],
            weight_sems.at[kind],
        )
        for kind, own in enumerate((gate_in, up_in, down_in))
    ]
    gate_w, up_w, down_w = [weights.at[kind] for kind in range(3)]
    split = width + LANES
    puts = [
        pltpu.make_async_copy(
            out_held.at[:, pl.ds(first, size)],
            back.at[:, pl.ds(first, size)],
            out_sems.at[index],
        )
        for index, (first, size) in enumerate(((0, split), (split, width)))
    ]
    for copy in (get_rows, *get_gate, *get_up, get_grads, *get_down):
        copy.start()

    def wait_all(copies):
        for copy in copies:
            copy.wait()

    get_rows.wait()
    rows = rows_held[...]
    logits = contract(rows, router[...], 1, 1)
    logits = jnp.exp(logits - jnp.max(logits, -1, keepdims=True))
    mine = lax.broadcasted_iota(jnp.int32, logits.shape, 1) == meta[0]
    gate = jnp.sum(jnp.where(mine, logits, 0.0), -1, keepdims=True) / jnp.sum(
        logits, -1, keepdims=True
    )
    slot_gate[...] = jnp.broadcast_to(gate, (count, LANES))
    wait_all(get_gate)
    gate_pre = contract(rows, gate_w[...], 1, 1)
    sig = jax.nn.sigmoid(gate_pre)
    wait_all(get_up)
    up_pre = contract(rows, up_w[...], 1, 1)
    low = (gate_pre * sig * up_pre).astype(LOW)
    hidden_out[...] = low
    get_grads.wait()
    wait_all(get_down)
    hidden_back = contract(grad_held[...], down_w[...], 1, 1)
    dots = jnp.sum(low.astype(FULL) * hidden_back, -1, keepdims=True)
    hidden_back = hidden_back * gate
    gate_low = (hidden_back * up_pre * sig * (1.0 + gate_pre * (1.0 - sig))).astype(LOW)
    up_low = (hidden_back * gate_pre * sig).astype(LOW)
    gate_out[...] = gate_low
    up_out[...] = up_low
    out_held[:, :width] = (
        jnp.dot(gate_low, gate_w[...], preferred_element_type=FULL)
        + jnp.dot(up_low, up_w[...], preferred_element_type=FULL)
    ).astype(LOW)
    high = dots.astype(LOW).astype(FULL)
    lane = lax.broadcasted_iota(jnp.int32, (count, LANES), 1)
    out_held[:, width:split] = jnp.where(
        lane == 0, high, jnp.where(lane == 1, dots - high, 0.0)
    ).astype(LOW)
    puts[0].start()
    out_held[:, split:] = (jnp.dot(low, down_w[...], preferred_element_type=FULL) * gate).astype(
        LOW
    )
    puts[1].start()
    wait_all(puts)


def expert_in_grad_kernel(rows, low, *grads):
    part = grads[0].shape[0]
    grad = contract(low[...], rows[...], 0, 0).astype(LOW)
    for index, ref in enumerate(grads):
        ref[...] = grad[index * part : (index + 1) * part]


def expert_out_grad_kernel(grad_in, hidden, slot_gate, *grads):
    part = grads[0].shape[0]
    scaled = (grad_in[...].astype(FULL) * slot_gate[:, :1]).astype(LOW)
    grad = contract(hidden[...], scaled, 0, 0).astype(LOW)
    for index, ref in enumerate(grads):
        ref[...] = grad[index * part : (index + 1) * part]


def combine_kernel(meta, combine, returned, shared_back, shared_part, payload):
    width = shared_back.shape[1]
    payload[:, :width] = (
        jnp.dot(combine[...], returned[:, :width], preferred_element_type=FULL)
        + shared_back[...].astype(FULL)
    ).astype(LOW)
    slot_rows = returned.shape[0]
    slot = lax.broadcasted_iota(jnp.int32, (slot_rows, EXPERTS), 0) // CAP
    at_expert = slot * meta[1] + meta[0] == lax.broadcasted_iota(
        jnp.int32, (slot_rows, EXPERTS), 1
    )
    dots = returned[:, width : width + LANES].astype(FULL)
    summed = 0.0
    for index in range(2):
        columns = jnp.where(at_expert, dots[:, index : index + 1], 0.0).astype(LOW)
        summed = summed + jnp.dot(combine[...], columns, preferred_element_type=FULL)
    high = summed.astype(LOW)
    rest = (summed - high.astype(FULL)).astype(LOW)
    payload[:, width : width + LANES] = jnp.concatenate([high, rest], -1)
    payload[:, width + LANES :] = (
        jnp.dot(combine[...], returned[:, width + LANES :], preferred_element_type=FULL)
        + shared_part[...].astype(FULL)
    ).astype(LOW)


def token_grad_kernel(attn_in, query_low, attn_low, spread, ffn, heads_low, *refs):
    blocks, (grads, output) = refs[:-2], refs[-2:]
    width = attn_in.shape[1]
    output[...] = spread[:, width + LANES :]
    rows = attn_in.shape[0]
    start = query_low.shape[1]
    grads[:start] = contract(query_low[...], attn_in[...], 0, 0)
    end = start + attn_low.shape[1]
    grads[start:end] = contract(attn_low[...], spread[:, :width], 0, 0)
    start, end = end, end + EXPERTS
    grads[start:end] = contract(spread[:, width : width + LANES], ffn[...], 0, 0)[:EXPERTS]
    total = 0.0
    for index, ref in enumerate(blocks):
        total = total + contract(ref[:, :RANK], heads_low[index * rows : (index + 1) * rows], 0, 0)
    owners = width // LANES
    lines = total.shape[0] // owners
    for column in range(total.shape[1] // LANES):
        for owner in range(owners):
            grads[
                end + column * lines : end + (column + 1) * lines,
                owner * LANES : (owner + 1) * LANES,
            ] = total[owner * lines : (owner + 1) * lines, column * LANES : (column + 1) * LANES]


def place_kernel(meta, first, second, third, fourth, out):
    for shift, chunk in enumerate((first, second, third, fourth)):
        out[lax.rem(meta[0] + shift, out.shape[0])] = chunk[...].astype(FULL)


def ffn_back_kernel(
    meta, middle, ffn, router, gain, cot, got, middle_grad, copies, gain_grad, sums
):
    part_rows, width = middle.shape
    start = pl.multiple_of(meta[0] * part_rows, part_rows)
    here = pl.ds(start, part_rows)
    total = got[0].astype(FULL)
    for index in range(1, got.shape[0]):
        total = total + got[index].astype(FULL)
    extra = total[:, width : width + LANES]
    prob_grad = extra[:, :EXPERTS] + extra[:, EXPERTS:]
    logits = contract(ffn[here, :], router[...], 1, 1)
    logits = jnp.exp(logits - jnp.max(logits, -1, keepdims=True))
    prob = logits / jnp.sum(logits, -1, keepdims=True)
    logit_low = (
        prob * (prob_grad - jnp.sum(prob * prob_grad, -1, keepdims=True))
    ).astype(LOW)
    ffn_grad = total[:, :width] + jnp.dot(logit_low, router[...], preferred_element_type=FULL)
    values = middle[...]
    inverse = inverse_rms(values)
    back, gains = norm_backward(ffn_grad, values * inverse, inverse, gain[...])
    gain_grad[...] = gains
    grad = cot[here, :].astype(FULL) + back
    middle_grad[...] = grad
    low = grad.astype(LOW)
    tail = jnp.concatenate([logit_low, jnp.zeros_like(logit_low)], -1)
    result = values + total[:, width + LANES :]
    result_low = result.astype(LOW)
    for index in range(copies.shape[0]):
        copies[index, :, :width] = low
        copies[index, :, width : width + LANES] = tail
        copies[index, :, width + LANES :] = result_low
    lane = lax.broadcasted_iota(jnp.int32, sums.shape, 1)
    sums[...] = jnp.where(lane == 2, jnp.sum(values * values), 0.0) + jnp.where(
        lane == 3, jnp.sum(result * result), 0.0
    )


def attend_back_kernel(
    meta,
    out_weight,
    first,
    second,
    third,
    fourth,
    own,
    query,
    heads,
    log_sum,
    kv_up,
    cos,
    sin,
    spread,
    q_weight,
    kv_part,
    query_part,
    heads_low,
    query_low,
):
    blocks = (first, second, third, fourth, own)
    rows = own.shape[0]
    parts, part_rows, _ = kv_part.shape
    kv_width = RANK + 2 * ROPE
    scaling = (NOPE + ROPE) ** (-0.5)
    attn_grad = contract(spread[:, : out_weight.shape[1]], out_weight[...], 1, 1).astype(LOW)
    masks = [visible_keys(meta, block, (rows, rows)) for block in range(len(blocks))]
    ropes = [0.0] * len(blocks)
    step = NOPE + ROPE
    for head in range(query.shape[1] // (2 * LANES)):
        asked = query[:, head * 2 * LANES : (head + 1) * 2 * LANES]
        out_grad = attn_grad[:, head * VDIM : (head + 1) * VDIM]
        logs = log_sum[:, head * LANES : head * LANES + 1]
        start = head * (NOPE + VDIM)
        probs, backs = [], []
        summed = 0.0
        for block, ref in enumerate(blocks):
            here = slice(block * rows, (block + 1) * rows)
            key = head_key(heads[here], ref[:, RANK:], head)
            raw = contract(asked, key, 1, 1) * scaling
            prob = jnp.exp(jnp.where(masks[block], raw, -1e30) - logs)
            back = contract(out_grad, heads[here, start + NOPE : start + NOPE + VDIM], 1, 1)
            summed = summed + prob * back
            probs.append(prob)
            backs.append(back)
        total = jnp.sum(summed, -1, keepdims=True)
        asked_grad = 0.0
        for block, ref in enumerate(blocks):
            here = slice(block * rows, (block + 1) * rows)
            score_low = (scaling * probs[block] * (backs[block] - total)).astype(LOW)
            key = head_key(heads[here], ref[:, RANK:], head)
            asked_grad = asked_grad + jnp.dot(score_low, key, preferred_element_type=FULL)
            key_grad = contract(score_low, asked, 0, 0)
            heads_low[here, start : start + NOPE] = key_grad[:, :NOPE].astype(LOW)
            heads_low[here, start + NOPE : start + NOPE + VDIM] = contract(
                probs[block].astype(LOW), out_grad, 0, 0
            ).astype(LOW)
            ropes[block] = ropes[block] + key_grad[:, NOPE:]
        query_low[:, head * step : head * step + NOPE] = asked_grad[:, :NOPE].astype(LOW)
        query_low[:, head * step + NOPE : (head + 1) * step] = rotate(
            asked_grad[:, NOPE:step], cos[...], -sin[...]
        ).astype(LOW)
    for block in range(len(blocks)):
        here = slice(block * rows, (block + 1) * rows)
        latent = contract(heads_low[here], kv_up[...], 1, 1).astype(LOW)
        rope = ropes[block].astype(LOW)
        start = block * kv_width
        for index in range(parts):
            mine = slice(index * part_rows, (index + 1) * part_rows)
            kv_part[index, :, start : start + RANK] = latent[mine]
            kv_part[index, :, start + RANK : start + kv_width] = rope[mine]
    query_part[...] = contract(query_low[...], q_weight[...], 1, 1).astype(LOW)


def kv_sum_kernel(got, first, second, third, fourth, own):
    kv_width = own.shape[1]
    total = got[0].astype(FULL)
    for index in range(1, got.shape[0]):
        total = total + got[index].astype(FULL)
    blocks = (first, second, third, fourth)
    for block, out in enumerate(blocks):
        out[...] = total[:, block * kv_width : (block + 1) * kv_width].astype(LOW)
    own[...] = total[:, len(blocks) * kv_width :]


def kv_join_kernel(first, second, third, fourth, out):
    total = first[...].astype(FULL) + second[...].astype(FULL)
    out[...] = (total + third[...].astype(FULL) + fourth[...].astype(FULL)).astype(LOW)


def last_kernel(
    meta,
    joined,
    other,
    own,
    kv_raw,
    kv_gain,
    cos,
    sin,
    down_rows,
    hidden,
    gain,
    middle_grad,
    sums_in,
    got_query,
    copies,
    grad_low,
    gain_grad,
    kv_gain_grad,
    sums,
):
    part_rows, width = middle_grad.shape
    here = pl.ds(pl.multiple_of(meta[0] * part_rows, part_rows), part_rows)
    in_prompt = meta[1] < PROMPT // hidden.shape[0]
    found = joined[...].astype(FULL) + other[...].astype(FULL)
    total = jnp.where(in_prompt, found, own[...])
    latent = kv_raw[here, :RANK]
    inverse = inverse_rms(latent)
    latent_grad, kv_gains = norm_backward(
        total[:, :RANK], latent * inverse, inverse, kv_gain[...]
    )
    kv_gain_grad[...] = kv_gains
    rope = rotate(total[:, RANK : RANK + ROPE], cos[here, :], -sin[here, :]).astype(LOW)
    latent_low = latent_grad.astype(LOW)
    kv_low = jnp.concatenate([latent_low, rope], -1)
    tail = jnp.concatenate([rope, jnp.zeros_like(rope)], -1)
    for index in range(copies.shape[0]):
        copies[index, :, :RANK] = latent_low
        copies[index, :, RANK:] = tail
    attn_in_grad = jnp.dot(kv_low, down_rows[...], preferred_element_type=FULL)
    for index in range(got_query.shape[0]):
        attn_in_grad = attn_in_grad + got_query[index].astype(FULL)
    values = hidden[here, :].astype(FULL)
    inverse = inverse_rms(values)
    back, gains = norm_backward(attn_in_grad, values * inverse, inverse, gain[...])
    gain_grad[...] = gains
    grad = middle_grad[...] + back
    grad_low[...] = grad.astype(LOW)
    lane = lax.broadcasted_iota(jnp.int32, sums.shape, 1)
    found = sums_in[...]
    for index, part in ((0, values), (1, latent), (4, grad)):
        found = found + jnp.where(lane == index, jnp.sum(part * part), 0.0)
    sums[...] = found


def split_rows(rows):
    high = [row.astype(LOW).astype(FULL) for row in rows]
    low = [row - part for row, part in zip(rows, high)]
    blank = jnp.zeros((16 - 2 * len(rows), LANES), FULL)
    return jnp.concatenate(high + low + [blank], 0).astype(LOW)


def mix_kernel(meta, kv_low, attn_in, attn_gain, ffn_gain, kv_gain, sums, payload):
    owners, rows, _ = payload.shape
    share = rows - 16
    shape = (kv_low.shape[1], share)
    pick = lax.broadcasted_iota(jnp.int32, shape, 0) == meta[0] * share + lax.broadcasted_iota(
        jnp.int32, shape, 1
    )
    mine = jnp.dot(
        kv_low[...], pick.astype(FULL).astype(LOW), preferred_element_type=FULL
    ).astype(LOW)
    grad = contract(mine, attn_in[...], 0, 0).astype(LOW)
    own_rank = RANK // owners
    blank = jnp.zeros((1, LANES - own_rank), FULL)
    for owner in range(owners):
        here = slice(owner * LANES, (owner + 1) * LANES)
        payload[owner, :share] = grad[:, here]
        own_kv = jnp.concatenate(
            [kv_gain[:, owner * own_rank : (owner + 1) * own_rank], blank], -1
        )
        payload[owner, share:] = split_rows(
            [attn_gain[:, here], ffn_gain[:, here], own_kv, sums[...]]
        )


def join_rows(rows, count=4):
    values = rows.astype(FULL)
    return [values[i : i + 1] + values[count + i : count + i + 1] for i in range(count)]


def mix_sum_kernel(got, copies):
    share = got.shape[1] - 16
    total = got[0].astype(FULL)
    for index in range(1, got.shape[0]):
        total = total + got[index].astype(FULL)
    mixed = jnp.concatenate(
        [total[:share].astype(LOW), split_rows(join_rows(total[share:]))], 0
    )
    for index in range(copies.shape[0]):
        copies[index] = mixed


def final_kernel(
    got,
    tokens,
    *refs,
):
    grads, refs = refs[: got.shape[0]], refs[got.shape[0] :]
    shared, refs = refs[:4], refs[4:]
    input_grad, down_grad, attn_gain, ffn_gain, kv_gain, rms = refs[:6]
    query_grad, up_grad, out_grad, router_grad = refs[6:10]
    gate_grad, shared_up_grad, shared_down_grad, held = refs[10:]
    count, share, _ = got.shape
    share = share - 16
    rows, width = grads[0].shape
    gains = 0.0
    for index in range(count):
        owner = lax.rem(lax.axis_index("tensor") + count - index, count)
        input_grad[pl.ds(pl.multiple_of(owner * rows, rows), rows), :] = grads[index][...]
        held[index * share : (index + 1) * share] = got[index, :share].astype(FULL)
        gains = gains + jnp.concatenate(join_rows(got[index, share:]), 0)
    down_grad[...] = held[: down_grad.shape[0]]
    attn_gain[...] = gains[0:1]
    ffn_gain[...] = gains[1:2]
    kv_gain[...] = gains[2:3, : kv_gain.shape[1]]
    entries = jnp.where(
        lax.broadcasted_iota(jnp.int32, rms.shape, 1) == 1, float(RANK), float(width)
    )
    rms[...] = jnp.sqrt(
        gains[3:4, : rms.shape[1]] / (entries * (rows * count * lax.axis_size("dp")))
    )
    start = query_grad.shape[1]
    query_grad[...] = tokens[:start].T
    end = start + out_grad.shape[0]
    out_grad[...] = tokens[start:end]
    router_grad[...] = tokens[end : end + EXPERTS]
    lines = up_grad.shape[0]
    for column in range(up_grad.shape[1] // LANES):
        first = end + EXPERTS + column * lines
        up_grad[:, column * LANES : (column + 1) * LANES] = tokens[first : first + lines]
    rows = gate_grad.shape[0]
    for index, out in enumerate((gate_grad, shared_up_grad, shared_down_grad)):
        here = slice(index * rows, (index + 1) * rows)
        total = shared[0][here]
        for ref in shared[1:]:
            total = total + ref[here].astype(FULL)
        out[...] = total


def after(value, *others):
    return lax.optimization_barrier((value, *others))[0]


def swap_blocks(blocks, axis, groups=None):
    return lax.all_to_all(blocks, axis, 0, 0, tiled=True, axis_index_groups=groups)


def shift_z(block, shift):
    if shift == 0:
        return block
    count = lax.axis_size("tensor")
    return lax.ppermute(block, "tensor", [(i, (i + 2 * shift) % count) for i in range(count)])


def shift_tensor(block, shift):
    if shift == 0:
        return block
    count = lax.axis_size("tensor")
    return lax.ppermute(block, "tensor", [(i, (i + shift) % count) for i in range(count)])


def per_device(
    hidden_in,
    norm_attn,
    q_weight,
    kv_down,
    kv_norm,
    kv_up,
    out_weight,
    norm_ffn,
    router,
    expert_gate,
    expert_up,
    expert_down,
    shared_gate,
    shared_up,
    shared_down,
    routes,
    cotangent,
):
    tok_rows, width = hidden_in.shape
    dp_count = lax.axis_size("dp")
    tensor_count = lax.axis_size("tensor")
    local_experts = expert_gate.shape[0]
    part_rows = tok_rows // tensor_count
    hidden_part = expert_gate.shape[2]
    heads_local = q_weight.shape[1] // (NOPE + ROPE)
    heads_width = heads_local * (NOPE + VDIM)
    scaling = (NOPE + ROPE) ** (-0.5)
    group_devs = GROUP // tok_rows
    prompt_devs = PROMPT // tok_rows
    dp_place = lax.axis_index("dp")
    tensor_place = lax.axis_index("tensor")
    place = dp_place % group_devs
    quarter = place % prompt_devs
    z_place = tensor_place // 2
    group_base = (dp_place - place) * tok_rows

    def own_part(values):
        return lax.dynamic_slice_in_dim(values, tensor_place * part_rows, part_rows, 0)

    def meta(*entries):
        return jnp.stack([jnp.asarray(entry, jnp.int32) for entry in entries])

    ramp = jnp.arange(tok_rows, dtype=jnp.int32)
    position, unused_seg, unused_group = token_layout(dp_place * tok_rows + ramp)
    cos_table, sin_table = angle_tables(position)
    gain_first, gain_second, gain_kv = norm_attn[None], norm_ffn[None], kv_norm[None]
    down_rows_kv = kv_down.T
    router_rows = router.T
    kv_width = RANK + 2 * ROPE
    stacks = [expert_gate.transpose(0, 2, 1), expert_up.transpose(0, 2, 1), expert_down]
    near_rows = 3 * hidden_part
    slot_count = dp_count * CAP
    attn_in, packed_own, kv_raw, pack_ahead, pack_behind = run_kernel(
        latent_kernel,
        (hidden_in, gain_first, down_rows_kv, gain_kv, cos_table, sin_table, *stacks),
        [VMEM] * 6 + [HBM] * 3,
        [
            ((tok_rows, width), LOW),
            ((tok_rows, kv_width), LOW),
            ((tok_rows, RANK + ROPE), FULL),
            ((near_rows, width), LOW),
            ((near_rows, width), LOW),
        ],
        [pltpu.VMEM((2 * near_rows, width), LOW), pltpu.SemaphoreType.DMA((8,))],
        [VMEM] * 3 + [HBM] * 2,
    )
    ahead, behind = shift_z(pack_ahead, 1), shift_z(pack_behind, 3)
    copied = lax.ppermute(
        packed_own,
        "dp",
        [
            (base + i, base + prompt_devs + i)
            for base in range(0, dp_count, group_devs)
            for i in range(prompt_devs)
        ],
    )
    query, dispatch, taken_grads = run_kernel(
        early_kernel,
        (after(attn_in, copied), q_weight, cos_table, sin_table, routes.T, cotangent),
        [VMEM] * 6,
        [
            ((tok_rows, heads_local * 2 * LANES), LOW),
            ((slot_count, tok_rows), LOW),
            ((slot_count, 2 * width), LOW),
        ],
        [pltpu.VMEM((slot_count, width), LOW), pltpu.SemaphoreType.DMA],
        [VMEM] * 2 + [HBM],
    )
    combine = dispatch.T
    (pack_far,) = run_kernel(
        far_pack_kernel,
        (*stacks[:2], after(stacks[2], query)),
        [HBM] * 3,
        [((near_rows, width), LOW)],
        [pltpu.VMEM((near_rows, width), LOW), pltpu.SemaphoreType.DMA((4,))],
        [HBM],
    )
    first_block = jnp.where(place < prompt_devs, packed_own, copied)
    blocks = [first_block]
    for shift in range(1, prompt_devs):
        blocks.append(
            lax.ppermute(
                first_block,
                "dp",
                [
                    (base + i, base + (i + shift) % prompt_devs)
                    for base in range(0, dp_count, prompt_devs)
                    for i in range(prompt_devs)
                ],
            )
        )
    blocks.append(packed_own)
    attend_meta = meta(
        place, *[(quarter - shift) % prompt_devs for shift in range(prompt_devs)]
    )
    key_rows = len(blocks) * tok_rows
    attn_part, attn_low, kv_heads, log_sum = run_kernel(
        attend_kernel,
        (attend_meta, *blocks, query, kv_up, out_weight),
        [SMEM] + [VMEM] * 8,
        [
            ((tok_rows, width), LOW),
            ((tok_rows, heads_local * VDIM), LOW),
            ((key_rows, heads_width), LOW),
            ((tok_rows, heads_local * LANES), FULL),
        ],
    )
    part_meta = meta(tensor_place)

    def by_part(values):
        return values.reshape(tensor_count, part_rows, values.shape[-1])

    middle, copies = run_kernel(
        middle_kernel,
        (part_meta, swap_blocks(by_part(attn_part), "tensor"), hidden_in, gain_second),
        [SMEM] + [VMEM] * 3,
        [((part_rows, width), FULL), ((tensor_count, part_rows, width), LOW)],
    )
    ffn_in = swap_blocks(after(copies, ahead, behind, pack_far), "tensor").reshape(tok_rows, width)

    (taken_rows,) = run_kernel(
        take_kernel,
        (dispatch, ffn_in, taken_grads),
        [VMEM] * 2 + [HBM],
        [((slot_count, 2 * width), LOW)],
        [pltpu.VMEM((slot_count, width), LOW), pltpu.SemaphoreType.DMA],
        [HBM],
        aliases={2: 0},
    )
    expert_rows = swap_blocks(taken_rows.reshape(dp_count, CAP, 2 * width), "dp").reshape(
        slot_count, 2 * width
    )
    far = shift_z(after(pack_far, taken_rows), 2)

    shared_width = shared_gate.shape[1]
    shared_back, shared_part, shared_keep, shared_send = run_kernel(
        shared_kernel,
        (after(ffn_in, taken_rows), cotangent, shared_gate.T, shared_up.T, shared_down),
        [VMEM] * 5,
        [
            ((tok_rows, width), LOW),
            ((tok_rows, width), LOW),
            ((3 * shared_width, width // 2), LOW),
            ((3 * shared_width, width // 2), LOW),
        ],
        [pltpu.VMEM((3 * shared_width, width), FULL)],
        mib=32,
    )

    def exchange_dp(block, flip):
        return lax.ppermute(block, "dp", [(i, i ^ flip) for i in range(dp_count)])

    def join_cores(keep, arrived):
        shape = (keep.shape[0], keep.shape[1] // 2)
        return run_kernel(
            join_cores_kernel, (keep, arrived), [VMEM] * 2, [(shape, FULL), (shape, LOW)],
        mib=16,
    )

    def join_sides(keep, arrived):
        shape = (keep.shape[0], LANES)
        return run_kernel(
            join_sides_kernel, (keep, arrived), [VMEM] * 2, [(shape, FULL)] + [(shape, LOW)] * 3
        )

    def along_x(blocks):
        return [
            lax.ppermute(block, "dp", [(i, (i + 4 * shift) % dp_count) for i in range(dp_count)])
            for shift, block in enumerate(blocks, 1)
        ]

    shared_keep, shared_send = join_cores(shared_keep, after(exchange_dp(shared_send, 1), far))
    shared_arrived = exchange_dp(shared_send, 2)

    own_hidden = local_experts * hidden_part
    wide = 2 * width + LANES
    back_rows, hidden_low, gate_low, up_low, slot_gate = run_kernel(
        expert_kernel,
        (
            meta(dp_place * local_experts + z_place),
            expert_rows,
            *stacks,
            ahead,
            far,
            behind,
            after(router_rows, shared_keep),
        ),
        [SMEM] + [HBM] * 7 + [VMEM],
        [
            ((slot_count, wide), LOW),
            ((slot_count, own_hidden), LOW),
            ((slot_count, own_hidden), LOW),
            ((slot_count, own_hidden), LOW),
            ((slot_count, LANES), FULL),
        ],
        [
            pltpu.VMEM((slot_count, width), LOW),
            pltpu.VMEM((slot_count, width), LOW),
            pltpu.VMEM((3, own_hidden, width), LOW),
            pltpu.VMEM((slot_count, wide), LOW),
            pltpu.SemaphoreType.DMA((2,)),
            pltpu.SemaphoreType.DMA((3, 4)),
            pltpu.SemaphoreType.DMA((2,)),
        ],
        [HBM] + [VMEM] * 4,
        mib=44,
    )

    back_rows = swap_blocks(
        after(back_rows, shared_arrived).reshape(dp_count, CAP, wide), "dp"
    ).reshape(slot_count, wide)
    shared_own, *shared_blocks = join_sides(shared_keep, shared_arrived)
    turns = 2
    step = width // turns

    def weight_grad(kernel, operands, first):
        whole = [pl.BlockSpec(v.shape, lambda turn: (0, 0)) for v in operands]
        return run_kernel(
            kernel,
            (expert_rows, *operands),
            [pl.BlockSpec((slot_count, step), lambda turn: (0, first * turns + turn))] + whole,
            [((hidden_part, width), LOW)] * local_experts,
            out_specs=[pl.BlockSpec((hidden_part, step), lambda turn: (0, turn))] * local_experts,
            grid=(turns,),
            mib=20,
        )

    in_grads = [weight_grad(expert_in_grad_kernel, (low,), 0) for low in (gate_low, up_low)]
    down_grads = weight_grad(expert_out_grad_kernel, (hidden_low, slot_gate), 1)
    back_rows = after(
        back_rows, in_grads[0][0], in_grads[1][0], down_grads[0], shared_own
    )
    early = [(0, 1), (0, 3), (1, 1), (1, 3), (0, 2)]
    early_homes = {
        (kind, shift): shift_z(in_grads[kind][shift], local_experts - shift)
        for kind, shift in early
    }

    (payload,) = run_kernel(
        combine_kernel,
        (
            meta(z_place, local_experts),
            combine,
            after(back_rows, down_grads[0], *early_homes.values()),
            shared_back,
            shared_part,
        ),
        [SMEM] + [VMEM] * 4,
        [((tok_rows, wide), LOW)],
        mib=24,
    )
    middle_grad, copies, norm_ffn_grad, middle_sums = run_kernel(
        ffn_back_kernel,
        (
            part_meta,
            middle,
            ffn_in,
            router_rows,
            gain_second,
            cotangent,
            swap_blocks(by_part(payload), "tensor"),
        ),
        [SMEM] + [VMEM] * 6,
        [
            ((part_rows, width), FULL),
            ((tensor_count, part_rows, wide), LOW),
            ((1, width), FULL),
            ((1, LANES), FULL),
        ],
        mib=20,
    )
    shared_blocks = along_x(lax.optimization_barrier((*shared_blocks, payload))[:-1])
    shared_blocks = [shared_own, *shared_blocks]
    spread = after(swap_blocks(copies, "tensor"), *shared_blocks).reshape(tok_rows, wide)
    late_homes = {(1, 2): shift_z(after(in_grads[1][2], spread), local_experts - 2)}

    kv_part, query_part, heads_low, query_low = run_kernel(
        attend_back_kernel,
        (
            attend_meta,
            out_weight,
            *blocks,
            query,
            kv_heads,
            log_sum,
            kv_up,
            cos_table,
            sin_table,
            spread,
            q_weight,
        ),
        [SMEM] + [VMEM] * 14,
        [
            ((tensor_count, part_rows, len(blocks) * kv_width), LOW),
            ((tok_rows, width), LOW),
            ((key_rows, heads_width), LOW),
            ((tok_rows, heads_local * (NOPE + ROPE)), LOW),
        ],
    )
    got_parts = swap_blocks(after(kv_part, late_homes[1, 2]), "tensor")
    *prompt_parts, kv_own = run_kernel(
        kv_sum_kernel,
        (got_parts,),
        [VMEM],
        [((part_rows, kv_width), LOW)] * prompt_devs + [((part_rows, kv_width), FULL)],
    )
    (joined,) = run_kernel(
        kv_join_kernel,
        [prompt_parts[0]]
        + [
            lax.ppermute(
                prompt_parts[shift],
                "dp",
                [
                    (base + i, base + (i - shift) % prompt_devs)
                    for base in range(0, dp_count, prompt_devs)
                    for i in range(prompt_devs)
                ],
            )
            for shift in range(1, prompt_devs)
        ],
        [VMEM] * prompt_devs,
        [((part_rows, kv_width), LOW)],
    )
    other = lax.ppermute(
        joined,
        "dp",
        [
            (base + prompt_devs + i, base + i)
            for base in range(0, dp_count, group_devs)
            for i in range(prompt_devs)
        ],
    )
    got_query = swap_blocks(after(by_part(query_part), kv_own), "tensor")
    for shift in (1, 3, 2):
        late_homes[2, shift] = shift_z(after(down_grads[shift], kv_own), local_experts - shift)

    def place_grads(kind):
        grads = (*in_grads, down_grads)[kind]
        arrived = early_homes | late_homes
        return run_kernel(
            place_kernel,
            (
                meta(z_place),
                grads[0],
                *[arrived[kind, shift] for shift in range(1, local_experts)],
            ),
            [SMEM] + [VMEM] * 4,
            [((local_experts, hidden_part, width), FULL)],
        )[0]

    gate_wgrad = place_grads(0)
    copies, grad_low, norm_attn_grad, kv_norm_grad, square_sums = run_kernel(
        last_kernel,
        (
            meta(tensor_place, place),
            joined,
            other,
            kv_own,
            kv_raw,
            gain_kv,
            cos_table,
            sin_table,
            down_rows_kv,
            hidden_in,
            gain_first,
            after(middle_grad, gate_wgrad),
            middle_sums,
            got_query,
        ),
        [SMEM] + [VMEM] * 13,
        [
            ((tensor_count, part_rows, kv_width), LOW),
            ((part_rows, width), LOW),
            ((1, width), FULL),
            ((1, RANK), FULL),
            ((1, LANES), FULL),
        ],
    )
    up_wgrad = place_grads(1)
    kv_low_all = swap_blocks(copies, "tensor").reshape(tok_rows, kv_width)
    down_wgrad = place_grads(2)

    query_width = q_weight.shape[1]
    own_width, own_rank = width // dp_count, RANK // dp_count
    up_lines = own_rank * heads_width // LANES
    attn_width = heads_local * VDIM
    token_rows = query_width + attn_width + EXPERTS + up_lines
    token_grads, output = run_kernel(
        token_grad_kernel,
        (attn_in, query_low, attn_low, spread, ffn_in, heads_low, *blocks),
        [VMEM] * (6 + len(blocks)),
        [
            ((token_rows, width), FULL),
            ((tok_rows, width), LOW),
        ],
        mib=28,
    )
    token_grads = lax.psum_scatter(
        after(token_grads, got_parts), "dp", scatter_dimension=1, tiled=True
    )
    share = kv_width // tensor_count
    grad_low = after(grad_low, kv_low_all)
    grad_parts = [shift_tensor(grad_low, shift) for shift in range(tensor_count)]
    (mixed,) = run_kernel(
        mix_kernel,
        (
            part_meta,
            after(kv_low_all, up_wgrad, late_homes[2, 1], late_homes[2, 3]),
            attn_in,
            norm_attn_grad,
            norm_ffn_grad,
            kv_norm_grad,
            square_sums,
        ),
        [SMEM] + [VMEM] * 6,
        [((dp_count, share + 16, LANES), LOW)],
        mib=16,
    )
    (copies,) = run_kernel(
        mix_sum_kernel,
        (after(swap_blocks(mixed, "dp"), late_homes[2, 2], *grad_parts[1:5]),),
        [VMEM],
        [((tensor_count, share + 16, LANES), LOW)],
        mib=16,
    )
    shared_width = shared_gate.shape[1]
    (
        input_grad,
        down_grad,
        attn_gain,
        ffn_gain,
        kv_gain,
        rms,
        query_grad,
        up_grad,
        out_grad,
        router_grad,
        *shared_out,
    ) = run_kernel(
        final_kernel,
        (swap_blocks(copies, "tensor"), token_grads, *grad_parts, *shared_blocks),
        [VMEM] * (2 + tensor_count + len(shared_blocks)),
        [
            ((tok_rows, width), LOW),
            ((RANK + ROPE, own_width), FULL),
            ((1, LANES), FULL),
            ((1, LANES), FULL),
            ((1, own_rank), FULL),
            ((1, 5), FULL),
            ((own_width, query_width), FULL),
            ((own_rank, heads_width), FULL),
            ((attn_width, own_width), FULL),
            ((EXPERTS, own_width), FULL),
        ]
        + [((shared_width, own_width), FULL)] * 3,
        [pltpu.VMEM((kv_width, LANES), FULL)],
        mib=16,
    )
    return (
        output,
        input_grad,
        attn_gain.reshape(own_width),
        query_grad,
        down_grad.T,
        kv_gain.reshape(own_rank),
        up_grad,
        out_grad,
        ffn_gain.reshape(own_width),
        router_grad.T,
        gate_wgrad.transpose(0, 2, 1),
        up_wgrad.transpose(0, 2, 1),
        down_wgrad,
        shared_out[0].T,
        shared_out[1].T,
        shared_out[2],
        rms.reshape(5),
    )


def solution(mesh):
    return jax.shard_map(
        per_device,
        mesh=mesh,
        in_specs=(
            P("dp", None),
            P(),
            P(None, "tensor"),
            P(),
            P(),
            P(None, "tensor"),
            P("tensor", None),
            P(),
            P(),
            P("dp", None, "tensor"),
            P("dp", None, "tensor"),
            P("dp", "tensor", None),
            P(None, "tensor"),
            P(None, "tensor"),
            P("tensor", None),
            P("dp", None),
            P("dp", None),
        ),
        out_specs=(
            P("dp", None),
            P("dp", None),
            P("dp"),
            P("dp", "tensor"),
            P("dp", None),
            P("dp"),
            P("dp", "tensor"),
            P("tensor", "dp"),
            P("dp"),
            P("dp", None),
            P("dp", None, "tensor"),
            P("dp", None, "tensor"),
            P("dp", "tensor", None),
            P("dp", "tensor"),
            P("dp", "tensor"),
            P("tensor", "dp"),
            P(),
        ),
        check_vma=False,
    )
```

```python
import functools

import jax
import jax.numpy as jnp
from jax import lax
from jax.experimental import pallas as pl
from jax.experimental.pallas import tpu as pltpu
from jax.sharding import PartitionSpec as P

NOPE = 128
ROPE = 64
RANK = 512
VDIM = 128
TOP = 6
CAP = 32
PROMPT = 1024
CONT = 128
GROUP = 2048
EXPERTS = 64
LANES = 128
EPSILON = 1e-06
THETA = 10000.0
LOW = jnp.bfloat16
FULL = jnp.float32


def contract(first_arr, second_arr, first_axis, second_axis):
    return lax.dot_general(
        first_arr,
        second_arr,
        (((first_axis,), (second_axis,)), ((), ())),
        preferred_element_type=FULL,
    )


def rotate(values, cos_table, sin_table):
    half_width = values.shape[-1] // 2
    front = values[..., :half_width]
    behind = values[..., half_width:]
    return jnp.concatenate(
        [front * cos_table - behind * sin_table, behind * cos_table + front * sin_table], -1
    )


def token_layout(row_index):
    offset = row_index % GROUP
    in_prompt = offset < PROMPT
    position = jnp.where(in_prompt, offset, PROMPT + (offset - PROMPT) % CONT)
    segment = jnp.where(in_prompt, 0, 1 + (offset - PROMPT) // CONT)
    return (position, segment, row_index // GROUP)


def angle_tables(position):
    half_width = ROPE // 2
    frequency = THETA ** (-2.0 * jnp.arange(half_width, dtype=FULL) / ROPE)
    angles = position.astype(FULL)[:, None] * frequency[None]
    return (jnp.cos(angles), jnp.sin(angles))


def inverse_rms(values):
    return lax.rsqrt(jnp.mean(values * values, -1, keepdims=True) + EPSILON)


def norm_backward(grad_normed, normed, inverse, gain):
    scaled = grad_normed * gain
    return (
        inverse * (scaled - normed * jnp.mean(scaled * normed, -1, keepdims=True)),
        jnp.sum(grad_normed * normed, 0, keepdims=True),
    )


VMEM = pl.BlockSpec(memory_space=pltpu.VMEM)
SMEM = pl.BlockSpec(memory_space=pltpu.SMEM)
HBM = pl.BlockSpec(memory_space=pl.ANY)


def run_kernel(
    kernel, operands, specs, outs, scratch=(), out_specs=None, grid=(), aliases=None, mib=56
):
    shapes = [jax.ShapeDtypeStruct(shape, dtype) for shape, dtype in outs]
    return pl.pallas_call(
        kernel,
        out_shape=shapes,
        grid=grid,
        input_output_aliases=aliases or {},
        in_specs=list(specs),
        out_specs=list(out_specs or [VMEM] * len(shapes)),
        scratch_shapes=list(scratch),
        compiler_params=pltpu.CompilerParams(vmem_limit_bytes=mib * 1024 * 1024),
        cost_estimate=pl.CostEstimate(flops=1000, bytes_accessed=1000, transcendentals=0),
    )(*operands)


def latent_kernel(
    hidden,
    gain,
    down_rows,
    kv_gain,
    cos,
    sin,
    gate,
    up,
    down,
    attn_in,
    packed,
    kv_raw,
    ahead,
    behind,
    held,
    sems,
):
    parts = [[(kind, shift) for kind in range(3)] for shift in (1, 3)]
    picks = RowPicks((gate, up, down), (ahead, behind), parts, held, sems)
    picks.get()
    values = hidden[...].astype(FULL)
    normed = (values * inverse_rms(values) * gain[...]).astype(LOW)
    attn_in[...] = normed
    picks.put()
    raw = contract(normed, down_rows[...], 1, 1)
    kv_raw[...] = raw
    latent = raw[:, :RANK]
    packed[:, :RANK] = (latent * inverse_rms(latent) * kv_gain[...]).astype(LOW)
    rope = rotate(raw[:, RANK:], cos[...], sin[...]).astype(LOW)
    packed[:, RANK:] = jnp.concatenate([rope, jnp.zeros_like(rope)], -1)
    picks.wait()


def turn_queries(attn_in, q_weight, cos, sin, query):
    turned = jnp.dot(attn_in[...], q_weight[...], preferred_element_type=FULL)
    step = NOPE + ROPE
    for head in range(turned.shape[1] // step):
        place = head * 2 * LANES
        start = head * step
        query[:, place : place + NOPE] = turned[:, start : start + NOPE].astype(LOW)
        rope = rotate(turned[:, start + NOPE : start + step], cos[...], sin[...]).astype(LOW)
        query[:, place + NOPE : place + 2 * LANES] = jnp.concatenate(
            [rope, jnp.zeros_like(rope)], -1
        )


def visible_keys(meta, block, shape):
    rows = lax.broadcasted_iota(jnp.int32, shape, 0)
    cols = lax.broadcasted_iota(jnp.int32, shape, 1)
    place, prompt_devs = meta[0], PROMPT // shape[1]
    if block < prompt_devs:
        return cols - rows <= (place - meta[1 + block]) * shape[1]
    own = (cols <= rows) & (rows // CONT == cols // CONT)
    return own & (place >= prompt_devs)


def head_key(heads, rope, head):
    start = head * (NOPE + VDIM)
    return jnp.concatenate([heads[:, start : start + NOPE], rope], -1)


def attend_kernel(
    meta, first, second, third, fourth, own, query, kv_up, out_weight, part, attn, heads, log_sum
):
    blocks = (first, second, third, fourth, own)
    rows = own.shape[0]
    scaling = (NOPE + ROPE) ** (-0.5)
    for block, ref in enumerate(blocks):
        heads[block * rows : (block + 1) * rows] = jnp.dot(
            ref[:, :RANK], kv_up[...], preferred_element_type=FULL
        ).astype(LOW)
    masks = [visible_keys(meta, block, (rows, rows)) for block in range(len(blocks))]
    for head in range(query.shape[1] // (2 * LANES)):
        asked = query[:, head * 2 * LANES : (head + 1) * 2 * LANES]
        scores = []
        for block, ref in enumerate(blocks):
            key = head_key(heads[block * rows : (block + 1) * rows], ref[:, RANK:], head)
            raw = contract(asked, key, 1, 1) * scaling
            scores.append(jnp.where(masks[block], raw, -1e30))
        peak = scores[0]
        for score in scores[1:]:
            peak = jnp.maximum(peak, score)
        peak = jnp.max(peak, -1, keepdims=True)
        weights = [jnp.exp(score - peak) for score in scores]
        total = jnp.sum(functools.reduce(jnp.add, weights), -1, keepdims=True)
        scale = 1.0 / total
        summed = 0.0
        start = head * (NOPE + VDIM) + NOPE
        for block, weight in enumerate(weights):
            value = heads[block * rows : (block + 1) * rows, start : start + VDIM]
            summed = summed + jnp.dot(
                (weight * scale).astype(LOW), value, preferred_element_type=FULL
            )
        attn[:, head * VDIM : (head + 1) * VDIM] = summed.astype(LOW)
        log_sum[:, head * LANES : (head + 1) * LANES] = jnp.broadcast_to(
            peak + jnp.log(total), (rows, LANES)
        )
    part[...] = jnp.dot(attn[...], out_weight[...], preferred_element_type=FULL).astype(LOW)


def middle_kernel(meta, got, hidden, gain, middle, copies):
    part_rows = middle.shape[0]
    start = pl.multiple_of(meta[0] * part_rows, part_rows)
    values = hidden[pl.ds(start, part_rows), :].astype(FULL)
    for index in range(got.shape[0]):
        values = values + got[index].astype(FULL)
    middle[...] = values
    normed = (values * inverse_rms(values) * gain[...]).astype(LOW)
    for index in range(copies.shape[0]):
        copies[index] = normed


def split_cores(grads, keep, send):
    core = lax.axis_index("dp") % 2
    for chip in range(keep.shape[1] // LANES):
        here = slice(chip * LANES, (chip + 1) * LANES)
        first = pl.multiple_of((2 * chip + core) * LANES, LANES)
        other = pl.multiple_of((2 * chip + 1 - core) * LANES, LANES)
        keep[:, here] = grads[:, pl.ds(first, LANES)].astype(LOW)
        send[:, here] = grads[:, pl.ds(other, LANES)].astype(LOW)


def join_cores_kernel(kept, arrived, keep, send):
    side = lax.axis_index("dp") // 2 % 2
    for row in range(keep.shape[1] // LANES):
        here = slice(row * LANES, (row + 1) * LANES)
        for out, which in ((keep, 2 * row + side), (send, 2 * row + 1 - side)):
            there = pl.ds(pl.multiple_of(which * LANES, LANES), LANES)
            total = kept[:, there].astype(FULL) + arrived[:, there].astype(FULL)
            out[:, here] = total.astype(out.dtype)


def join_sides_kernel(kept, arrived, own, *outs):
    place, count = lax.axis_index("dp") // 4, len(outs) + 1
    for shift, out in enumerate((own, *outs)):
        owner = lax.rem(place + shift, count)
        there = pl.ds(pl.multiple_of(owner * LANES, LANES), LANES)
        total = kept[:, there] + arrived[:, there].astype(FULL)
        out[...] = total.astype(out.dtype)


def shared_kernel(ffn, cot, gate, up, down, back, out, keep, send, grads):
    rows = gate.shape[0]
    gate_pre = contract(ffn[...], gate[...], 1, 1)
    up_pre = contract(ffn[...], up[...], 1, 1)
    hidden_back = contract(cot[...], down[...], 1, 1)
    sig = jax.nn.sigmoid(gate_pre)
    low = (gate_pre * sig * up_pre).astype(LOW)
    gate_low = (hidden_back * up_pre * sig * (1.0 + gate_pre * (1.0 - sig))).astype(LOW)
    up_low = (hidden_back * gate_pre * sig).astype(LOW)
    out[...] = jnp.dot(low, down[...], preferred_element_type=FULL).astype(LOW)
    back[...] = (
        jnp.dot(gate_low, gate[...], preferred_element_type=FULL)
        + jnp.dot(up_low, up[...], preferred_element_type=FULL)
    ).astype(LOW)
    grads[:rows] = contract(gate_low, ffn[...], 0, 0)
    grads[rows : 2 * rows] = contract(up_low, ffn[...], 0, 0)
    grads[2 * rows :] = contract(low, cot[...], 0, 0)
    split_cores(grads, keep, send)


class RowPicks:
    def __init__(self, stacks, outs, parts, held, sems):
        count, rows = stacks[0].shape[:2]
        z_place = lax.axis_index("tensor") // 2
        self.gets, self.puts, start = [], [], 0
        for out, wanted in zip(outs, parts):
            first = start
            for kind, shift in wanted:
                source = stacks[kind].at[lax.rem(z_place + shift, count)]
                target = held.at[pl.ds(start, rows)]
                self.gets.append(pltpu.make_async_copy(source, target, sems.at[len(self.gets)]))
                start += rows
            self.puts.append((first, start, out, len(self.gets)))
        self.puts = [
            (
                needed,
                pltpu.make_async_copy(
                    held.at[pl.ds(first, end - first)], out, sems.at[len(self.gets) + index]
                ),
            )
            for index, (first, end, out, needed) in enumerate(self.puts)
        ]

    def get(self):
        for copy in self.gets:
            copy.start()

    def put(self):
        done = 0
        for needed, copy in self.puts:
            for earlier in self.gets[done:needed]:
                earlier.wait()
            done = needed
            copy.start()

    def wait(self):
        for needed, copy in self.puts:
            copy.wait()


def far_pack_kernel(gate, up, down, far, held, sems):
    picks = RowPicks((gate, up, down), (far,), [[(kind, 2) for kind in range(3)]], held, sems)
    picks.get()
    picks.put()
    picks.wait()


def early_kernel(
    attn_in, q_weight, cos, sin, routes, cot, query, dispatch, taken, held, sem
):
    copy = dispatch_rows(routes, cot, dispatch, held, taken, sem)
    turn_queries(attn_in, q_weight, cos, sin, query)
    copy.wait()


def dispatch_rows(routes, cot, dispatch, held, taken, sem):
    owners, tokens = dispatch.shape[0] // CAP, routes.shape[1]
    local_experts = EXPERTS // owners
    owner = lax.broadcasted_iota(jnp.int32, (owners, tokens), 0)
    expert = owner * local_experts + lax.axis_index("tensor") // 2
    chosen = jnp.zeros((owners, tokens), FULL)
    for turn in range(routes.shape[0]):
        chosen = jnp.where(routes[turn : turn + 1, :] == expert, 1.0, chosen)
    square = (tokens, tokens)
    earlier = lax.broadcasted_iota(jnp.int32, square, 0) < lax.broadcasted_iota(
        jnp.int32, square, 1
    )
    ranking = jnp.dot(
        chosen.astype(LOW), earlier.astype(FULL).astype(LOW), preferred_element_type=FULL
    )
    ranking = jnp.where(chosen > 0.0, ranking, -1.0)
    slot = lax.broadcasted_iota(jnp.int32, (CAP, tokens), 0).astype(FULL)
    for index in range(owners):
        dispatch[index * CAP : (index + 1) * CAP] = jnp.where(
            ranking[index : index + 1, :] == slot, 1.0, 0.0
        ).astype(LOW)
    held[...] = jnp.dot(dispatch[...], cot[...], preferred_element_type=FULL).astype(LOW)
    width = cot.shape[1]
    copy = pltpu.make_async_copy(held, taken.at[:, pl.ds(width, width)], sem)
    copy.start()
    return copy


def take_kernel(dispatch, rows, grads, taken, held, sem):
    held[...] = jnp.dot(dispatch[...], rows[...], preferred_element_type=FULL).astype(LOW)
    copy = pltpu.make_async_copy(held, taken.at[:, pl.ds(0, rows.shape[1])], sem)
    copy.start()
    copy.wait()


def chunk_copies(own, pieces, held, sems):
    part = own.shape[1]
    sources = [own.at[lax.axis_index("tensor") // 2]]
    sources += [ref.at[pl.ds(first, part)] for ref, first in pieces]
    return [
        pltpu.make_async_copy(source, held.at[pl.ds(index * part, part)], sems.at[index])
        for index, source in enumerate(sources)
    ]


def expert_kernel(
    meta,
    rows_in,
    gate_in,
    up_in,
    down_in,
    ahead,
    far,
    behind,
    router,
    back,
    hidden_out,
    gate_out,
    up_out,
    slot_gate,
    rows_held,
    grad_held,
    weights,
    out_held,
    row_sems,
    weight_sems,
    out_sems,
):
    count, width = rows_held.shape
    part = gate_in.shape[1]
    get_rows, get_grads = [
        pltpu.make_async_copy(rows_in.at[:, pl.ds(first, width)], held, row_sems.at[index])
        for index, (first, held) in enumerate(((0, rows_held), (width, grad_held)))
    ]
    get_gate, get_up, get_down = [
        chunk_copies(
            own,
            [(ref, kind * part) for ref in (ahead, far, behind)],
            weights.at[kind],
            weight_sems.at[kind],
        )
        for kind, own in enumerate((gate_in, up_in, down_in))
    ]
    gate_w, up_w, down_w = [weights.at[kind] for kind in range(3)]
    split = width + LANES
    puts = [
        pltpu.make_async_copy(
            out_held.at[:, pl.ds(first, size)],
            back.at[:, pl.ds(first, size)],
            out_sems.at[index],
        )
        for index, (first, size) in enumerate(((0, split), (split, width)))
    ]
    for copy in (get_rows, *get_gate, *get_up, get_grads, *get_down):
        copy.start()

    def wait_all(copies):
        for copy in copies:
            copy.wait()

    get_rows.wait()
    rows = rows_held[...]
    logits = contract(rows, router[...], 1, 1)
    logits = jnp.exp(logits - jnp.max(logits, -1, keepdims=True))
    mine = lax.broadcasted_iota(jnp.int32, logits.shape, 1) == meta[0]
    gate = jnp.sum(jnp.where(mine, logits, 0.0), -1, keepdims=True) / jnp.sum(
        logits, -1, keepdims=True
    )
    slot_gate[...] = jnp.broadcast_to(gate, (count, LANES))
    wait_all(get_gate)
    gate_pre = contract(rows, gate_w[...], 1, 1)
    sig = jax.nn.sigmoid(gate_pre)
    wait_all(get_up)
    up_pre = contract(rows, up_w[...], 1, 1)
    low = (gate_pre * sig * up_pre).astype(LOW)
    hidden_out[...] = low
    get_grads.wait()
    wait_all(get_down)
    hidden_back = contract(grad_held[...], down_w[...], 1, 1)
    dots = jnp.sum(low.astype(FULL) * hidden_back, -1, keepdims=True)
    hidden_back = hidden_back * gate
    gate_low = (hidden_back * up_pre * sig * (1.0 + gate_pre * (1.0 - sig))).astype(LOW)
    up_low = (hidden_back * gate_pre * sig).astype(LOW)
    gate_out[...] = gate_low
    up_out[...] = up_low
    out_held[:, :width] = (
        jnp.dot(gate_low, gate_w[...], preferred_element_type=FULL)
        + jnp.dot(up_low, up_w[...], preferred_element_type=FULL)
    ).astype(LOW)
    high = dots.astype(LOW).astype(FULL)
    lane = lax.broadcasted_iota(jnp.int32, (count, LANES), 1)
    out_held[:, width:split] = jnp.where(
        lane == 0, high, jnp.where(lane == 1, dots - high, 0.0)
    ).astype(LOW)
    puts[0].start()
    out_held[:, split:] = (jnp.dot(low, down_w[...], preferred_element_type=FULL) * gate).astype(
        LOW
    )
    puts[1].start()
    wait_all(puts)


def expert_in_grad_kernel(rows, low, *grads):
    part = grads[0].shape[0]
    grad = contract(low[...], rows[...], 0, 0).astype(LOW)
    for index, ref in enumerate(grads):
        ref[...] = grad[index * part : (index + 1) * part]


def expert_out_grad_kernel(grad_in, hidden, slot_gate, *grads):
    part = grads[0].shape[0]
    scaled = (grad_in[...].astype(FULL) * slot_gate[:, :1]).astype(LOW)
    grad = contract(hidden[...], scaled, 0, 0).astype(LOW)
    for index, ref in enumerate(grads):
        ref[...] = grad[index * part : (index + 1) * part]


def combine_kernel(meta, combine, returned, shared_back, shared_part, payload):
    width = shared_back.shape[1]
    payload[:, :width] = (
        jnp.dot(combine[...], returned[:, :width], preferred_element_type=FULL)
        + shared_back[...].astype(FULL)
    ).astype(LOW)
    slot_rows = returned.shape[0]
    slot = lax.broadcasted_iota(jnp.int32, (slot_rows, EXPERTS), 0) // CAP
    at_expert = slot * meta[1] + meta[0] == lax.broadcasted_iota(
        jnp.int32, (slot_rows, EXPERTS), 1
    )
    dots = returned[:, width : width + LANES].astype(FULL)
    summed = 0.0
    for index in range(2):
        columns = jnp.where(at_expert, dots[:, index : index + 1], 0.0).astype(LOW)
        summed = summed + jnp.dot(combine[...], columns, preferred_element_type=FULL)
    high = summed.astype(LOW)
    rest = (summed - high.astype(FULL)).astype(LOW)
    payload[:, width : width + LANES] = jnp.concatenate([high, rest], -1)
    payload[:, width + LANES :] = (
        jnp.dot(combine[...], returned[:, width + LANES :], preferred_element_type=FULL)
        + shared_part[...].astype(FULL)
    ).astype(LOW)


def token_grad_kernel(attn_in, query_low, attn_low, spread, ffn, heads_low, *refs):
    blocks, (grads, output) = refs[:-2], refs[-2:]
    width = attn_in.shape[1]
    output[...] = spread[:, width + LANES :]
    rows = attn_in.shape[0]
    start = query_low.shape[1]
    grads[:start] = contract(query_low[...], attn_in[...], 0, 0)
    end = start + attn_low.shape[1]
    grads[start:end] = contract(attn_low[...], spread[:, :width], 0, 0)
    start, end = end, end + EXPERTS
    grads[start:end] = contract(spread[:, width : width + LANES], ffn[...], 0, 0)[:EXPERTS]
    total = 0.0
    for index, ref in enumerate(blocks):
        total = total + contract(ref[:, :RANK], heads_low[index * rows : (index + 1) * rows], 0, 0)
    owners = width // LANES
    lines = total.shape[0] // owners
    for column in range(total.shape[1] // LANES):
        for owner in range(owners):
            grads[
                end + column * lines : end + (column + 1) * lines,
                owner * LANES : (owner + 1) * LANES,
            ] = total[owner * lines : (owner + 1) * lines, column * LANES : (column + 1) * LANES]


def place_kernel(meta, first, second, third, fourth, out):
    for shift, chunk in enumerate((first, second, third, fourth)):
        out[lax.rem(meta[0] + shift, out.shape[0])] = chunk[...].astype(FULL)


def ffn_back_kernel(
    meta, middle, ffn, router, gain, cot, got, middle_grad, copies, gain_grad, sums
):
    part_rows, width = middle.shape
    start = pl.multiple_of(meta[0] * part_rows, part_rows)
    here = pl.ds(start, part_rows)
    total = got[0].astype(FULL)
    for index in range(1, got.shape[0]):
        total = total + got[index].astype(FULL)
    extra = total[:, width : width + LANES]
    prob_grad = extra[:, :EXPERTS] + extra[:, EXPERTS:]
    logits = contract(ffn[here, :], router[...], 1, 1)
    logits = jnp.exp(logits - jnp.max(logits, -1, keepdims=True))
    prob = logits / jnp.sum(logits, -1, keepdims=True)
    logit_low = (
        prob * (prob_grad - jnp.sum(prob * prob_grad, -1, keepdims=True))
    ).astype(LOW)
    ffn_grad = total[:, :width] + jnp.dot(logit_low, router[...], preferred_element_type=FULL)
    values = middle[...]
    inverse = inverse_rms(values)
    back, gains = norm_backward(ffn_grad, values * inverse, inverse, gain[...])
    gain_grad[...] = gains
    grad = cot[here, :].astype(FULL) + back
    middle_grad[...] = grad
    low = grad.astype(LOW)
    tail = jnp.concatenate([logit_low, jnp.zeros_like(logit_low)], -1)
    result = values + total[:, width + LANES :]
    result_low = result.astype(LOW)
    for index in range(copies.shape[0]):
        copies[index, :, :width] = low
        copies[index, :, width : width + LANES] = tail
        copies[index, :, width + LANES :] = result_low
    lane = lax.broadcasted_iota(jnp.int32, sums.shape, 1)
    sums[...] = jnp.where(lane == 2, jnp.sum(values * values), 0.0) + jnp.where(
        lane == 3, jnp.sum(result * result), 0.0
    )


def attend_back_kernel(
    meta,
    out_weight,
    first,
    second,
    third,
    fourth,
    own,
    query,
    heads,
    log_sum,
    kv_up,
    cos,
    sin,
    spread,
    q_weight,
    kv_part,
    query_part,
    heads_low,
    query_low,
):
    blocks = (first, second, third, fourth, own)
    rows = own.shape[0]
    parts, part_rows, _ = kv_part.shape
    kv_width = RANK + 2 * ROPE
    scaling = (NOPE + ROPE) ** (-0.5)
    attn_grad = contract(spread[:, : out_weight.shape[1]], out_weight[...], 1, 1).astype(LOW)
    masks = [visible_keys(meta, block, (rows, rows)) for block in range(len(blocks))]
    ropes = [0.0] * len(blocks)
    step = NOPE + ROPE
    for head in range(query.shape[1] // (2 * LANES)):
        asked = query[:, head * 2 * LANES : (head + 1) * 2 * LANES]
        out_grad = attn_grad[:, head * VDIM : (head + 1) * VDIM]
        logs = log_sum[:, head * LANES : head * LANES + 1]
        start = head * (NOPE + VDIM)
        probs, backs = [], []
        summed = 0.0
        for block, ref in enumerate(blocks):
            here = slice(block * rows, (block + 1) * rows)
            key = head_key(heads[here], ref[:, RANK:], head)
            raw = contract(asked, key, 1, 1) * scaling
            prob = jnp.exp(jnp.where(masks[block], raw, -1e30) - logs)
            back = contract(out_grad, heads[here, start + NOPE : start + NOPE + VDIM], 1, 1)
            summed = summed + prob * back
            probs.append(prob)
            backs.append(back)
        total = jnp.sum(summed, -1, keepdims=True)
        asked_grad = 0.0
        for block, ref in enumerate(blocks):
            here = slice(block * rows, (block + 1) * rows)
            score_low = (scaling * probs[block] * (backs[block] - total)).astype(LOW)
            key = head_key(heads[here], ref[:, RANK:], head)
            asked_grad = asked_grad + jnp.dot(score_low, key, preferred_element_type=FULL)
            key_grad = contract(score_low, asked, 0, 0)
            heads_low[here, start : start + NOPE] = key_grad[:, :NOPE].astype(LOW)
            heads_low[here, start + NOPE : start + NOPE + VDIM] = contract(
                probs[block].astype(LOW), out_grad, 0, 0
            ).astype(LOW)
            ropes[block] = ropes[block] + key_grad[:, NOPE:]
        query_low[:, head * step : head * step + NOPE] = asked_grad[:, :NOPE].astype(LOW)
        query_low[:, head * step + NOPE : (head + 1) * step] = rotate(
            asked_grad[:, NOPE:step], cos[...], -sin[...]
        ).astype(LOW)
    for block in range(len(blocks)):
        here = slice(block * rows, (block + 1) * rows)
        latent = contract(heads_low[here], kv_up[...], 1, 1).astype(LOW)
        rope = ropes[block].astype(LOW)
        start = block * kv_width
        for index in range(parts):
            mine = slice(index * part_rows, (index + 1) * part_rows)
            kv_part[index, :, start : start + RANK] = latent[mine]
            kv_part[index, :, start + RANK : start + kv_width] = rope[mine]
    query_part[...] = contract(query_low[...], q_weight[...], 1, 1).astype(LOW)


def kv_sum_kernel(got, first, second, third, fourth, own):
    kv_width = own.shape[1]
    total = got[0].astype(FULL)
    for index in range(1, got.shape[0]):
        total = total + got[index].astype(FULL)
    blocks = (first, second, third, fourth)
    for block, out in enumerate(blocks):
        out[...] = total[:, block * kv_width : (block + 1) * kv_width].astype(LOW)
    own[...] = total[:, len(blocks) * kv_width :]


def kv_join_kernel(first, second, third, fourth, out):
    total = first[...].astype(FULL) + second[...].astype(FULL)
    out[...] = (total + third[...].astype(FULL) + fourth[...].astype(FULL)).astype(LOW)


def last_kernel(
    meta,
    joined,
    other,
    own,
    kv_raw,
    kv_gain,
    cos,
    sin,
    down_rows,
    hidden,
    gain,
    middle_grad,
    sums_in,
    got_query,
    copies,
    grad_low,
    gain_grad,
    kv_gain_grad,
    sums,
):
    part_rows, width = middle_grad.shape
    here = pl.ds(pl.multiple_of(meta[0] * part_rows, part_rows), part_rows)
    in_prompt = meta[1] < PROMPT // hidden.shape[0]
    found = joined[...].astype(FULL) + other[...].astype(FULL)
    total = jnp.where(in_prompt, found, own[...])
    latent = kv_raw[here, :RANK]
    inverse = inverse_rms(latent)
    latent_grad, kv_gains = norm_backward(
        total[:, :RANK], latent * inverse, inverse, kv_gain[...]
    )
    kv_gain_grad[...] = kv_gains
    rope = rotate(total[:, RANK : RANK + ROPE], cos[here, :], -sin[here, :]).astype(LOW)
    latent_low = latent_grad.astype(LOW)
    kv_low = jnp.concatenate([latent_low, rope], -1)
    tail = jnp.concatenate([rope, jnp.zeros_like(rope)], -1)
    for index in range(copies.shape[0]):
        copies[index, :, :RANK] = latent_low
        copies[index, :, RANK:] = tail
    attn_in_grad = jnp.dot(kv_low, down_rows[...], preferred_element_type=FULL)
    for index in range(got_query.shape[0]):
        attn_in_grad = attn_in_grad + got_query[index].astype(FULL)
    values = hidden[here, :].astype(FULL)
    inverse = inverse_rms(values)
    back, gains = norm_backward(attn_in_grad, values * inverse, inverse, gain[...])
    gain_grad[...] = gains
    grad = middle_grad[...] + back
    grad_low[...] = grad.astype(LOW)
    lane = lax.broadcasted_iota(jnp.int32, sums.shape, 1)
    found = sums_in[...]
    for index, part in ((0, values), (1, latent), (4, grad)):
        found = found + jnp.where(lane == index, jnp.sum(part * part), 0.0)
    sums[...] = found


def split_rows(rows):
    high = [row.astype(LOW).astype(FULL) for row in rows]
    low = [row - part for row, part in zip(rows, high)]
    blank = jnp.zeros((16 - 2 * len(rows), LANES), FULL)
    return jnp.concatenate(high + low + [blank], 0).astype(LOW)


def mix_kernel(meta, kv_low, attn_in, attn_gain, ffn_gain, kv_gain, sums, payload):
    owners, rows, _ = payload.shape
    share = rows - 16
    shape = (kv_low.shape[1], share)
    pick = lax.broadcasted_iota(jnp.int32, shape, 0) == meta[0] * share + lax.broadcasted_iota(
        jnp.int32, shape, 1
    )
    mine = jnp.dot(
        kv_low[...], pick.astype(FULL).astype(LOW), preferred_element_type=FULL
    ).astype(LOW)
    grad = contract(mine, attn_in[...], 0, 0).astype(LOW)
    own_rank = RANK // owners
    blank = jnp.zeros((1, LANES - own_rank), FULL)
    for owner in range(owners):
        here = slice(owner * LANES, (owner + 1) * LANES)
        payload[owner, :share] = grad[:, here]
        own_kv = jnp.concatenate(
            [kv_gain[:, owner * own_rank : (owner + 1) * own_rank], blank], -1
        )
        payload[owner, share:] = split_rows(
            [attn_gain[:, here], ffn_gain[:, here], own_kv, sums[...]]
        )


def join_rows(rows, count=4):
    values = rows.astype(FULL)
    return [values[i : i + 1] + values[count + i : count + i + 1] for i in range(count)]


def mix_sum_kernel(got, copies):
    share = got.shape[1] - 16
    total = got[0].astype(FULL)
    for index in range(1, got.shape[0]):
        total = total + got[index].astype(FULL)
    mixed = jnp.concatenate(
        [total[:share].astype(LOW), split_rows(join_rows(total[share:]))], 0
    )
    for index in range(copies.shape[0]):
        copies[index] = mixed


def final_kernel(
    got,
    tokens,
    *refs,
):
    grads, refs = refs[: got.shape[0]], refs[got.shape[0] :]
    shared, refs = refs[:4], refs[4:]
    input_grad, down_grad, attn_gain, ffn_gain, kv_gain, rms = refs[:6]
    query_grad, up_grad, out_grad, router_grad = refs[6:10]
    gate_grad, shared_up_grad, shared_down_grad, held = refs[10:]
    count, share, _ = got.shape
    share = share - 16
    rows, width = grads[0].shape
    gains = 0.0
    for index in range(count):
        owner = lax.rem(lax.axis_index("tensor") + count - index, count)
        input_grad[pl.ds(pl.multiple_of(owner * rows, rows), rows), :] = grads[index][...]
        held[index * share : (index + 1) * share] = got[index, :share].astype(FULL)
        gains = gains + jnp.concatenate(join_rows(got[index, share:]), 0)
    down_grad[...] = held[: down_grad.shape[0]]
    attn_gain[...] = gains[0:1]
    ffn_gain[...] = gains[1:2]
    kv_gain[...] = gains[2:3, : kv_gain.shape[1]]
    entries = jnp.where(
        lax.broadcasted_iota(jnp.int32, rms.shape, 1) == 1, float(RANK), float(width)
    )
    rms[...] = jnp.sqrt(
        gains[3:4, : rms.shape[1]] / (entries * (rows * count * lax.axis_size("dp")))
    )
    start = query_grad.shape[1]
    query_grad[...] = tokens[:start].T
    end = start + out_grad.shape[0]
    out_grad[...] = tokens[start:end]
    router_grad[...] = tokens[end : end + EXPERTS]
    lines = up_grad.shape[0]
    for column in range(up_grad.shape[1] // LANES):
        first = end + EXPERTS + column * lines
        up_grad[:, column * LANES : (column + 1) * LANES] = tokens[first : first + lines]
    rows = gate_grad.shape[0]
    for index, out in enumerate((gate_grad, shared_up_grad, shared_down_grad)):
        here = slice(index * rows, (index + 1) * rows)
        total = shared[0][here]
        for ref in shared[1:]:
            total = total + ref[here].astype(FULL)
        out[...] = total


def after(value, *others):
    return lax.optimization_barrier((value, *others))[0]


def swap_blocks(blocks, axis, groups=None):
    return lax.all_to_all(blocks, axis, 0, 0, tiled=True, axis_index_groups=groups)


def shift_z(block, shift):
    if shift == 0:
        return block
    count = lax.axis_size("tensor")
    return lax.ppermute(block, "tensor", [(i, (i + 2 * shift) % count) for i in range(count)])


def shift_tensor(block, shift):
    if shift == 0:
        return block
    count = lax.axis_size("tensor")
    return lax.ppermute(block, "tensor", [(i, (i + shift) % count) for i in range(count)])


def per_device(
    hidden_in,
    norm_attn,
    q_weight,
    kv_down,
    kv_norm,
    kv_up,
    out_weight,
    norm_ffn,
    router,
    expert_gate,
    expert_up,
    expert_down,
    shared_gate,
    shared_up,
    shared_down,
    routes,
    cotangent,
):
    tok_rows, width = hidden_in.shape
    dp_count = lax.axis_size("dp")
    tensor_count = lax.axis_size("tensor")
    local_experts = expert_gate.shape[0]
    part_rows = tok_rows // tensor_count
    hidden_part = expert_gate.shape[2]
    heads_local = q_weight.shape[1] // (NOPE + ROPE)
    heads_width = heads_local * (NOPE + VDIM)
    scaling = (NOPE + ROPE) ** (-0.5)
    group_devs = GROUP // tok_rows
    prompt_devs = PROMPT // tok_rows
    dp_place = lax.axis_index("dp")
    tensor_place = lax.axis_index("tensor")
    place = dp_place % group_devs
    quarter = place % prompt_devs
    z_place = tensor_place // 2
    group_base = (dp_place - place) * tok_rows

    def own_part(values):
        return lax.dynamic_slice_in_dim(values, tensor_place * part_rows, part_rows, 0)

    def meta(*entries):
        return jnp.stack([jnp.asarray(entry, jnp.int32) for entry in entries])

    ramp = jnp.arange(tok_rows, dtype=jnp.int32)
    position, unused_seg, unused_group = token_layout(dp_place * tok_rows + ramp)
    cos_table, sin_table = angle_tables(position)
    gain_first, gain_second, gain_kv = norm_attn[None], norm_ffn[None], kv_norm[None]
    down_rows_kv = kv_down.T
    router_rows = router.T
    kv_width = RANK + 2 * ROPE
    stacks = [expert_gate.transpose(0, 2, 1), expert_up.transpose(0, 2, 1), expert_down]
    near_rows = 3 * hidden_part
    slot_count = dp_count * CAP
    attn_in, packed_own, kv_raw, pack_ahead, pack_behind = run_kernel(
        latent_kernel,
        (hidden_in, gain_first, down_rows_kv, gain_kv, cos_table, sin_table, *stacks),
        [VMEM] * 6 + [HBM] * 3,
        [
            ((tok_rows, width), LOW),
            ((tok_rows, kv_width), LOW),
            ((tok_rows, RANK + ROPE), FULL),
            ((near_rows, width), LOW),
            ((near_rows, width), LOW),
        ],
        [pltpu.VMEM((2 * near_rows, width), LOW), pltpu.SemaphoreType.DMA((8,))],
        [VMEM] * 3 + [HBM] * 2,
    )
    ahead, behind = shift_z(pack_ahead, 1), shift_z(pack_behind, 3)
    copied = lax.ppermute(
        packed_own,
        "dp",
        [
            (base + i, base + prompt_devs + i)
            for base in range(0, dp_count, group_devs)
            for i in range(prompt_devs)
        ],
    )
    query, dispatch, taken_grads = run_kernel(
        early_kernel,
        (after(attn_in, copied), q_weight, cos_table, sin_table, routes.T, cotangent),
        [VMEM] * 6,
        [
            ((tok_rows, heads_local * 2 * LANES), LOW),
            ((slot_count, tok_rows), LOW),
            ((slot_count, 2 * width), LOW),
        ],
        [pltpu.VMEM((slot_count, width), LOW), pltpu.SemaphoreType.DMA],
        [VMEM] * 2 + [HBM],
    )
    combine = dispatch.T
    (pack_far,) = run_kernel(
        far_pack_kernel,
        (*stacks[:2], after(stacks[2], query)),
        [HBM] * 3,
        [((near_rows, width), LOW)],
        [pltpu.VMEM((near_rows, width), LOW), pltpu.SemaphoreType.DMA((4,))],
        [HBM],
    )
    first_block = jnp.where(place < prompt_devs, packed_own, copied)
    blocks = [first_block]
    for shift in range(1, prompt_devs):
        blocks.append(
            lax.ppermute(
                first_block,
                "dp",
                [
                    (base + i, base + (i + shift) % prompt_devs)
                    for base in range(0, dp_count, prompt_devs)
                    for i in range(prompt_devs)
                ],
            )
        )
    blocks.append(packed_own)
    attend_meta = meta(
        place, *[(quarter - shift) % prompt_devs for shift in range(prompt_devs)]
    )
    key_rows = len(blocks) * tok_rows
    attn_part, attn_low, kv_heads, log_sum = run_kernel(
        attend_kernel,
        (attend_meta, *blocks, query, kv_up, out_weight),
        [SMEM] + [VMEM] * 8,
        [
            ((tok_rows, width), LOW),
            ((tok_rows, heads_local * VDIM), LOW),
            ((key_rows, heads_width), LOW),
            ((tok_rows, heads_local * LANES), FULL),
        ],
    )
    part_meta = meta(tensor_place)

    def by_part(values):
        return values.reshape(tensor_count, part_rows, values.shape[-1])

    middle, copies = run_kernel(
        middle_kernel,
        (part_meta, swap_blocks(by_part(attn_part), "tensor"), hidden_in, gain_second),
        [SMEM] + [VMEM] * 3,
        [((part_rows, width), FULL), ((tensor_count, part_rows, width), LOW)],
    )
    ffn_in = swap_blocks(after(copies, ahead, behind, pack_far), "tensor").reshape(tok_rows, width)

    (taken_rows,) = run_kernel(
        take_kernel,
        (dispatch, ffn_in, taken_grads),
        [VMEM] * 2 + [HBM],
        [((slot_count, 2 * width), LOW)],
        [pltpu.VMEM((slot_count, width), LOW), pltpu.SemaphoreType.DMA],
        [HBM],
        aliases={2: 0},
    )
    expert_rows = swap_blocks(taken_rows.reshape(dp_count, CAP, 2 * width), "dp").reshape(
        slot_count, 2 * width
    )
    far = shift_z(after(pack_far, taken_rows), 2)

    shared_width = shared_gate.shape[1]
    shared_back, shared_part, shared_keep, shared_send = run_kernel(
        shared_kernel,
        (after(ffn_in, taken_rows), cotangent, shared_gate.T, shared_up.T, shared_down),
        [VMEM] * 5,
        [
            ((tok_rows, width), LOW),
            ((tok_rows, width), LOW),
            ((3 * shared_width, width // 2), LOW),
            ((3 * shared_width, width // 2), LOW),
        ],
        [pltpu.VMEM((3 * shared_width, width), FULL)],
        mib=32,
    )

    def exchange_dp(block, flip):
        return lax.ppermute(block, "dp", [(i, i ^ flip) for i in range(dp_count)])

    def join_cores(keep, arrived):
        shape = (keep.shape[0], keep.shape[1] // 2)
        return run_kernel(
            join_cores_kernel, (keep, arrived), [VMEM] * 2, [(shape, FULL), (shape, LOW)],
        mib=16,
    )

    def join_sides(keep, arrived):
        shape = (keep.shape[0], LANES)
        return run_kernel(
            join_sides_kernel, (keep, arrived), [VMEM] * 2, [(shape, FULL)] + [(shape, LOW)] * 3
        )

    def along_x(blocks):
        return [
            lax.ppermute(block, "dp", [(i, (i + 4 * shift) % dp_count) for i in range(dp_count)])
            for shift, block in enumerate(blocks, 1)
        ]

    shared_keep, shared_send = join_cores(shared_keep, after(exchange_dp(shared_send, 1), far))
    shared_arrived = exchange_dp(shared_send, 2)

    own_hidden = local_experts * hidden_part
    wide = 2 * width + LANES
    back_rows, hidden_low, gate_low, up_low, slot_gate = run_kernel(
        expert_kernel,
        (
            meta(dp_place * local_experts + z_place),
            expert_rows,
            *stacks,
            ahead,
            far,
            behind,
            after(router_rows, shared_keep),
        ),
        [SMEM] + [HBM] * 7 + [VMEM],
        [
            ((slot_count, wide), LOW),
            ((slot_count, own_hidden), LOW),
            ((slot_count, own_hidden), LOW),
            ((slot_count, own_hidden), LOW),
            ((slot_count, LANES), FULL),
        ],
        [
            pltpu.VMEM((slot_count, width), LOW),
            pltpu.VMEM((slot_count, width), LOW),
            pltpu.VMEM((3, own_hidden, width), LOW),
            pltpu.VMEM((slot_count, wide), LOW),
            pltpu.SemaphoreType.DMA((2,)),
            pltpu.SemaphoreType.DMA((3, 4)),
            pltpu.SemaphoreType.DMA((2,)),
        ],
        [HBM] + [VMEM] * 4,
        mib=44,
    )

    back_rows = swap_blocks(
        after(back_rows, shared_arrived).reshape(dp_count, CAP, wide), "dp"
    ).reshape(slot_count, wide)
    shared_own, *shared_blocks = join_sides(shared_keep, shared_arrived)
    turns = 2
    step = width // turns

    def weight_grad(kernel, operands, first):
        whole = [pl.BlockSpec(v.shape, lambda turn: (0, 0)) for v in operands]
        return run_kernel(
            kernel,
            (expert_rows, *operands),
            [pl.BlockSpec((slot_count, step), lambda turn: (0, first * turns + turn))] + whole,
            [((hidden_part, width), LOW)] * local_experts,
            out_specs=[pl.BlockSpec((hidden_part, step), lambda turn: (0, turn))] * local_experts,
            grid=(turns,),
            mib=20,
        )

    in_grads = [weight_grad(expert_in_grad_kernel, (low,), 0) for low in (gate_low, up_low)]
    down_grads = weight_grad(expert_out_grad_kernel, (hidden_low, slot_gate), 1)
    back_rows = after(
        back_rows, in_grads[0][0], in_grads[1][0], down_grads[0], shared_own
    )
    early = [(0, 1), (0, 3), (1, 1), (1, 3), (0, 2)]
    early_homes = {
        (kind, shift): shift_z(in_grads[kind][shift], local_experts - shift)
        for kind, shift in early
    }

    (payload,) = run_kernel(
        combine_kernel,
        (
            meta(z_place, local_experts),
            combine,
            after(back_rows, down_grads[0], *early_homes.values()),
            shared_back,
            shared_part,
        ),
        [SMEM] + [VMEM] * 4,
        [((tok_rows, wide), LOW)],
        mib=24,
    )
    middle_grad, copies, norm_ffn_grad, middle_sums = run_kernel(
        ffn_back_kernel,
        (
            part_meta,
            middle,
            ffn_in,
            router_rows,
            gain_second,
            cotangent,
            swap_blocks(by_part(payload), "tensor"),
        ),
        [SMEM] + [VMEM] * 6,
        [
            ((part_rows, width), FULL),
            ((tensor_count, part_rows, wide), LOW),
            ((1, width), FULL),
            ((1, LANES), FULL),
        ],
        mib=20,
    )
    shared_blocks = along_x(lax.optimization_barrier((*shared_blocks, payload))[:-1])
    shared_blocks = [shared_own, *shared_blocks]
    spread = after(swap_blocks(copies, "tensor"), *shared_blocks).reshape(tok_rows, wide)
    late_homes = {(1, 2): shift_z(after(in_grads[1][2], spread), local_experts - 2)}

    kv_part, query_part, heads_low, query_low = run_kernel(
        attend_back_kernel,
        (
            attend_meta,
            out_weight,
            *blocks,
            query,
            kv_heads,
            log_sum,
            kv_up,
            cos_table,
            sin_table,
            spread,
            q_weight,
        ),
        [SMEM] + [VMEM] * 14,
        [
            ((tensor_count, part_rows, len(blocks) * kv_width), LOW),
            ((tok_rows, width), LOW),
            ((key_rows, heads_width), LOW),
            ((tok_rows, heads_local * (NOPE + ROPE)), LOW),
        ],
    )
    got_parts = swap_blocks(after(kv_part, late_homes[1, 2]), "tensor")
    *prompt_parts, kv_own = run_kernel(
        kv_sum_kernel,
        (got_parts,),
        [VMEM],
        [((part_rows, kv_width), LOW)] * prompt_devs + [((part_rows, kv_width), FULL)],
    )
    (joined,) = run_kernel(
        kv_join_kernel,
        [prompt_parts[0]]
        + [
            lax.ppermute(
                prompt_parts[shift],
                "dp",
                [
                    (base + i, base + (i - shift) % prompt_devs)
                    for base in range(0, dp_count, prompt_devs)
                    for i in range(prompt_devs)
                ],
            )
            for shift in range(1, prompt_devs)
        ],
        [VMEM] * prompt_devs,
        [((part_rows, kv_width), LOW)],
    )
    other = lax.ppermute(
        joined,
        "dp",
        [
            (base + prompt_devs + i, base + i)
            for base in range(0, dp_count, group_devs)
            for i in range(prompt_devs)
        ],
    )
    got_query = swap_blocks(after(by_part(query_part), kv_own), "tensor")
    for shift in (1, 3, 2):
        late_homes[2, shift] = shift_z(after(down_grads[shift], kv_own), local_experts - shift)

    def place_grads(kind):
        grads = (*in_grads, down_grads)[kind]
        arrived = early_homes | late_homes
        return run_kernel(
            place_kernel,
            (
                meta(z_place),
                grads[0],
                *[arrived[kind, shift] for shift in range(1, local_experts)],
            ),
            [SMEM] + [VMEM] * 4,
            [((local_experts, hidden_part, width), FULL)],
        )[0]

    gate_wgrad = place_grads(0)
    copies, grad_low, norm_attn_grad, kv_norm_grad, square_sums = run_kernel(
        last_kernel,
        (
            meta(tensor_place, place),
            joined,
            other,
            kv_own,
            kv_raw,
            gain_kv,
            cos_table,
            sin_table,
            down_rows_kv,
            hidden_in,
            gain_first,
            after(middle_grad, gate_wgrad),
            middle_sums,
            got_query,
        ),
        [SMEM] + [VMEM] * 13,
        [
            ((tensor_count, part_rows, kv_width), LOW),
            ((part_rows, width), LOW),
            ((1, width), FULL),
            ((1, RANK), FULL),
            ((1, LANES), FULL),
        ],
    )
    up_wgrad = place_grads(1)
    kv_low_all = swap_blocks(copies, "tensor").reshape(tok_rows, kv_width)
    down_wgrad = place_grads(2)

    query_width = q_weight.shape[1]
    own_width, own_rank = width // dp_count, RANK // dp_count
    up_lines = own_rank * heads_width // LANES
    attn_width = heads_local * VDIM
    token_rows = query_width + attn_width + EXPERTS + up_lines
    token_grads, output = run_kernel(
        token_grad_kernel,
        (attn_in, query_low, attn_low, spread, ffn_in, heads_low, *blocks),
        [VMEM] * (6 + len(blocks)),
        [
            ((token_rows, width), FULL),
            ((tok_rows, width), LOW),
        ],
        mib=28,
    )
    token_grads = lax.psum_scatter(
        after(token_grads, got_parts), "dp", scatter_dimension=1, tiled=True
    )
    share = kv_width // tensor_count
    grad_low = after(grad_low, kv_low_all)
    grad_parts = [shift_tensor(grad_low, shift) for shift in range(tensor_count)]
    (mixed,) = run_kernel(
        mix_kernel,
        (
            part_meta,
            after(kv_low_all, up_wgrad, late_homes[2, 1], late_homes[2, 3]),
            attn_in,
            norm_attn_grad,
            norm_ffn_grad,
            kv_norm_grad,
            square_sums,
        ),
        [SMEM] + [VMEM] * 6,
        [((dp_count, share + 16, LANES), LOW)],
        mib=16,
    )
    (copies,) = run_kernel(
        mix_sum_kernel,
        (after(swap_blocks(mixed, "dp"), late_homes[2, 2], *grad_parts[1:6]),),
        [VMEM],
        [((tensor_count, share + 16, LANES), LOW)],
        mib=16,
    )
    shared_width = shared_gate.shape[1]
    (
        input_grad,
        down_grad,
        attn_gain,
        ffn_gain,
        kv_gain,
        rms,
        query_grad,
        up_grad,
        out_grad,
        router_grad,
        *shared_out,
    ) = run_kernel(
        final_kernel,
        (swap_blocks(copies, "tensor"), token_grads, *grad_parts, *shared_blocks),
        [VMEM] * (2 + tensor_count + len(shared_blocks)),
        [
            ((tok_rows, width), LOW),
            ((RANK + ROPE, own_width), FULL),
            ((1, LANES), FULL),
            ((1, LANES), FULL),
            ((1, own_rank), FULL),
            ((1, 5), FULL),
            ((own_width, query_width), FULL),
            ((own_rank, heads_width), FULL),
            ((attn_width, own_width), FULL),
            ((EXPERTS, own_width), FULL),
        ]
        + [((shared_width, own_width), FULL)] * 3,
        [pltpu.VMEM((kv_width, LANES), FULL)],
        mib=16,
    )
    return (
        output,
        input_grad,
        attn_gain.reshape(own_width),
        query_grad,
        down_grad.T,
        kv_gain.reshape(own_rank),
        up_grad,
        out_grad,
        ffn_gain.reshape(own_width),
        router_grad.T,
        gate_wgrad.transpose(0, 2, 1),
        up_wgrad.transpose(0, 2, 1),
        down_wgrad,
        shared_out[0].T,
        shared_out[1].T,
        shared_out[2],
        rms.reshape(5),
    )


def solution(mesh):
    return jax.shard_map(
        per_device,
        mesh=mesh,
        in_specs=(
            P("dp", None),
            P(),
            P(None, "tensor"),
            P(),
            P(),
            P(None, "tensor"),
            P("tensor", None),
            P(),
            P(),
            P("dp", None, "tensor"),
            P("dp", None, "tensor"),
            P("dp", "tensor", None),
            P(None, "tensor"),
            P(None, "tensor"),
            P("tensor", None),
            P("dp", None),
            P("dp", None),
        ),
        out_specs=(
            P("dp", None),
            P("dp", None),
            P("dp"),
            P("dp", "tensor"),
            P("dp", None),
            P("dp"),
            P("dp", "tensor"),
            P("tensor", "dp"),
            P("dp"),
            P("dp", None),
            P("dp", None, "tensor"),
            P("dp", None, "tensor"),
            P("dp", "tensor", None),
            P("dp", "tensor"),
            P("dp", "tensor"),
            P("tensor", "dp"),
            P(),
        ),
        check_vma=False,
    )
```

```python
import functools

import jax
import jax.numpy as jnp
from jax import lax
from jax.experimental import pallas as pl
from jax.experimental.pallas import tpu as pltpu
from jax.sharding import PartitionSpec as P

NOPE = 128
ROPE = 64
RANK = 512
VDIM = 128
TOP = 6
CAP = 32
PROMPT = 1024
CONT = 128
GROUP = 2048
EXPERTS = 64
LANES = 128
EPSILON = 1e-06
THETA = 10000.0
LOW = jnp.bfloat16
FULL = jnp.float32


def contract(first_arr, second_arr, first_axis, second_axis):
    return lax.dot_general(
        first_arr,
        second_arr,
        (((first_axis,), (second_axis,)), ((), ())),
        preferred_element_type=FULL,
    )


def rotate(values, cos_table, sin_table):
    half_width = values.shape[-1] // 2
    front = values[..., :half_width]
    behind = values[..., half_width:]
    return jnp.concatenate(
        [front * cos_table - behind * sin_table, behind * cos_table + front * sin_table], -1
    )


def token_layout(row_index):
    offset = row_index % GROUP
    in_prompt = offset < PROMPT
    position = jnp.where(in_prompt, offset, PROMPT + (offset - PROMPT) % CONT)
    segment = jnp.where(in_prompt, 0, 1 + (offset - PROMPT) // CONT)
    return (position, segment, row_index // GROUP)


def angle_tables(position):
    half_width = ROPE // 2
    frequency = THETA ** (-2.0 * jnp.arange(half_width, dtype=FULL) / ROPE)
    angles = position.astype(FULL)[:, None] * frequency[None]
    return (jnp.cos(angles), jnp.sin(angles))


def inverse_rms(values):
    return lax.rsqrt(jnp.mean(values * values, -1, keepdims=True) + EPSILON)


def norm_backward(grad_normed, normed, inverse, gain):
    scaled = grad_normed * gain
    return (
        inverse * (scaled - normed * jnp.mean(scaled * normed, -1, keepdims=True)),
        jnp.sum(grad_normed * normed, 0, keepdims=True),
    )


VMEM = pl.BlockSpec(memory_space=pltpu.VMEM)
SMEM = pl.BlockSpec(memory_space=pltpu.SMEM)
HBM = pl.BlockSpec(memory_space=pl.ANY)


def run_kernel(
    kernel, operands, specs, outs, scratch=(), out_specs=None, grid=(), aliases=None, mib=56
):
    shapes = [jax.ShapeDtypeStruct(shape, dtype) for shape, dtype in outs]
    return pl.pallas_call(
        kernel,
        out_shape=shapes,
        grid=grid,
        input_output_aliases=aliases or {},
        in_specs=list(specs),
        out_specs=list(out_specs or [VMEM] * len(shapes)),
        scratch_shapes=list(scratch),
        compiler_params=pltpu.CompilerParams(vmem_limit_bytes=mib * 1024 * 1024),
        cost_estimate=pl.CostEstimate(flops=1000, bytes_accessed=1000, transcendentals=0),
    )(*operands)


def latent_kernel(
    hidden,
    gain,
    down_rows,
    kv_gain,
    cos,
    sin,
    gate,
    up,
    down,
    attn_in,
    packed,
    kv_raw,
    ahead,
    behind,
    held,
    sems,
):
    parts = [[(kind, shift) for kind in range(3)] for shift in (1, 3)]
    picks = RowPicks((gate, up, down), (ahead, behind), parts, held, sems)
    picks.get()
    values = hidden[...].astype(FULL)
    normed = (values * inverse_rms(values) * gain[...]).astype(LOW)
    attn_in[...] = normed
    picks.put()
    raw = contract(normed, down_rows[...], 1, 1)
    kv_raw[...] = raw
    latent = raw[:, :RANK]
    packed[:, :RANK] = (latent * inverse_rms(latent) * kv_gain[...]).astype(LOW)
    rope = rotate(raw[:, RANK:], cos[...], sin[...]).astype(LOW)
    packed[:, RANK:] = jnp.concatenate([rope, jnp.zeros_like(rope)], -1)
    picks.wait()


def turn_queries(attn_in, q_weight, cos, sin, query):
    turned = jnp.dot(attn_in[...], q_weight[...], preferred_element_type=FULL)
    step = NOPE + ROPE
    for head in range(turned.shape[1] // step):
        place = head * 2 * LANES
        start = head * step
        query[:, place : place + NOPE] = turned[:, start : start + NOPE].astype(LOW)
        rope = rotate(turned[:, start + NOPE : start + step], cos[...], sin[...]).astype(LOW)
        query[:, place + NOPE : place + 2 * LANES] = jnp.concatenate(
            [rope, jnp.zeros_like(rope)], -1
        )


def visible_keys(meta, block, shape):
    rows = lax.broadcasted_iota(jnp.int32, shape, 0)
    cols = lax.broadcasted_iota(jnp.int32, shape, 1)
    place, prompt_devs = meta[0], PROMPT // shape[1]
    if block < prompt_devs:
        return cols - rows <= (place - meta[1 + block]) * shape[1]
    own = (cols <= rows) & (rows // CONT == cols // CONT)
    return own & (place >= prompt_devs)


def head_key(heads, rope, head):
    start = head * (NOPE + VDIM)
    return jnp.concatenate([heads[:, start : start + NOPE], rope], -1)


def attend_kernel(
    meta, first, second, third, fourth, own, query, kv_up, out_weight, part, attn, heads, log_sum
):
    blocks = (first, second, third, fourth, own)
    rows = own.shape[0]
    scaling = (NOPE + ROPE) ** (-0.5)
    for block, ref in enumerate(blocks):
        heads[block * rows : (block + 1) * rows] = jnp.dot(
            ref[:, :RANK], kv_up[...], preferred_element_type=FULL
        ).astype(LOW)
    masks = [visible_keys(meta, block, (rows, rows)) for block in range(len(blocks))]
    for head in range(query.shape[1] // (2 * LANES)):
        asked = query[:, head * 2 * LANES : (head + 1) * 2 * LANES]
        scores = []
        for block, ref in enumerate(blocks):
            key = head_key(heads[block * rows : (block + 1) * rows], ref[:, RANK:], head)
            raw = contract(asked, key, 1, 1) * scaling
            scores.append(jnp.where(masks[block], raw, -1e30))
        peak = scores[0]
        for score in scores[1:]:
            peak = jnp.maximum(peak, score)
        peak = jnp.max(peak, -1, keepdims=True)
        weights = [jnp.exp(score - peak) for score in scores]
        total = jnp.sum(functools.reduce(jnp.add, weights), -1, keepdims=True)
        scale = 1.0 / total
        summed = 0.0
        start = head * (NOPE + VDIM) + NOPE
        for block, weight in enumerate(weights):
            value = heads[block * rows : (block + 1) * rows, start : start + VDIM]
            summed = summed + jnp.dot(
                (weight * scale).astype(LOW), value, preferred_element_type=FULL
            )
        attn[:, head * VDIM : (head + 1) * VDIM] = summed.astype(LOW)
        log_sum[:, head * LANES : (head + 1) * LANES] = jnp.broadcast_to(
            peak + jnp.log(total), (rows, LANES)
        )
    part[...] = jnp.dot(attn[...], out_weight[...], preferred_element_type=FULL).astype(LOW)


def middle_kernel(meta, got, hidden, gain, middle, copies):
    part_rows = middle.shape[0]
    start = pl.multiple_of(meta[0] * part_rows, part_rows)
    values = hidden[pl.ds(start, part_rows), :].astype(FULL)
    for index in range(got.shape[0]):
        values = values + got[index].astype(FULL)
    middle[...] = values
    normed = (values * inverse_rms(values) * gain[...]).astype(LOW)
    for index in range(copies.shape[0]):
        copies[index] = normed


def split_cores(grads, keep, send):
    core = lax.axis_index("dp") % 2
    for chip in range(keep.shape[1] // LANES):
        here = slice(chip * LANES, (chip + 1) * LANES)
        first = pl.multiple_of((2 * chip + core) * LANES, LANES)
        other = pl.multiple_of((2 * chip + 1 - core) * LANES, LANES)
        keep[:, here] = grads[:, pl.ds(first, LANES)].astype(LOW)
        send[:, here] = grads[:, pl.ds(other, LANES)].astype(LOW)


def join_cores_kernel(kept, arrived, keep, send):
    side = lax.axis_index("dp") // 2 % 2
    for row in range(keep.shape[1] // LANES):
        here = slice(row * LANES, (row + 1) * LANES)
        for out, which in ((keep, 2 * row + side), (send, 2 * row + 1 - side)):
            there = pl.ds(pl.multiple_of(which * LANES, LANES), LANES)
            total = kept[:, there].astype(FULL) + arrived[:, there].astype(FULL)
            out[:, here] = total.astype(out.dtype)


def join_sides_kernel(kept, arrived, own, *outs):
    place, count = lax.axis_index("dp") // 4, len(outs) + 1
    for shift, out in enumerate((own, *outs)):
        owner = lax.rem(place + shift, count)
        there = pl.ds(pl.multiple_of(owner * LANES, LANES), LANES)
        total = kept[:, there] + arrived[:, there].astype(FULL)
        out[...] = total.astype(out.dtype)


def shared_kernel(ffn, cot, gate, up, down, back, out, keep, send, grads):
    rows = gate.shape[0]
    gate_pre = contract(ffn[...], gate[...], 1, 1)
    up_pre = contract(ffn[...], up[...], 1, 1)
    hidden_back = contract(cot[...], down[...], 1, 1)
    sig = jax.nn.sigmoid(gate_pre)
    low = (gate_pre * sig * up_pre).astype(LOW)
    gate_low = (hidden_back * up_pre * sig * (1.0 + gate_pre * (1.0 - sig))).astype(LOW)
    up_low = (hidden_back * gate_pre * sig).astype(LOW)
    out[...] = jnp.dot(low, down[...], preferred_element_type=FULL).astype(LOW)
    back[...] = (
        jnp.dot(gate_low, gate[...], preferred_element_type=FULL)
        + jnp.dot(up_low, up[...], preferred_element_type=FULL)
    ).astype(LOW)
    grads[:rows] = contract(gate_low, ffn[...], 0, 0)
    grads[rows : 2 * rows] = contract(up_low, ffn[...], 0, 0)
    grads[2 * rows :] = contract(low, cot[...], 0, 0)
    split_cores(grads, keep, send)


class RowPicks:
    def __init__(self, stacks, outs, parts, held, sems):
        count, rows = stacks[0].shape[:2]
        z_place = lax.axis_index("tensor") // 2
        self.gets, self.puts, start = [], [], 0
        for out, wanted in zip(outs, parts):
            first = start
            for kind, shift in wanted:
                source = stacks[kind].at[lax.rem(z_place + shift, count)]
                target = held.at[pl.ds(start, rows)]
                self.gets.append(pltpu.make_async_copy(source, target, sems.at[len(self.gets)]))
                start += rows
            self.puts.append((first, start, out, len(self.gets)))
        self.puts = [
            (
                needed,
                pltpu.make_async_copy(
                    held.at[pl.ds(first, end - first)], out, sems.at[len(self.gets) + index]
                ),
            )
            for index, (first, end, out, needed) in enumerate(self.puts)
        ]

    def get(self):
        for copy in self.gets:
            copy.start()

    def put(self):
        done = 0
        for needed, copy in self.puts:
            for earlier in self.gets[done:needed]:
                earlier.wait()
            done = needed
            copy.start()

    def wait(self):
        for needed, copy in self.puts:
            copy.wait()


def far_pack_kernel(gate, up, down, far, held, sems):
    picks = RowPicks((gate, up, down), (far,), [[(kind, 2) for kind in range(3)]], held, sems)
    picks.get()
    picks.put()
    picks.wait()


def early_kernel(
    attn_in, q_weight, cos, sin, routes, cot, query, dispatch, taken, held, sem
):
    copy = dispatch_rows(routes, cot, dispatch, held, taken, sem)
    turn_queries(attn_in, q_weight, cos, sin, query)
    copy.wait()


def dispatch_rows(routes, cot, dispatch, held, taken, sem):
    owners, tokens = dispatch.shape[0] // CAP, routes.shape[1]
    local_experts = EXPERTS // owners
    owner = lax.broadcasted_iota(jnp.int32, (owners, tokens), 0)
    expert = owner * local_experts + lax.axis_index("tensor") // 2
    chosen = jnp.zeros((owners, tokens), FULL)
    for turn in range(routes.shape[0]):
        chosen = jnp.where(routes[turn : turn + 1, :] == expert, 1.0, chosen)
    square = (tokens, tokens)
    earlier = lax.broadcasted_iota(jnp.int32, square, 0) < lax.broadcasted_iota(
        jnp.int32, square, 1
    )
    ranking = jnp.dot(
        chosen.astype(LOW), earlier.astype(FULL).astype(LOW), preferred_element_type=FULL
    )
    ranking = jnp.where(chosen > 0.0, ranking, -1.0)
    slot = lax.broadcasted_iota(jnp.int32, (CAP, tokens), 0).astype(FULL)
    for index in range(owners):
        dispatch[index * CAP : (index + 1) * CAP] = jnp.where(
            ranking[index : index + 1, :] == slot, 1.0, 0.0
        ).astype(LOW)
    held[...] = jnp.dot(dispatch[...], cot[...], preferred_element_type=FULL).astype(LOW)
    width = cot.shape[1]
    copy = pltpu.make_async_copy(held, taken.at[:, pl.ds(width, width)], sem)
    copy.start()
    return copy


def take_kernel(dispatch, rows, grads, taken, held, sem):
    held[...] = jnp.dot(dispatch[...], rows[...], preferred_element_type=FULL).astype(LOW)
    copy = pltpu.make_async_copy(held, taken.at[:, pl.ds(0, rows.shape[1])], sem)
    copy.start()
    copy.wait()


def chunk_copies(own, pieces, held, sems):
    part = own.shape[1]
    sources = [own.at[lax.axis_index("tensor") // 2]]
    sources += [ref.at[pl.ds(first, part)] for ref, first in pieces]
    return [
        pltpu.make_async_copy(source, held.at[pl.ds(index * part, part)], sems.at[index])
        for index, source in enumerate(sources)
    ]


def expert_kernel(
    meta,
    rows_in,
    gate_in,
    up_in,
    down_in,
    ahead,
    far,
    behind,
    router,
    back,
    hidden_out,
    gate_out,
    up_out,
    slot_gate,
    rows_held,
    grad_held,
    weights,
    out_held,
    row_sems,
    weight_sems,
    out_sems,
):
    count, width = rows_held.shape
    part = gate_in.shape[1]
    get_rows, get_grads = [
        pltpu.make_async_copy(rows_in.at[:, pl.ds(first, width)], held, row_sems.at[index])
        for index, (first, held) in enumerate(((0, rows_held), (width, grad_held)))
    ]
    get_gate, get_up, get_down = [
        chunk_copies(
            own,
            [(ref, kind * part) for ref in (ahead, far, behind)],
            weights.at[kind],
            weight_sems.at[kind],
        )
        for kind, own in enumerate((gate_in, up_in, down_in))
    ]
    gate_w, up_w, down_w = [weights.at[kind] for kind in range(3)]
    split = width + LANES
    puts = [
        pltpu.make_async_copy(
            out_held.at[:, pl.ds(first, size)],
            back.at[:, pl.ds(first, size)],
            out_sems.at[index],
        )
        for index, (first, size) in enumerate(((0, split), (split, width)))
    ]
    for copy in (get_rows, *get_gate, *get_up, get_grads, *get_down):
        copy.start()

    def wait_all(copies):
        for copy in copies:
            copy.wait()

    get_rows.wait()
    rows = rows_held[...]
    logits = contract(rows, router[...], 1, 1)
    logits = jnp.exp(logits - jnp.max(logits, -1, keepdims=True))
    mine = lax.broadcasted_iota(jnp.int32, logits.shape, 1) == meta[0]
    gate = jnp.sum(jnp.where(mine, logits, 0.0), -1, keepdims=True) / jnp.sum(
        logits, -1, keepdims=True
    )
    slot_gate[...] = jnp.broadcast_to(gate, (count, LANES))
    wait_all(get_gate)
    gate_pre = contract(rows, gate_w[...], 1, 1)
    sig = jax.nn.sigmoid(gate_pre)
    wait_all(get_up)
    up_pre = contract(rows, up_w[...], 1, 1)
    low = (gate_pre * sig * up_pre).astype(LOW)
    hidden_out[...] = low
    get_grads.wait()
    wait_all(get_down)
    hidden_back = contract(grad_held[...], down_w[...], 1, 1)
    dots = jnp.sum(low.astype(FULL) * hidden_back, -1, keepdims=True)
    hidden_back = hidden_back * gate
    gate_low = (hidden_back * up_pre * sig * (1.0 + gate_pre * (1.0 - sig))).astype(LOW)
    up_low = (hidden_back * gate_pre * sig).astype(LOW)
    gate_out[...] = gate_low
    up_out[...] = up_low
    out_held[:, :width] = (
        jnp.dot(gate_low, gate_w[...], preferred_element_type=FULL)
        + jnp.dot(up_low, up_w[...], preferred_element_type=FULL)
    ).astype(LOW)
    high = dots.astype(LOW).astype(FULL)
    lane = lax.broadcasted_iota(jnp.int32, (count, LANES), 1)
    out_held[:, width:split] = jnp.where(
        lane == 0, high, jnp.where(lane == 1, dots - high, 0.0)
    ).astype(LOW)
    puts[0].start()
    out_held[:, split:] = (jnp.dot(low, down_w[...], preferred_element_type=FULL) * gate).astype(
        LOW
    )
    puts[1].start()
    wait_all(puts)


def expert_in_grad_kernel(rows, low, *grads):
    part = grads[0].shape[0]
    grad = contract(low[...], rows[...], 0, 0).astype(LOW)
    for index, ref in enumerate(grads):
        ref[...] = grad[index * part : (index + 1) * part]


def expert_out_grad_kernel(grad_in, hidden, slot_gate, *grads):
    part = grads[0].shape[0]
    scaled = (grad_in[...].astype(FULL) * slot_gate[:, :1]).astype(LOW)
    grad = contract(hidden[...], scaled, 0, 0).astype(LOW)
    for index, ref in enumerate(grads):
        ref[...] = grad[index * part : (index + 1) * part]


def combine_kernel(meta, combine, returned, shared_back, shared_part, payload):
    width = shared_back.shape[1]
    payload[:, :width] = (
        jnp.dot(combine[...], returned[:, :width], preferred_element_type=FULL)
        + shared_back[...].astype(FULL)
    ).astype(LOW)
    slot_rows = returned.shape[0]
    slot = lax.broadcasted_iota(jnp.int32, (slot_rows, EXPERTS), 0) // CAP
    at_expert = slot * meta[1] + meta[0] == lax.broadcasted_iota(
        jnp.int32, (slot_rows, EXPERTS), 1
    )
    dots = returned[:, width : width + LANES].astype(FULL)
    summed = 0.0
    for index in range(2):
        columns = jnp.where(at_expert, dots[:, index : index + 1], 0.0).astype(LOW)
        summed = summed + jnp.dot(combine[...], columns, preferred_element_type=FULL)
    high = summed.astype(LOW)
    rest = (summed - high.astype(FULL)).astype(LOW)
    payload[:, width : width + LANES] = jnp.concatenate([high, rest], -1)
    payload[:, width + LANES :] = (
        jnp.dot(combine[...], returned[:, width + LANES :], preferred_element_type=FULL)
        + shared_part[...].astype(FULL)
    ).astype(LOW)


def token_grad_kernel(attn_in, query_low, attn_low, spread, ffn, heads_low, *refs):
    blocks, (grads, router_part, output) = refs[:-3], refs[-3:]
    width = attn_in.shape[1]
    output[...] = spread[:, width + LANES :]
    rows = attn_in.shape[0]
    start = query_low.shape[1]
    grads[:start] = contract(query_low[...], attn_in[...], 0, 0)
    end = start + attn_low.shape[1]
    grads[start:end] = contract(attn_low[...], spread[:, :width], 0, 0)
    router_part[...] = contract(spread[:, width : width + LANES], ffn[...], 0, 0)[:EXPERTS].astype(LOW)
    total = 0.0
    for index, ref in enumerate(blocks):
        total = total + contract(ref[:, :RANK], heads_low[index * rows : (index + 1) * rows], 0, 0)
    owners = width // LANES
    lines = total.shape[0] // owners
    for column in range(total.shape[1] // LANES):
        for owner in range(owners):
            grads[
                end + column * lines : end + (column + 1) * lines,
                owner * LANES : (owner + 1) * LANES,
            ] = total[owner * lines : (owner + 1) * lines, column * LANES : (column + 1) * LANES]


def place_kernel(meta, first, second, third, fourth, out):
    for shift, chunk in enumerate((first, second, third, fourth)):
        out[lax.rem(meta[0] + shift, out.shape[0])] = chunk[...].astype(FULL)


def ffn_back_kernel(
    meta, middle, ffn, router, gain, cot, got, middle_grad, copies, gain_grad, sums
):
    part_rows, width = middle.shape
    start = pl.multiple_of(meta[0] * part_rows, part_rows)
    here = pl.ds(start, part_rows)
    total = got[0].astype(FULL)
    for index in range(1, got.shape[0]):
        total = total + got[index].astype(FULL)
    extra = total[:, width : width + LANES]
    prob_grad = extra[:, :EXPERTS] + extra[:, EXPERTS:]
    logits = contract(ffn[here, :], router[...], 1, 1)
    logits = jnp.exp(logits - jnp.max(logits, -1, keepdims=True))
    prob = logits / jnp.sum(logits, -1, keepdims=True)
    logit_low = (
        prob * (prob_grad - jnp.sum(prob * prob_grad, -1, keepdims=True))
    ).astype(LOW)
    ffn_grad = total[:, :width] + jnp.dot(logit_low, router[...], preferred_element_type=FULL)
    values = middle[...]
    inverse = inverse_rms(values)
    back, gains = norm_backward(ffn_grad, values * inverse, inverse, gain[...])
    gain_grad[...] = gains
    grad = cot[here, :].astype(FULL) + back
    middle_grad[...] = grad
    low = grad.astype(LOW)
    tail = jnp.concatenate([logit_low, jnp.zeros_like(logit_low)], -1)
    result = values + total[:, width + LANES :]
    result_low = result.astype(LOW)
    for index in range(copies.shape[0]):
        copies[index, :, :width] = low
        copies[index, :, width : width + LANES] = tail
        copies[index, :, width + LANES :] = result_low
    lane = lax.broadcasted_iota(jnp.int32, sums.shape, 1)
    sums[...] = jnp.where(lane == 2, jnp.sum(values * values), 0.0) + jnp.where(
        lane == 3, jnp.sum(result * result), 0.0
    )


def attend_back_kernel(
    meta,
    out_weight,
    first,
    second,
    third,
    fourth,
    own,
    query,
    heads,
    log_sum,
    kv_up,
    cos,
    sin,
    spread,
    q_weight,
    kv_part,
    query_part,
    heads_low,
    query_low,
):
    blocks = (first, second, third, fourth, own)
    rows = own.shape[0]
    parts, part_rows, _ = kv_part.shape
    kv_width = RANK + 2 * ROPE
    scaling = (NOPE + ROPE) ** (-0.5)
    attn_grad = contract(spread[:, : out_weight.shape[1]], out_weight[...], 1, 1).astype(LOW)
    masks = [visible_keys(meta, block, (rows, rows)) for block in range(len(blocks))]
    ropes = [0.0] * len(blocks)
    step = NOPE + ROPE
    for head in range(query.shape[1] // (2 * LANES)):
        asked = query[:, head * 2 * LANES : (head + 1) * 2 * LANES]
        out_grad = attn_grad[:, head * VDIM : (head + 1) * VDIM]
        logs = log_sum[:, head * LANES : head * LANES + 1]
        start = head * (NOPE + VDIM)
        probs, backs = [], []
        summed = 0.0
        for block, ref in enumerate(blocks):
            here = slice(block * rows, (block + 1) * rows)
            key = head_key(heads[here], ref[:, RANK:], head)
            raw = contract(asked, key, 1, 1) * scaling
            prob = jnp.exp(jnp.where(masks[block], raw, -1e30) - logs)
            back = contract(out_grad, heads[here, start + NOPE : start + NOPE + VDIM], 1, 1)
            summed = summed + prob * back
            probs.append(prob)
            backs.append(back)
        total = jnp.sum(summed, -1, keepdims=True)
        asked_grad = 0.0
        for block, ref in enumerate(blocks):
            here = slice(block * rows, (block + 1) * rows)
            score_low = (scaling * probs[block] * (backs[block] - total)).astype(LOW)
            key = head_key(heads[here], ref[:, RANK:], head)
            asked_grad = asked_grad + jnp.dot(score_low, key, preferred_element_type=FULL)
            key_grad = contract(score_low, asked, 0, 0)
            heads_low[here, start : start + NOPE] = key_grad[:, :NOPE].astype(LOW)
            heads_low[here, start + NOPE : start + NOPE + VDIM] = contract(
                probs[block].astype(LOW), out_grad, 0, 0
            ).astype(LOW)
            ropes[block] = ropes[block] + key_grad[:, NOPE:]
        query_low[:, head * step : head * step + NOPE] = asked_grad[:, :NOPE].astype(LOW)
        query_low[:, head * step + NOPE : (head + 1) * step] = rotate(
            asked_grad[:, NOPE:step], cos[...], -sin[...]
        ).astype(LOW)
    for block in range(len(blocks)):
        here = slice(block * rows, (block + 1) * rows)
        latent = contract(heads_low[here], kv_up[...], 1, 1).astype(LOW)
        rope = ropes[block].astype(LOW)
        start = block * kv_width
        for index in range(parts):
            mine = slice(index * part_rows, (index + 1) * part_rows)
            kv_part[index, :, start : start + RANK] = latent[mine]
            kv_part[index, :, start + RANK : start + kv_width] = rope[mine]
    query_part[...] = contract(query_low[...], q_weight[...], 1, 1).astype(LOW)


def kv_sum_kernel(got, first, second, third, fourth, own):
    kv_width = own.shape[1]
    total = got[0].astype(FULL)
    for index in range(1, got.shape[0]):
        total = total + got[index].astype(FULL)
    blocks = (first, second, third, fourth)
    for block, out in enumerate(blocks):
        out[...] = total[:, block * kv_width : (block + 1) * kv_width].astype(LOW)
    own[...] = total[:, len(blocks) * kv_width :]


def kv_join_kernel(first, second, third, fourth, out):
    total = first[...].astype(FULL) + second[...].astype(FULL)
    out[...] = (total + third[...].astype(FULL) + fourth[...].astype(FULL)).astype(LOW)


def last_kernel(
    meta,
    joined,
    other,
    own,
    kv_raw,
    kv_gain,
    cos,
    sin,
    down_rows,
    hidden,
    gain,
    middle_grad,
    sums_in,
    got_query,
    copies,
    grad_low,
    gain_grad,
    kv_gain_grad,
    sums,
):
    part_rows, width = middle_grad.shape
    here = pl.ds(pl.multiple_of(meta[0] * part_rows, part_rows), part_rows)
    in_prompt = meta[1] < PROMPT // hidden.shape[0]
    found = joined[...].astype(FULL) + other[...].astype(FULL)
    total = jnp.where(in_prompt, found, own[...])
    latent = kv_raw[here, :RANK]
    inverse = inverse_rms(latent)
    latent_grad, kv_gains = norm_backward(
        total[:, :RANK], latent * inverse, inverse, kv_gain[...]
    )
    kv_gain_grad[...] = kv_gains
    rope = rotate(total[:, RANK : RANK + ROPE], cos[here, :], -sin[here, :]).astype(LOW)
    latent_low = latent_grad.astype(LOW)
    kv_low = jnp.concatenate([latent_low, rope], -1)
    tail = jnp.concatenate([rope, jnp.zeros_like(rope)], -1)
    for index in range(copies.shape[0]):
        copies[index, :, :RANK] = latent_low
        copies[index, :, RANK:] = tail
    attn_in_grad = jnp.dot(kv_low, down_rows[...], preferred_element_type=FULL)
    for index in range(got_query.shape[0]):
        attn_in_grad = attn_in_grad + got_query[index].astype(FULL)
    values = hidden[here, :].astype(FULL)
    inverse = inverse_rms(values)
    back, gains = norm_backward(attn_in_grad, values * inverse, inverse, gain[...])
    gain_grad[...] = gains
    grad = middle_grad[...] + back
    grad_low[...] = grad.astype(LOW)
    lane = lax.broadcasted_iota(jnp.int32, sums.shape, 1)
    found = sums_in[...]
    for index, part in ((0, values), (1, latent), (4, grad)):
        found = found + jnp.where(lane == index, jnp.sum(part * part), 0.0)
    sums[...] = found


def split_rows(rows):
    high = [row.astype(LOW).astype(FULL) for row in rows]
    low = [row - part for row, part in zip(rows, high)]
    blank = jnp.zeros((16 - 2 * len(rows), LANES), FULL)
    return jnp.concatenate(high + low + [blank], 0).astype(LOW)


def mix_kernel(meta, kv_low, attn_in, attn_gain, ffn_gain, kv_gain, sums, router_part, payload):
    owners, rows, _ = payload.shape
    share = rows - 16 - EXPERTS
    shape = (kv_low.shape[1], share)
    pick = lax.broadcasted_iota(jnp.int32, shape, 0) == meta[0] * share + lax.broadcasted_iota(
        jnp.int32, shape, 1
    )
    mine = jnp.dot(
        kv_low[...], pick.astype(FULL).astype(LOW), preferred_element_type=FULL
    ).astype(LOW)
    grad = contract(mine, attn_in[...], 0, 0).astype(LOW)
    own_rank = RANK // owners
    blank = jnp.zeros((1, LANES - own_rank), FULL)
    for owner in range(owners):
        here = slice(owner * LANES, (owner + 1) * LANES)
        payload[owner, :share] = grad[:, here]
        own_kv = jnp.concatenate(
            [kv_gain[:, owner * own_rank : (owner + 1) * own_rank], blank], -1
        )
        payload[owner, share + 16 :] = router_part[:, here]
        payload[owner, share : share + 16] = split_rows(
            [attn_gain[:, here], ffn_gain[:, here], own_kv, sums[...]]
        )


def join_rows(rows, count=4):
    values = rows.astype(FULL)
    return [values[i : i + 1] + values[count + i : count + i + 1] for i in range(count)]


def mix_sum_kernel(got, copies, router_grad):
    share = got.shape[1] - 16 - EXPERTS
    total = got[0].astype(FULL)
    for index in range(1, got.shape[0]):
        total = total + got[index].astype(FULL)
    mixed = jnp.concatenate(
        [total[:share].astype(LOW), split_rows(join_rows(total[share : share + 16]))], 0
    )
    for index in range(copies.shape[0]):
        copies[index] = mixed
    router_grad[...] = total[share + 16 :]


def final_kernel(
    got,
    tokens,
    *refs,
):
    grads, refs = refs[: got.shape[0]], refs[got.shape[0] :]
    shared, refs = refs[:4], refs[4:]
    input_grad, down_grad, attn_gain, ffn_gain, kv_gain, rms = refs[:6]
    query_grad, up_grad, out_grad = refs[6:9]
    gate_grad, shared_up_grad, shared_down_grad, held = refs[9:]
    count, share, _ = got.shape
    share = share - 16
    rows, width = grads[0].shape
    gains = 0.0
    for index in range(count):
        owner = lax.rem(lax.axis_index("tensor") + count - index, count)
        input_grad[pl.ds(pl.multiple_of(owner * rows, rows), rows), :] = grads[index][...]
        held[index * share : (index + 1) * share] = got[index, :share].astype(FULL)
        gains = gains + jnp.concatenate(join_rows(got[index, share:]), 0)
    down_grad[...] = held[: down_grad.shape[0]]
    attn_gain[...] = gains[0:1]
    ffn_gain[...] = gains[1:2]
    kv_gain[...] = gains[2:3, : kv_gain.shape[1]]
    entries = jnp.where(
        lax.broadcasted_iota(jnp.int32, rms.shape, 1) == 1, float(RANK), float(width)
    )
    rms[...] = jnp.sqrt(
        gains[3:4, : rms.shape[1]] / (entries * (rows * count * lax.axis_size("dp")))
    )
    start = query_grad.shape[1]
    query_grad[...] = tokens[:start].T
    end = start + out_grad.shape[0]
    out_grad[...] = tokens[start:end]
    lines = up_grad.shape[0]
    for column in range(up_grad.shape[1] // LANES):
        first = end + column * lines
        up_grad[:, column * LANES : (column + 1) * LANES] = tokens[first : first + lines]
    rows = gate_grad.shape[0]
    for index, out in enumerate((gate_grad, shared_up_grad, shared_down_grad)):
        here = slice(index * rows, (index + 1) * rows)
        total = shared[0][here]
        for ref in shared[1:]:
            total = total + ref[here].astype(FULL)
        out[...] = total


def after(value, *others):
    return lax.optimization_barrier((value, *others))[0]


def swap_blocks(blocks, axis, groups=None):
    return lax.all_to_all(blocks, axis, 0, 0, tiled=True, axis_index_groups=groups)


def shift_z(block, shift):
    if shift == 0:
        return block
    count = lax.axis_size("tensor")
    return lax.ppermute(block, "tensor", [(i, (i + 2 * shift) % count) for i in range(count)])


def shift_tensor(block, shift):
    if shift == 0:
        return block
    count = lax.axis_size("tensor")
    return lax.ppermute(block, "tensor", [(i, (i + shift) % count) for i in range(count)])


def per_device(
    hidden_in,
    norm_attn,
    q_weight,
    kv_down,
    kv_norm,
    kv_up,
    out_weight,
    norm_ffn,
    router,
    expert_gate,
    expert_up,
    expert_down,
    shared_gate,
    shared_up,
    shared_down,
    routes,
    cotangent,
):
    tok_rows, width = hidden_in.shape
    dp_count = lax.axis_size("dp")
    tensor_count = lax.axis_size("tensor")
    local_experts = expert_gate.shape[0]
    part_rows = tok_rows // tensor_count
    hidden_part = expert_gate.shape[2]
    heads_local = q_weight.shape[1] // (NOPE + ROPE)
    heads_width = heads_local * (NOPE + VDIM)
    scaling = (NOPE + ROPE) ** (-0.5)
    group_devs = GROUP // tok_rows
    prompt_devs = PROMPT // tok_rows
    dp_place = lax.axis_index("dp")
    tensor_place = lax.axis_index("tensor")
    place = dp_place % group_devs
    quarter = place % prompt_devs
    z_place = tensor_place // 2
    group_base = (dp_place - place) * tok_rows

    def own_part(values):
        return lax.dynamic_slice_in_dim(values, tensor_place * part_rows, part_rows, 0)

    def meta(*entries):
        return jnp.stack([jnp.asarray(entry, jnp.int32) for entry in entries])

    ramp = jnp.arange(tok_rows, dtype=jnp.int32)
    position, unused_seg, unused_group = token_layout(dp_place * tok_rows + ramp)
    cos_table, sin_table = angle_tables(position)
    gain_first, gain_second, gain_kv = norm_attn[None], norm_ffn[None], kv_norm[None]
    down_rows_kv = kv_down.T
    router_rows = router.T
    kv_width = RANK + 2 * ROPE
    stacks = [expert_gate.transpose(0, 2, 1), expert_up.transpose(0, 2, 1), expert_down]
    near_rows = 3 * hidden_part
    slot_count = dp_count * CAP
    attn_in, packed_own, kv_raw, pack_ahead, pack_behind = run_kernel(
        latent_kernel,
        (hidden_in, gain_first, down_rows_kv, gain_kv, cos_table, sin_table, *stacks),
        [VMEM] * 6 + [HBM] * 3,
        [
            ((tok_rows, width), LOW),
            ((tok_rows, kv_width), LOW),
            ((tok_rows, RANK + ROPE), FULL),
            ((near_rows, width), LOW),
            ((near_rows, width), LOW),
        ],
        [pltpu.VMEM((2 * near_rows, width), LOW), pltpu.SemaphoreType.DMA((8,))],
        [VMEM] * 3 + [HBM] * 2,
    )
    ahead, behind = shift_z(pack_ahead, 1), shift_z(pack_behind, 3)
    copied = lax.ppermute(
        packed_own,
        "dp",
        [
            (base + i, base + prompt_devs + i)
            for base in range(0, dp_count, group_devs)
            for i in range(prompt_devs)
        ],
    )
    query, dispatch, taken_grads = run_kernel(
        early_kernel,
        (after(attn_in, copied), q_weight, cos_table, sin_table, routes.T, cotangent),
        [VMEM] * 6,
        [
            ((tok_rows, heads_local * 2 * LANES), LOW),
            ((slot_count, tok_rows), LOW),
            ((slot_count, 2 * width), LOW),
        ],
        [pltpu.VMEM((slot_count, width), LOW), pltpu.SemaphoreType.DMA],
        [VMEM] * 2 + [HBM],
    )
    combine = dispatch.T
    (pack_far,) = run_kernel(
        far_pack_kernel,
        (*stacks[:2], after(stacks[2], query)),
        [HBM] * 3,
        [((near_rows, width), LOW)],
        [pltpu.VMEM((near_rows, width), LOW), pltpu.SemaphoreType.DMA((4,))],
        [HBM],
    )
    first_block = jnp.where(place < prompt_devs, packed_own, copied)
    blocks = [first_block]
    for shift in range(1, prompt_devs):
        blocks.append(
            lax.ppermute(
                first_block,
                "dp",
                [
                    (base + i, base + (i + shift) % prompt_devs)
                    for base in range(0, dp_count, prompt_devs)
                    for i in range(prompt_devs)
                ],
            )
        )
    blocks.append(packed_own)
    attend_meta = meta(
        place, *[(quarter - shift) % prompt_devs for shift in range(prompt_devs)]
    )
    key_rows = len(blocks) * tok_rows
    attn_part, attn_low, kv_heads, log_sum = run_kernel(
        attend_kernel,
        (attend_meta, *blocks, query, kv_up, out_weight),
        [SMEM] + [VMEM] * 8,
        [
            ((tok_rows, width), LOW),
            ((tok_rows, heads_local * VDIM), LOW),
            ((key_rows, heads_width), LOW),
            ((tok_rows, heads_local * LANES), FULL),
        ],
    )
    part_meta = meta(tensor_place)

    def by_part(values):
        return values.reshape(tensor_count, part_rows, values.shape[-1])

    middle, copies = run_kernel(
        middle_kernel,
        (part_meta, swap_blocks(by_part(attn_part), "tensor"), hidden_in, gain_second),
        [SMEM] + [VMEM] * 3,
        [((part_rows, width), FULL), ((tensor_count, part_rows, width), LOW)],
    )
    ffn_in = swap_blocks(after(copies, ahead, behind, pack_far), "tensor").reshape(tok_rows, width)

    (taken_rows,) = run_kernel(
        take_kernel,
        (dispatch, ffn_in, taken_grads),
        [VMEM] * 2 + [HBM],
        [((slot_count, 2 * width), LOW)],
        [pltpu.VMEM((slot_count, width), LOW), pltpu.SemaphoreType.DMA],
        [HBM],
        aliases={2: 0},
    )
    expert_rows = swap_blocks(taken_rows.reshape(dp_count, CAP, 2 * width), "dp").reshape(
        slot_count, 2 * width
    )
    far = shift_z(after(pack_far, taken_rows), 2)

    shared_width = shared_gate.shape[1]
    shared_back, shared_part, shared_keep, shared_send = run_kernel(
        shared_kernel,
        (after(ffn_in, taken_rows), cotangent, shared_gate.T, shared_up.T, shared_down),
        [VMEM] * 5,
        [
            ((tok_rows, width), LOW),
            ((tok_rows, width), LOW),
            ((3 * shared_width, width // 2), LOW),
            ((3 * shared_width, width // 2), LOW),
        ],
        [pltpu.VMEM((3 * shared_width, width), FULL)],
        mib=32,
    )

    def exchange_dp(block, flip):
        return lax.ppermute(block, "dp", [(i, i ^ flip) for i in range(dp_count)])

    def join_cores(keep, arrived):
        shape = (keep.shape[0], keep.shape[1] // 2)
        return run_kernel(
            join_cores_kernel, (keep, arrived), [VMEM] * 2, [(shape, FULL), (shape, LOW)],
        mib=16,
    )

    def join_sides(keep, arrived):
        shape = (keep.shape[0], LANES)
        return run_kernel(
            join_sides_kernel, (keep, arrived), [VMEM] * 2, [(shape, FULL)] + [(shape, LOW)] * 3
        )

    def along_x(blocks):
        return [
            lax.ppermute(block, "dp", [(i, (i + 4 * shift) % dp_count) for i in range(dp_count)])
            for shift, block in enumerate(blocks, 1)
        ]

    shared_keep, shared_send = join_cores(shared_keep, after(exchange_dp(shared_send, 1), far))
    shared_arrived = exchange_dp(shared_send, 2)

    own_hidden = local_experts * hidden_part
    wide = 2 * width + LANES
    back_rows, hidden_low, gate_low, up_low, slot_gate = run_kernel(
        expert_kernel,
        (
            meta(dp_place * local_experts + z_place),
            expert_rows,
            *stacks,
            ahead,
            far,
            behind,
            after(router_rows, shared_keep),
        ),
        [SMEM] + [HBM] * 7 + [VMEM],
        [
            ((slot_count, wide), LOW),
            ((slot_count, own_hidden), LOW),
            ((slot_count, own_hidden), LOW),
            ((slot_count, own_hidden), LOW),
            ((slot_count, LANES), FULL),
        ],
        [
            pltpu.VMEM((slot_count, width), LOW),
            pltpu.VMEM((slot_count, width), LOW),
            pltpu.VMEM((3, own_hidden, width), LOW),
            pltpu.VMEM((slot_count, wide), LOW),
            pltpu.SemaphoreType.DMA((2,)),
            pltpu.SemaphoreType.DMA((3, 4)),
            pltpu.SemaphoreType.DMA((2,)),
        ],
        [HBM] + [VMEM] * 4,
        mib=44,
    )

    back_rows = swap_blocks(
        after(back_rows, shared_arrived).reshape(dp_count, CAP, wide), "dp"
    ).reshape(slot_count, wide)
    shared_own, *shared_blocks = join_sides(shared_keep, shared_arrived)
    turns = 2
    step = width // turns

    def weight_grad(kernel, operands, first):
        whole = [pl.BlockSpec(v.shape, lambda turn: (0, 0)) for v in operands]
        return run_kernel(
            kernel,
            (expert_rows, *operands),
            [pl.BlockSpec((slot_count, step), lambda turn: (0, first * turns + turn))] + whole,
            [((hidden_part, width), LOW)] * local_experts,
            out_specs=[pl.BlockSpec((hidden_part, step), lambda turn: (0, turn))] * local_experts,
            grid=(turns,),
            mib=20,
        )

    in_grads = [weight_grad(expert_in_grad_kernel, (low,), 0) for low in (gate_low, up_low)]
    down_grads = weight_grad(expert_out_grad_kernel, (hidden_low, slot_gate), 1)
    back_rows = after(
        back_rows, in_grads[0][0], in_grads[1][0], down_grads[0], shared_own
    )
    early = [(0, 1), (0, 3), (1, 1), (1, 3), (0, 2)]
    early_homes = {
        (kind, shift): shift_z(in_grads[kind][shift], local_experts - shift)
        for kind, shift in early
    }

    (payload,) = run_kernel(
        combine_kernel,
        (
            meta(z_place, local_experts),
            combine,
            after(back_rows, down_grads[0], *early_homes.values()),
            shared_back,
            shared_part,
        ),
        [SMEM] + [VMEM] * 4,
        [((tok_rows, wide), LOW)],
        mib=24,
    )
    middle_grad, copies, norm_ffn_grad, middle_sums = run_kernel(
        ffn_back_kernel,
        (
            part_meta,
            middle,
            ffn_in,
            router_rows,
            gain_second,
            cotangent,
            swap_blocks(by_part(payload), "tensor"),
        ),
        [SMEM] + [VMEM] * 6,
        [
            ((part_rows, width), FULL),
            ((tensor_count, part_rows, wide), LOW),
            ((1, width), FULL),
            ((1, LANES), FULL),
        ],
        mib=20,
    )
    shared_blocks = along_x(lax.optimization_barrier((*shared_blocks, payload))[:-1])
    shared_blocks = [shared_own, *shared_blocks]
    spread = after(swap_blocks(copies, "tensor"), *shared_blocks).reshape(tok_rows, wide)
    late_homes = {(1, 2): shift_z(after(in_grads[1][2], spread), local_experts - 2)}

    kv_part, query_part, heads_low, query_low = run_kernel(
        attend_back_kernel,
        (
            attend_meta,
            out_weight,
            *blocks,
            query,
            kv_heads,
            log_sum,
            kv_up,
            cos_table,
            sin_table,
            spread,
            q_weight,
        ),
        [SMEM] + [VMEM] * 14,
        [
            ((tensor_count, part_rows, len(blocks) * kv_width), LOW),
            ((tok_rows, width), LOW),
            ((key_rows, heads_width), LOW),
            ((tok_rows, heads_local * (NOPE + ROPE)), LOW),
        ],
    )
    got_parts = swap_blocks(after(kv_part, late_homes[1, 2]), "tensor")
    *prompt_parts, kv_own = run_kernel(
        kv_sum_kernel,
        (got_parts,),
        [VMEM],
        [((part_rows, kv_width), LOW)] * prompt_devs + [((part_rows, kv_width), FULL)],
    )
    (joined,) = run_kernel(
        kv_join_kernel,
        [prompt_parts[0]]
        + [
            lax.ppermute(
                prompt_parts[shift],
                "dp",
                [
                    (base + i, base + (i - shift) % prompt_devs)
                    for base in range(0, dp_count, prompt_devs)
                    for i in range(prompt_devs)
                ],
            )
            for shift in range(1, prompt_devs)
        ],
        [VMEM] * prompt_devs,
        [((part_rows, kv_width), LOW)],
    )
    other = lax.ppermute(
        joined,
        "dp",
        [
            (base + prompt_devs + i, base + i)
            for base in range(0, dp_count, group_devs)
            for i in range(prompt_devs)
        ],
    )
    got_query = swap_blocks(after(by_part(query_part), kv_own), "tensor")
    for shift in (1, 3, 2):
        late_homes[2, shift] = shift_z(after(down_grads[shift], kv_own), local_experts - shift)

    def place_grads(kind):
        grads = (*in_grads, down_grads)[kind]
        arrived = early_homes | late_homes
        return run_kernel(
            place_kernel,
            (
                meta(z_place),
                grads[0],
                *[arrived[kind, shift] for shift in range(1, local_experts)],
            ),
            [SMEM] + [VMEM] * 4,
            [((local_experts, hidden_part, width), FULL)],
        )[0]

    gate_wgrad = place_grads(0)
    copies, grad_low, norm_attn_grad, kv_norm_grad, square_sums = run_kernel(
        last_kernel,
        (
            meta(tensor_place, place),
            joined,
            other,
            kv_own,
            kv_raw,
            gain_kv,
            cos_table,
            sin_table,
            down_rows_kv,
            hidden_in,
            gain_first,
            after(middle_grad, gate_wgrad),
            middle_sums,
            got_query,
        ),
        [SMEM] + [VMEM] * 13,
        [
            ((tensor_count, part_rows, kv_width), LOW),
            ((part_rows, width), LOW),
            ((1, width), FULL),
            ((1, RANK), FULL),
            ((1, LANES), FULL),
        ],
    )
    up_wgrad = place_grads(1)
    kv_low_all = swap_blocks(copies, "tensor").reshape(tok_rows, kv_width)
    down_wgrad = place_grads(2)

    query_width = q_weight.shape[1]
    own_width, own_rank = width // dp_count, RANK // dp_count
    up_lines = own_rank * heads_width // LANES
    attn_width = heads_local * VDIM
    token_rows = query_width + attn_width + up_lines
    token_grads, router_part, output = run_kernel(
        token_grad_kernel,
        (attn_in, query_low, attn_low, spread, ffn_in, heads_low, *blocks),
        [VMEM] * (6 + len(blocks)),
        [
            ((token_rows, width), FULL),
            ((EXPERTS, width), LOW),
            ((tok_rows, width), LOW),
        ],
        mib=28,
    )
    token_grads = lax.psum_scatter(
        after(token_grads, got_parts), "dp", scatter_dimension=1, tiled=True
    )
    share = kv_width // tensor_count
    grad_low = after(grad_low, kv_low_all)
    grad_parts = [shift_tensor(grad_low, shift) for shift in range(tensor_count)]
    (mixed,) = run_kernel(
        mix_kernel,
        (
            part_meta,
            after(kv_low_all, up_wgrad, late_homes[2, 1], late_homes[2, 3]),
            attn_in,
            norm_attn_grad,
            norm_ffn_grad,
            kv_norm_grad,
            square_sums,
            router_part,
        ),
        [SMEM] + [VMEM] * 7,
        [((dp_count, share + 16 + EXPERTS, LANES), LOW)],
        mib=16,
    )
    copies, router_grad = run_kernel(
        mix_sum_kernel,
        (after(swap_blocks(mixed, "dp"), late_homes[2, 2], *grad_parts[1:6]),),
        [VMEM],
        [((tensor_count, share + 16, LANES), LOW), ((EXPERTS, LANES), FULL)],
        mib=16,
    )
    shared_width = shared_gate.shape[1]
    (
        input_grad,
        down_grad,
        attn_gain,
        ffn_gain,
        kv_gain,
        rms,
        query_grad,
        up_grad,
        out_grad,
        *shared_out,
    ) = run_kernel(
        final_kernel,
        (swap_blocks(copies, "tensor"), token_grads, *grad_parts, *shared_blocks),
        [VMEM] * (2 + tensor_count + len(shared_blocks)),
        [
            ((tok_rows, width), LOW),
            ((RANK + ROPE, own_width), FULL),
            ((1, LANES), FULL),
            ((1, LANES), FULL),
            ((1, own_rank), FULL),
            ((1, 5), FULL),
            ((own_width, query_width), FULL),
            ((own_rank, heads_width), FULL),
            ((attn_width, own_width), FULL),
        ]
        + [((shared_width, own_width), FULL)] * 3,
        [pltpu.VMEM((kv_width, LANES), FULL)],
        mib=16,
    )
    return (
        output,
        input_grad,
        attn_gain.reshape(own_width),
        query_grad,
        down_grad.T,
        kv_gain.reshape(own_rank),
        up_grad,
        out_grad,
        ffn_gain.reshape(own_width),
        router_grad.T,
        gate_wgrad.transpose(0, 2, 1),
        up_wgrad.transpose(0, 2, 1),
        down_wgrad,
        shared_out[0].T,
        shared_out[1].T,
        shared_out[2],
        rms.reshape(5),
    )


def solution(mesh):
    return jax.shard_map(
        per_device,
        mesh=mesh,
        in_specs=(
            P("dp", None),
            P(),
            P(None, "tensor"),
            P(),
            P(),
            P(None, "tensor"),
            P("tensor", None),
            P(),
            P(),
            P("dp", None, "tensor"),
            P("dp", None, "tensor"),
            P("dp", "tensor", None),
            P(None, "tensor"),
            P(None, "tensor"),
            P("tensor", None),
            P("dp", None),
            P("dp", None),
        ),
        out_specs=(
            P("dp", None),
            P("dp", None),
            P("dp"),
            P("dp", "tensor"),
            P("dp", None),
            P("dp"),
            P("dp", "tensor"),
            P("tensor", "dp"),
            P("dp"),
            P("dp", None),
            P("dp", None, "tensor"),
            P("dp", None, "tensor"),
            P("dp", "tensor", None),
            P("dp", "tensor"),
            P("dp", "tensor"),
            P("tensor", "dp"),
            P(),
        ),
        check_vma=False,
    )
```
